32 devices in a mesh: dp: 8 (over z, x), head: 4 (over y, core).
Axes of the slice: x: 2, y: 2, z: 4, core: 2. Of those that a mesh axis runs over, the one named last changes fastest.
Arguments:
- inputs: bfloat16 [16384, 768], P(('dp', 'head')), may hold values from -6 to 6
- cotangent: bfloat16 [16384, 768], P(('dp', 'head')), may hold values from -6 to 6
- lengths: int32 [32], replicated, may hold values from 1 to 8192, 16128 in all
- w_qkv: float32 [2, 768, 2304], P(None, 'dp', 'head'), may hold values from -0.21875 to 0.21875
- m_qkv: float32 [2, 768, 2304], P(None, 'dp', 'head'), may hold values from -0.0004272461 to 0.0004272461
- v_qkv: float32 [2, 768, 2304], P(None, 'dp', 'head'), may hold values from 7.061189e-11 to 2.8244757e-10
- w_out: float32 [2, 768, 768], P(None, 'dp', 'head'), may hold values from -2.5 to 2.5
- m_out: float32 [2, 768, 768], P(None, 'dp', 'head'), may hold values from -0.0004272461 to 0.0004272461
- v_out: float32 [2, 768, 768], P(None, 'dp', 'head'), may hold values from 8.826486e-12 to 3.5305946e-11
- w_up: float32 [2, 768, 3072], P(None, 'dp', 'head'), may hold values from -0.21875 to 0.21875
- m_up: float32 [2, 768, 3072], P(None, 'dp', 'head'), may hold values from -0.0004272461 to 0.0004272461
- v_up: float32 [2, 768, 3072], P(None, 'dp', 'head'), may hold values from 7.061189e-11 to 2.8244757e-10
- w_down: float32 [2, 3072, 768], P(None, 'dp', 'head'), may hold values from -0.109375 to 0.109375
- m_down: float32 [2, 3072, 768], P(None, 'dp', 'head'), may hold values from -0.0004272461 to 0.0004272461
- v_down: float32 [2, 3072, 768], P(None, 'dp', 'head'), may hold values from 7.061189e-11 to 2.8244757e-10
- norm_params: float32 [2, 4, 768], P(None, 'head', 'dp'), may hold values from -0.8 to 2.4
- m_norm: float32 [2, 4, 768], P(None, 'head', 'dp'), may hold values from -0.0014648438 to 0.0014648438
- v_norm: float32 [2, 4, 768], P(None, 'head', 'dp'), may hold values from 7.0611894e-10 to 2.8244758e-09
Outputs:
- output: float32 [16384, 768], P(('dp', 'head'))
- grad_input: float32 [16384, 768], P(('dp', 'head'))
- grad_norm: float32 [1], replicated
- new_w_qkv: float32 [2, 768, 2304], P(None, 'dp', 'head')
- new_m_qkv: float32 [2, 768, 2304], P(None, 'dp', 'head')
- new_v_qkv: float32 [2, 768, 2304], P(None, 'dp', 'head')
- new_w_out: float32 [2, 768, 768], P(None, 'dp', 'head')
- new_m_out: float32 [2, 768, 768], P(None, 'dp', 'head')
- new_v_out: float32 [2, 768, 768], P(None, 'dp', 'head')
- new_w_up: float32 [2, 768, 3072], P(None, 'dp', 'head')
- new_m_up: float32 [2, 768, 3072], P(None, 'dp', 'head')
- new_v_up: float32 [2, 768, 3072], P(None, 'dp', 'head')
- new_w_down: float32 [2, 3072, 768], P(None, 'dp', 'head')
- new_m_down: float32 [2, 3072, 768], P(None, 'dp', 'head')
- new_v_down: float32 [2, 3072, 768], P(None, 'dp', 'head')
- new_norm: float32 [2, 4, 768], P(None, 'head', 'dp')
- new_m_norm: float32 [2, 4, 768], P(None, 'head', 'dp')
- new_v_norm: float32 [2, 4, 768], P(None, 'head', 'dp')
The draws below stay inside these ranges and needn't reach their ends.
Inputs may be any that keep to these rules, and one draw needn't show every extreme that they name: The lengths sum to 16128; the rows after them are padding; the largest is exactly 8192.
All inputs are finite; a program needn't handle non-finite values.
Results may differ from the reference program's by a relative error of at most 0.019.
Values may be sent and summed in bfloat16 or wider, within the bound.
A program may use at most 256 MiB of HBM per device.

```python
import math
import jax
import jax.numpy as jnp
import numpy as np
from jax import lax

D = 768
HEADS = 12
FF = 3072
L = 2
LONGEST = 8192
TOKENS = 16384
NSEQ = 32
PAD = 256
NPARAM = 14161920


def draw_norm_params(key, part):
    gain_key = jax.random.fold_in(key, 11)
    shift_key = jax.random.fold_in(key, 23)
    place = jnp.arange(D, dtype=jnp.int32).astype(jnp.float32) / (D - 1)
    ramp = 0.5 + place
    noise = 0.15 * jax.random.normal(gain_key, (L, 2, 1, D), jnp.float32)
    gains = jnp.clip(ramp * (1.0 + noise), 0.2, 2.4)
    shifts = jnp.clip(0.2 * jax.random.normal(shift_key, (L, 2, 1, D), jnp.float32), -0.8, 0.8)
    return jnp.concatenate([gains, shifts], axis=2).reshape(L, 4, D)


def level_of(key, extent, shards, least, high):
    def one(position, parts):
        heights = jax.random.uniform(jax.random.fold_in(jax.random.fold_in(key, 6), position), (parts,), jnp.float32, least / len(shards), high / len(shards))
        return jnp.repeat(jnp.exp(heights), extent[position] // parts).reshape((-1,) + (1,) * (len(extent) - position - 1))

    loudness = one(*shards[0])
    for cut in shards[1:]:
        loudness = loudness * one(*cut)
    return loudness


def profile(amount, total, bound, lean):
    loads = [(1 << 20) // math.isqrt(grade ** lean) + 1 for grade in range(2, amount + 1)]
    spare, given = total - bound - (amount - 1), [1] * (amount - 1)
    while spare > 0:
        candidates = [i for i in range(amount - 1) if given[i] < bound]
        whole, remaining = sum([loads[i] for i in candidates]), spare
        for i in candidates:
            more = min(bound - given[i], max(1, remaining * loads[i] // whole), spare)
            given[i] = given[i] + more
            spare = spare - more
    return np.array([bound] + given)


def ragged(rng, count, total, most, lean):
    if count == 2:
        one = jax.random.randint(rng, (), max(1, total - most), min(most, total - 1) + 1)
        return jnp.stack([one, total - one])
    tallies = jnp.asarray(profile(count, total, most, lean), jnp.int32)
    couples = (count - 1) // 2
    source_of, taker = tallies[1:1 + 2 * couples:2], tallies[2:2 + 2 * couples:2]
    room = jnp.minimum(source_of - 1, most - taker)
    passed = jax.random.randint(jax.random.fold_in(rng, 1), (couples,), 0, 1 << 20) % (room + 1)
    tallies = tallies.at[1:1 + 2 * couples:2].set(source_of - passed).at[2:2 + 2 * couples:2].set(taker + passed)
    return tallies[jax.random.permutation(jax.random.fold_in(rng, 2), count)]


def bell_draw(own_key, extent, spread, most, shards=(), held_as=jnp.bfloat16):
    entries = jax.random.normal(own_key, extent, jnp.float32) * spread
    if len(shards) > 0:
        entries = level_of(own_key, extent, shards, -0.22, 0.18) * entries
    return jnp.clip(entries, min=-most, max=most).astype(held_as)


def setup_inputs(seed: int = 0) -> dict:
    seeds = jax.random.split(jax.random.key(seed), 19)
    return {
        "inputs": bell_draw(seeds[0], (TOKENS, D), 1.0, 6.0, ((0, 32),)),
        "cotangent": bell_draw(seeds[1], (TOKENS, D), 1.0, 6.0, ((0, 32),)),
        "lengths": ragged(seeds[2], NSEQ, TOKENS - PAD, LONGEST, 2).astype(jnp.int32),
        "w_qkv": bell_draw(seeds[3], (L, D, 3 * D), D ** -0.5, 0.21875, ((1, 8), (2, 4)), jnp.float32),
        "m_qkv": bell_draw(seeds[4], (L, D, 3 * D), (0.11 / NPARAM ** 0.5), 0.0004272461, ((1, 8), (2, 4)), jnp.float32),
        "v_qkv": jnp.clip(jnp.exp(math.log(2.8244756533624127e-10) - 1.3862944 * jax.random.uniform(seeds[5], (L, D, 3 * D), jnp.float32) ** level_of(seeds[5], (L, D, 3 * D), ((1, 8), (2, 4)), -0.2, 0.2)), 7.061189133406032e-11, 2.8244756533624127e-10),
        "w_out": bell_draw(seeds[6], (L, D, D), (max(D // 128, 1)) ** -0.5, 2.5, ((1, 8), (2, 4)), jnp.float32),
        "m_out": bell_draw(seeds[7], (L, D, D), (0.11 / NPARAM ** 0.5), 0.0004272461, ((1, 8), (2, 4)), jnp.float32),
        "v_out": jnp.clip(jnp.exp(math.log(3.530594566703016e-11) - 1.3862944 * jax.random.uniform(seeds[8], (L, D, D), jnp.float32) ** level_of(seeds[8], (L, D, D), ((1, 8), (2, 4)), -0.2, 0.2)), 8.82648641675754e-12, 3.530594566703016e-11),
        "w_up": bell_draw(seeds[9], (L, D, FF), D ** -0.5, 0.21875, ((1, 8), (2, 4)), jnp.float32),
        "m_up": bell_draw(seeds[10], (L, D, FF), (0.11 / NPARAM ** 0.5), 0.0004272461, ((1, 8), (2, 4)), jnp.float32),
        "v_up": jnp.clip(jnp.exp(math.log(2.8244756533624127e-10) - 1.3862944 * jax.random.uniform(seeds[11], (L, D, FF), jnp.float32) ** level_of(seeds[11], (L, D, FF), ((1, 8), (2, 4)), -0.2, 0.2)), 7.061189133406032e-11, 2.8244756533624127e-10),
        "w_down": bell_draw(seeds[12], (L, FF, D), FF ** -0.5, 0.109375, ((1, 8), (2, 4)), jnp.float32),
        "m_down": bell_draw(seeds[13], (L, FF, D), (0.11 / NPARAM ** 0.5), 0.0004272461, ((1, 8), (2, 4)), jnp.float32),
        "v_down": jnp.clip(jnp.exp(math.log(2.8244756533624127e-10) - 1.3862944 * jax.random.uniform(seeds[14], (L, FF, D), jnp.float32) ** level_of(seeds[14], (L, FF, D), ((1, 8), (2, 4)), -0.2, 0.2)), 7.061189133406032e-11, 2.8244756533624127e-10),
        "norm_params": draw_norm_params(jax.random.fold_in(seeds[18], 71), 0),
        "m_norm": bell_draw(seeds[16], (L, 4, D), (0.35 / NPARAM ** 0.5), 0.0014648438, ((1, 4), (2, 8)), jnp.float32),
        "v_norm": jnp.clip(jnp.exp(math.log(2.824475764384715e-09) - 1.3862944 * jax.random.uniform(seeds[17], (L, 4, D), jnp.float32) ** level_of(seeds[17], (L, 4, D), ((1, 4), (2, 8)), -0.2, 0.2)), 7.061189410961788e-10, 2.824475764384715e-09),
    }


exact_mode = lax.Precision.HIGHEST
beta_one = 0.9
beta_two = 0.999
adam_eps = 1e-08
decay_rate = 0.1
rate_matrix = 0.1
rate_outproj = 0.5
rate_norm = 0.5
clip_limit = 1.0
norm_eps = 1e-05
step_fixed = 10.0

@jax.custom_vjp
def low(v):
    return lax.optimization_barrier(v.astype(jnp.bfloat16)).astype(jnp.float32)

@jax.custom_vjp
def low_back(v):
    return v

def low_keep(v):
    return (low(v), None)

def low_pass(kept, grad):
    return (grad,)

def back_keep(v):
    return (v, None)

def back_low(kept, grad):
    return (low(grad),)
low.defvjp(low_keep, low_pass)
low_back.defvjp(back_keep, back_low)

def stream_meta(lengths, first_row, row_count):
    seq_count = lengths.shape[0]
    seq_ends = jnp.cumsum(lengths, dtype=jnp.int32)
    seq_starts = seq_ends - lengths
    row_ids = first_row + jnp.arange(row_count, dtype=jnp.int32)
    begun = seq_starts[None, :] <= row_ids[:, None]
    seg_raw = lax.optimization_barrier(jnp.sum(begun.astype(jnp.int32), axis=1, dtype=jnp.int32)) - 1
    seg_start = lax.optimization_barrier(jnp.max(jnp.where(begun, seq_starts[None, :], 0), axis=1))
    inside = row_ids < seq_ends[seq_count - 1]
    seg_ids = jnp.where(inside, seg_raw, seq_count).astype(jnp.int32)
    offsets = jnp.where(inside, row_ids - seg_start, 0).astype(jnp.float32)
    angles = offsets * (0.5 * math.pi / LONGEST)
    return (seg_ids, jnp.cos(angles), jnp.sin(angles), inside.astype(jnp.float32))

def block_step(carry_in, block_data):
    state_cos, state_sin, sum_cos, sum_sin, carry_seg = carry_in
    queries, key_rows, value_rows, seg_ids, cos_row, sin_row = block_data
    block_len = seg_ids.shape[0]
    position_ids = jnp.arange(block_len, dtype=jnp.int32)
    allowed = (seg_ids[:, None] == seg_ids[None, :]) & (position_ids[None, :] <= position_ids[:, None])
    closeness = cos_row[:, None] * cos_row[None, :] + sin_row[:, None] * sin_row[None, :]
    weight_map = jnp.where(allowed, closeness, 0.0)
    scores = low(low_back(jnp.einsum('ihe,jhe->hij', queries, key_rows, precision=exact_mode) * weight_map[None]))
    numerator = jnp.einsum('hij,jhe->ihe', scores, value_rows, precision=exact_mode)
    denominator = jnp.transpose(lax.optimization_barrier(jnp.sum(scores, axis=2)))
    following = (seg_ids == carry_seg).astype(jnp.float32)
    q_cos = queries * (cos_row * following)[:, None, None]
    q_sin = queries * (sin_row * following)[:, None, None]
    numerator = numerator + jnp.einsum('ihe,hef->ihf', q_cos, state_cos, precision=exact_mode) + jnp.einsum('ihe,hef->ihf', q_sin, state_sin, precision=exact_mode)
    denominator = denominator + jnp.einsum('ihe,he->ih', q_cos, sum_cos, precision=exact_mode) + jnp.einsum('ihe,he->ih', q_sin, sum_sin, precision=exact_mode)
    last_seg = seg_ids[block_len - 1]
    in_last = (seg_ids == last_seg).astype(jnp.float32)
    k_cos = key_rows * (cos_row * in_last)[:, None, None]
    k_sin = key_rows * (sin_row * in_last)[:, None, None]
    keep_old = (carry_seg == last_seg).astype(jnp.float32)
    state_cos = keep_old * state_cos + jnp.einsum('jhe,jhf->hef', k_cos, value_rows, precision=exact_mode)
    state_sin = keep_old * state_sin + jnp.einsum('jhe,jhf->hef', k_sin, value_rows, precision=exact_mode)
    sum_cos = keep_old * sum_cos + lax.optimization_barrier(jnp.sum(k_cos, axis=0))
    sum_sin = keep_old * sum_sin + lax.optimization_barrier(jnp.sum(k_sin, axis=0))
    return ((state_cos, state_sin, sum_cos, sum_sin, last_seg), (numerator, denominator))

def run_blocks(queries, key_rows, value_rows, seg_ids, cos_row, sin_row, block_len):
    row_count, head_count, head_dim = queries.shape
    block_count = row_count // block_len

    def by_blocks(array):
        return array.reshape((block_count, block_len) + array.shape[1:])
    zero_state = jnp.zeros((head_count, head_dim, head_dim), jnp.float32)
    zero_sum = jnp.zeros((head_count, head_dim), jnp.float32)
    initial = (zero_state, zero_state, zero_sum, zero_sum, jnp.array(-1, jnp.int32))
    final_carry, results = lax.scan(jax.checkpoint(block_step), initial, (by_blocks(queries), by_blocks(key_rows), by_blocks(value_rows), by_blocks(seg_ids), by_blocks(cos_row), by_blocks(sin_row)))
    numerator = results[0].reshape(row_count, head_count, head_dim)
    denominator = results[1].reshape(row_count, head_count)
    return ((final_carry[0], final_carry[1], final_carry[2], final_carry[3]), numerator, denominator)

def layer_norm(inputs_row, gain_row, shift_row):
    mean_row = lax.optimization_barrier(jnp.mean(inputs_row, axis=-1, keepdims=True))
    centered = inputs_row - mean_row
    variance = lax.optimization_barrier(jnp.mean(centered * centered, axis=-1, keepdims=True))
    return centered * lax.rsqrt(variance + norm_eps) * gain_row + shift_row

def gelu_exact(inner_pre):
    return jax.nn.gelu(inner_pre, approximate=False)

def adam_step(weight, first_old, second_old, gradient, factor, step_rate, decay_coef):
    clipped = gradient * factor
    first_new = beta_one * first_old + (1.0 - beta_one) * clipped
    second_new = beta_two * second_old + (1.0 - beta_two) * clipped * clipped
    first_hat = first_new / (1.0 - beta_one ** step_fixed)
    second_hat = second_new / (1.0 - beta_two ** step_fixed)
    weight_new = weight - step_rate * (first_hat / (jnp.sqrt(second_hat) + adam_eps) + decay_coef * weight)
    return (weight_new, first_new, second_new)

def reference(inputs, cotangent, lengths, w_qkv, m_qkv, v_qkv, w_out, m_out, v_out, w_up, m_up, v_up, w_down, m_down, v_down, norm_params, m_norm, v_norm):
    seg_ids, cos_row, sin_row, valid_row = stream_meta(lengths, 0, TOKENS)
    block_len = min(512, TOKENS)
    head_dim = D // HEADS

    def forward(hidden, qkv_all, out_all, up_all, down_all, norm_all):
        for layer_idx in range(L):
            qkv_w = low(qkv_all[layer_idx])
            out_w = low(out_all[layer_idx])
            up_w = low(up_all[layer_idx])
            down_w = low(down_all[layer_idx])
            norm_rows = low(norm_all[layer_idx])
            acts_low = low(hidden)
            mixed_rows = jnp.dot(acts_low, qkv_w, precision=exact_mode)
            queries = low(low_back(jax.nn.softplus(mixed_rows[:, :D]))).reshape(TOKENS, HEADS, head_dim)
            key_rows = (low(low_back(jax.nn.softplus(mixed_rows[:, D:2 * D]))) * valid_row[:, None]).reshape(TOKENS, HEADS, head_dim)
            value_rows = low(low_back(mixed_rows[:, 2 * D:])).reshape(TOKENS, HEADS, head_dim)
            summary, numerator, denominator = run_blocks(queries, key_rows, value_rows, seg_ids, cos_row, sin_row, block_len)
            attended = numerator / jnp.maximum(denominator, 1.0)[:, :, None]
            attended_rows = low(low_back(attended.reshape(TOKENS, D)))
            first_in = hidden + low_back(jnp.dot(attended_rows, out_w, precision=exact_mode))
            first_out = layer_norm(first_in, norm_rows[0], norm_rows[1])
            inner_pre = low_back(jnp.dot(low(first_out), up_w, precision=exact_mode))
            activated = low(gelu_exact(inner_pre))
            second_in = first_out + low_back(jnp.dot(activated, down_w, precision=exact_mode))
            hidden = layer_norm(second_in, norm_rows[2], norm_rows[3])
        return hidden
    final_rows, pullback = jax.vjp(forward, inputs.astype(jnp.float32), w_qkv, w_out, w_up, w_down, norm_params)
    gradients = pullback(cotangent.astype(jnp.float32))
    grad_input = gradients[0]
    square_sum = jnp.float32(0.0)
    for gradient in gradients[1:]:
        square_sum = square_sum + jnp.sum(gradient * gradient)
    grad_norm = jnp.sqrt(square_sum)
    factor = clip_limit / jnp.maximum(grad_norm, clip_limit)
    new_qkv = adam_step(w_qkv, m_qkv, v_qkv, gradients[1], factor, rate_matrix, decay_rate)
    new_out = adam_step(w_out, m_out, v_out, gradients[2], factor, rate_outproj, decay_rate)
    new_up = adam_step(w_up, m_up, v_up, gradients[3], factor, rate_matrix, decay_rate)
    new_down = adam_step(w_down, m_down, v_down, gradients[4], factor, rate_matrix, decay_rate)
    new_norm = adam_step(norm_params, m_norm, v_norm, gradients[5], factor, rate_norm, 0.0)
    return (final_rows, grad_input, grad_norm.reshape(1), new_qkv[0], new_qkv[1], new_qkv[2], new_out[0], new_out[1], new_out[2], new_up[0], new_up[1], new_up[2], new_down[0], new_down[1], new_down[2], new_norm[0], new_norm[1], new_norm[2])
```

```python
import functools
import math
import jax
import jax.numpy as jnp
from jax import lax
from jax.experimental import pallas as pl
from jax.experimental.pallas import tpu as pltpu
from jax.sharding import PartitionSpec as P

HEADS = 12
LONGEST = 8192

exact_mode = lax.Precision.HIGHEST
beta_one = 0.9
beta_two = 0.999
adam_eps = 1e-08
decay_rate = 0.1
rate_matrix = 0.1
rate_outproj = 0.5
rate_norm = 0.5
clip_limit = 1.0
norm_eps = 1e-05
step_fixed = 10.0

MESH = pl.DeviceIdType.MESH


def place():
    dp, hd = lax.axis_index("dp"), lax.axis_index("head")
    return dp // 2, dp % 2, hd // 2, hd % 2


def at(z, x, y, c):
    return (z * 2 + x, y * 2 + c)


def greet(partners):
    barrier = pltpu.get_barrier_semaphore()
    for dev in partners:
        pl.semaphore_signal(barrier, inc=1, device_id=dev, device_id_type=MESH)
    pl.semaphore_wait(barrier, len(partners))


def gather_kernel(dims, *refs):
    count = len(dims)
    pieces, fulls = refs[:count], refs[count : 2 * count]
    send_sem, recv_sem, own_sem = refs[2 * count :]
    z, x, y, c = place()
    nx, ny, nc = 1 - x, 1 - y, 1 - c
    zs = [z] + [(z + d) % 4 for d in (1, 2, 3)]
    zo = [z] + [(z + 4 - d) % 4 for d in (1, 2, 3)]
    greet(
        [at(zs[d], x, y, c) for d in (1, 2, 3)]
        + [at(z, nx, y, c), at(z, x, ny, c), at(z, x, y, nc)]
    )

    def spot(t, zz, xx, yy):
        rows, cols, flat = dims[t]
        if flat:
            first = (((zz * 2 + xx) * 2 + yy) * 2 + c) * rows
            left = 0
        else:
            first = ((zz * 2 + xx) * 2 + c) * rows
            left = yy * cols
        return fulls[t].at[
            :, pl.ds(pl.multiple_of(first, rows), rows), pl.ds(pl.multiple_of(left, cols), cols)
        ]

    sent = {}

    def send(t, key, src, dst, dev):
        k = KEYS[key]
        copy = pltpu.make_async_remote_copy(
            src_ref=src,
            dst_ref=dst,
            send_sem=send_sem.at[t, k],
            recv_sem=recv_sem.at[t, k],
            device_id=dev,
            device_id_type=MESH,
        )
        copy.start()
        sent[t, key] = copy

    def forward(t, key, zz, xx, yy, dev):
        block = spot(t, zz, xx, yy)
        send(t, key, block, block, dev)

    to_x, to_y, to_c = at(z, nx, y, c), at(z, x, ny, c), at(z, x, y, nc)

    def fan(t, d):
        src = pieces[t] if d == 0 else spot(t, zo[d], x, y)
        dst = spot(t, zo[d], x, y)
        send(t, ("x", d), src, dst, to_x)
        send(t, ("y", d), src, dst, to_y)
        send(t, ("c", d), src, dst, to_c)

    def second(t, d):
        sent[t, ("x", d)].wait_recv()
        if d in FIRST_X:
            forward(t, ("d", d), zo[d], nx, y, to_y)
        forward(t, ("cx", d), zo[d], nx, y, to_c)
        sent[t, ("y", d)].wait_recv()
        if d not in FIRST_X:
            forward(t, ("d", d), zo[d], x, ny, to_x)
        forward(t, ("cy", d), zo[d], x, ny, to_c)

    def third(t, d):
        sent[t, ("d", d)].wait_recv()
        forward(t, ("cd", d), zo[d], nx, ny, to_c)

    owns = []
    for t in range(count):
        for d in (1, 2, 3):
            send(t, ("z", d), pieces[t], spot(t, z, x, y), at(zs[d], x, y, c))
        fan(t, 0)
        own = pltpu.make_async_copy(pieces[t], spot(t, z, x, y), own_sem.at[t])
        own.start()
        owns.append(own)
    for step in range(count + 2):
        for d in (1, 3, 2):
            if step < count:
                sent[step, ("z", d)].wait_recv()
                fan(step, d)
        for d in (0, 1, 3, 2):
            if 0 <= step - 1 < count:
                second(step - 1, d)
        for d in (0, 1, 3, 2):
            if 0 <= step - 2 < count:
                third(step - 2, d)
    for t in range(count):
        for kind in ("c", "cx", "cy", "cd"):
            for d in range(4):
                sent[t, (kind, d)].wait_recv()
    for copy in sent.values():
        copy.wait_send()
    for own in owns:
        own.wait()


FIRST_X = (0, 3)
KEYS = {("z", d): d - 1 for d in (1, 2, 3)}
for kind in ("x", "y", "c", "d", "cx", "cy", "cd"):
    for d in range(4):
        KEYS[kind, d] = len(KEYS)


def gather_all(pieces, flats, layers):
    dims = tuple((p.shape[1], p.shape[2], f) for p, f in zip(pieces, flats))
    shapes = [
        jax.ShapeDtypeStruct(
            (p.shape[0], p.shape[1] * 32, p.shape[2])
            if f
            else (p.shape[0], p.shape[1] * 16, p.shape[2] * 2),
            p.dtype,
        )
        for p, f in zip(pieces, flats)
    ]
    count = len(pieces)
    anywhere = pl.BlockSpec(memory_space=pl.ANY)
    return pl.pallas_call(
        functools.partial(gather_kernel, dims),
        out_shape=shapes,
        in_specs=[anywhere] * count,
        out_specs=[anywhere] * count,
        scratch_shapes=[
            pltpu.SemaphoreType.DMA((count, len(KEYS))),
            pltpu.SemaphoreType.DMA((count, len(KEYS))),
            pltpu.SemaphoreType.DMA((count,)),
        ],
        compiler_params=pltpu.CompilerParams(collective_id=0, has_side_effects=True),
        name="gather_weights",
    )(*pieces)

RS_KEYS = {"core": 0}
for stage in ("one", "two"):
    for d in range(4):
        RS_KEYS[stage, d] = len(RS_KEYS)
for d in (1, 2, 3):
    RS_KEYS["z", d] = len(RS_KEYS)


def reduce_kernel(dims, *refs):
    count = len(dims)
    grads, outs, total_out = refs[:count], refs[count : 2 * count], refs[2 * count]
    rest = refs[2 * count + 1 :]
    own, from_core, one_y, one_x, two, from_z = (
        rest[i * count : (i + 1) * count] for i in range(6)
    )
    square, sq_plane, sq_z, send_sem, recv_sem, own_sem, sq_send, sq_recv = rest[6 * count :]
    z, x, y, c = place()
    nx, ny, nc = 1 - x, 1 - y, 1 - c
    zs = [z] + [(z + d) % 4 for d in (1, 2, 3)]
    to_x, to_y, to_c = at(z, nx, y, c), at(z, x, ny, c), at(z, x, y, nc)
    plane = plane_partners(z, x, y, c)
    greet([at(zs[d], x, y, c) for d in (1, 2, 3)] + plane)
    sent = {}

    def send(t, key, src, dst, dev):
        k = RS_KEYS[key]
        copy = pltpu.make_async_remote_copy(
            src_ref=src,
            dst_ref=dst,
            send_sem=send_sem.at[t, k],
            recv_sem=recv_sem.at[t, k],
            device_id=dev,
            device_id_type=MESH,
        )
        copy.start()
        sent[t, key] = copy

    owns = []
    for t in range(count):
        send(t, "core", grads[t].at[:, nc], from_core[t], to_c)
        copy = pltpu.make_async_copy(grads[t].at[:, c], own[t], own_sem.at[t])
        copy.start()
        owns.append(copy)

    def cols(t, yy):
        width = dims[t][1]
        return pl.ds(pl.multiple_of(yy * width, width), width)

    def add(ref, other):
        ref[...] = (ref[...].astype(jnp.float32) + other.astype(jnp.float32)).astype(ref.dtype)

    def stage_one(t):
        owns[t].wait()
        sent[t, "core"].wait_recv()
        for d in (2, 3, 1, 0):
            strip = own[t].at[pl.ds(zs[d] * 2, 2)]
            add(strip, from_core[t][pl.ds(zs[d] * 2, 2)])
            if d in FIRST_X:
                send(t, ("one", d), strip.at[:, :, cols(t, ny)], one_y[t].at[FIRST_X.index(d)], to_y)
            else:
                send(t, ("one", d), strip.at[nx], one_x[t].at[d - 1], to_x)

    def stage_two(t):
        for d in (2, 3, 1, 0):
            sent[t, ("one", d)].wait_recv()
            sent[t, ("one", d)].wait_send()
            strip = own[t].at[pl.ds(zs[d] * 2, 2)]
            if d in FIRST_X:
                add(strip.at[:, :, cols(t, y)], one_y[t][FIRST_X.index(d)])
                send(t, ("two", d), strip.at[nx, :, cols(t, y)], two[t].at[d], to_x)
            else:
                add(strip.at[x], one_x[t][d - 1])
                send(t, ("two", d), strip.at[x, :, cols(t, ny)], two[t].at[d], to_y)

    def stage_three(t):
        for d in (2, 3, 1, 0):
            sent[t, ("two", d)].wait_recv()
            block = own[t].at[zs[d] * 2 + x, :, cols(t, y)]
            add(block, two[t][d])
            if d > 0:
                send(t, ("z", d), block, from_z[t].at[d - 1], at(zs[d], x, y, c))

    def stage_four(t):
        value = own[t][z * 2 + x, :, cols(t, y)].astype(jnp.float32)
        for d in (1, 2, 3):
            sent[t, ("z", d)].wait_recv()
            value = value + from_z[t][d - 1].astype(jnp.float32)
        outs[t][...] = value
        squares = value * value
        rows, width = dims[t]
        part = jnp.sum(squares.reshape(rows // 8, 8, width), axis=0)
        folded = part[:, :128]
        for j in range(1, width // 128):
            folded = folded + part[:, j * 128 : (j + 1) * 128]
        return folded

    total = jnp.zeros((8, 128), jnp.float32)
    for step in range(count + 3):
        if step < count:
            stage_one(step)
        if 0 <= step - 1 < count:
            stage_two(step - 1)
        if 0 <= step - 2 < count:
            stage_three(step - 2)
        if 0 <= step - 3 < count:
            total = total + stage_four(step - 3)
    square[0] = total
    copies = []
    for d in (1, 2, 3):
        copy = pltpu.make_async_remote_copy(
            src_ref=square.at[0],
            dst_ref=sq_z.at[d - 1],
            send_sem=sq_send.at[d - 1],
            recv_sem=sq_recv.at[d - 1],
            device_id=at(zs[d], x, y, c),
            device_id_type=MESH,
        )
        copy.start()
        copies.append(copy)
    for d in (1, 2, 3):
        copies[d - 1].wait_recv()
        total = total + sq_z[d - 1]
    square[1] = total
    for j, dev in enumerate(plane):
        copy = pltpu.make_async_remote_copy(
            src_ref=square.at[1],
            dst_ref=sq_plane.at[j],
            send_sem=sq_send.at[3 + j],
            recv_sem=sq_recv.at[3 + j],
            device_id=dev,
            device_id_type=MESH,
        )
        copy.start()
        copies.append(copy)
    for j in range(len(plane)):
        copies[3 + j].wait_recv()
        total = total + sq_plane[j]
    total_out[...] = total
    for (t, key), copy in sent.items():
        if not (isinstance(key, tuple) and key[0] == "one"):
            copy.wait_send()
    for copy in copies:
        copy.wait_send()


def plane_partners(z, x, y, c):
    out = []
    for d in range(1, 8):
        dx, dy, dc = d // 4, (d // 2) % 2, d % 2
        out.append(at(z, 1 - x if dx else x, 1 - y if dy else y, 1 - c if dc else c))
    return out


def reduce_all(grads):
    dims = tuple((g.shape[2], g.shape[3] // 2) for g in grads)
    count = len(grads)
    kind = grads[0].dtype
    vm = lambda *s: pltpu.VMEM(s, kind)
    scratch = (
        [vm(8, r, 2 * w) for r, w in dims]
        + [vm(8, r, 2 * w) for r, w in dims]
        + [vm(2, 2, r, w) for r, w in dims]
        + [vm(2, r, 2 * w) for r, w in dims]
        + [vm(4, r, w) for r, w in dims]
        + [vm(3, r, w) for r, w in dims]
        + [
            pltpu.VMEM((2, 8, 128), jnp.float32),
            pltpu.VMEM((7, 8, 128), jnp.float32),
            pltpu.VMEM((3, 8, 128), jnp.float32),
            pltpu.SemaphoreType.DMA((count, len(RS_KEYS))),
            pltpu.SemaphoreType.DMA((count, len(RS_KEYS))),
            pltpu.SemaphoreType.DMA((count,)),
            pltpu.SemaphoreType.DMA((10,)),
            pltpu.SemaphoreType.DMA((10,)),
        ]
    )
    return pl.pallas_call(
        functools.partial(reduce_kernel, dims),
        out_shape=[jax.ShapeDtypeStruct((r, w), jnp.float32) for r, w in dims]
        + [jax.ShapeDtypeStruct((8, 128), jnp.float32)],
        in_specs=[pl.BlockSpec(memory_space=pl.ANY)] * count,
        out_specs=[pl.BlockSpec(memory_space=pltpu.VMEM)] * (count + 1),
        scratch_shapes=scratch,
        compiler_params=pltpu.CompilerParams(
            collective_id=1, has_side_effects=True, vmem_limit_bytes=60 * 2**20
        ),
        name="reduce_gradients",
    )(*grads)

HD = 64


def flip(z, x, y, c, d):
    dx, dy, dc = d // 4, (d // 2) % 2, d % 2
    return 1 - x if dx else x, 1 - y if dy else y, 1 - c if dc else c


class Exchange:
    def __init__(self, coef, send_all, got, sums, got_z, back, result, sems, reverse):
        self.coef, self.reverse = coef, reverse
        self.mine, self.got, self.sums = send_all, got, sums
        self.got_z, self.back, self.result = got_z, back, result
        self.sems = sems
        self.z, self.x, self.y, self.c = place()
        self.index = self.x * 4 + self.y * 2 + self.c
        self.copies = []

    def partners(self):
        z, x, y, c = self.z, self.x, self.y, self.c
        return [at((z + d) % 4, x, y, c) for d in (1, 2, 3)] + plane_partners(z, x, y, c)

    def send(self, k, src, dst, dev):
        copy = pltpu.make_async_remote_copy(
            src_ref=src,
            dst_ref=dst,
            send_sem=self.sems[0].at[k],
            recv_sem=self.sems[1].at[k],
            device_id=dev,
            device_id_type=MESH,
        )
        copy.start()
        self.copies.append(copy)

    def scatter(self):
        self.got[self.index] = self.mine[self.index]
        for d in range(1, 8):
            nx, ny, nc = flip(self.z, self.x, self.y, self.c, d)
            self.send(
                d - 1,
                self.mine.at[nx * 4 + ny * 2 + nc],
                self.got.at[self.index],
                at(self.z, nx, ny, nc),
            )

    def across(self):
        for k in range(7):
            self.copies[k].wait_recv()
        for d in (1, 2, 3):
            other = (self.z + d) % 4
            total = jnp.zeros(self.got.shape[1:], jnp.float32)
            for j in range(8):
                total = total + self.coef[8 + d, j] * self.got[j].astype(jnp.float32)
            self.sums[d - 1] = total.astype(jnp.bfloat16)
            self.send(
                6 + d,
                self.sums.at[d - 1],
                self.got_z.at[d - 1],
                at(other, self.x, self.y, self.c),
            )

    def gather(self):
        for k in (7, 8, 9):
            self.copies[k].wait_recv()
        parts = [self.got[j].astype(jnp.float32) for j in range(8)]
        parts += [self.got_z[d].astype(jnp.float32) for d in range(3)]
        for i in range(8):
            total = jnp.zeros(self.got.shape[1:], jnp.float32)
            span = range(i + 1, 8) if self.reverse else range(i)
            for j in list(span) + [8, 9, 10]:
                total = total + self.coef[i, j] * parts[j]
            self.back[i] = total.astype(jnp.bfloat16)
        self.result[self.index] = self.back[self.index]
        for d in range(1, 8):
            nx, ny, nc = flip(self.z, self.x, self.y, self.c, d)
            self.send(
                9 + d,
                self.back.at[nx * 4 + ny * 2 + nc],
                self.result.at[self.index],
                at(self.z, nx, ny, nc),
            )

    def finish(self):
        for k in range(10, 17):
            self.copies[k].wait_recv()
        for copy in self.copies:
            copy.wait_send()


def exchange_scratch(width):
    return [
        pltpu.VMEM((8, 16, width), jnp.bfloat16),
        pltpu.VMEM((8, 16, width), jnp.bfloat16),
        pltpu.VMEM((3, 16, width), jnp.bfloat16),
        pltpu.VMEM((3, 16, width), jnp.bfloat16),
        pltpu.VMEM((8, 16, width), jnp.bfloat16),
        pltpu.VMEM((8, 16, width), jnp.bfloat16),
        pltpu.SemaphoreType.DMA((17,)),
        pltpu.SemaphoreType.DMA((17,)),
    ]


def mm(a, b):
    return lax.dot_general(a, b, (((1,), (0,)), ((), ())), preferred_element_type=jnp.float32)


def mm_nt(a, b):
    return lax.dot_general(a, b, (((1,), (1,)), ((), ())), preferred_element_type=jnp.float32)


def low_lanes(shape):
    return lax.broadcasted_iota(jnp.int32, shape, len(shape) - 1) < HD


def lane_is(shape, h):
    return lax.broadcasted_iota(jnp.int32, shape, len(shape) - 1) == h


def pair_cols(p):
    return slice(p * 128, (p + 1) * 128)


def pack_state(ref, p, kind, block, extra):
    first = kind * 64
    low = low_lanes((64, 128))
    packed = jnp.where(low, block[:64, :128], block[64:, :128]).astype(jnp.bfloat16)
    for s in range(4):
        ref[kind * 4 + s, :, pair_cols(p)] = packed[s * 16 : (s + 1) * 16]
    if extra is None:
        extra = jnp.zeros((64, 128), jnp.float32)
    extra = extra + jnp.where(lane_is((64, 128), 2 * p), block[:64, 128:], 0.0)
    return extra + jnp.where(lane_is((64, 128), 2 * p + 1), block[64:, 128:], 0.0)


def store_extra(ref, kind, extra, width):
    extra = extra.astype(jnp.bfloat16)
    for s in range(4):
        ref[kind * 4 + s, :, width - 128 :] = extra[s * 16 : (s + 1) * 16]


def unpack_state(ref, p, kind, width):
    packed = jnp.concatenate([ref[kind * 4 + s, :, pair_cols(p)] for s in range(4)], axis=0)
    sums = jnp.concatenate([ref[kind * 4 + s, :, width - 128 :] for s in range(4)], axis=0)
    low = low_lanes((64, 128))
    zero = jnp.zeros((64, 128), jnp.bfloat16)
    top = jnp.concatenate(
        [jnp.where(low, packed, zero), jnp.where(lane_is((64, 128), 2 * p), sums, zero)], axis=1
    )
    bottom = jnp.concatenate(
        [jnp.where(low, zero, packed), jnp.where(lane_is((64, 128), 2 * p + 1), sums, zero)],
        axis=1,
    )
    return jnp.concatenate([top, bottom], axis=0)


def spread(values, p):
    rows = values.shape[0]
    first = jnp.broadcast_to(values[:, 2 * p : 2 * p + 1], (rows, 128))
    second = jnp.broadcast_to(values[:, 2 * p + 1 : 2 * p + 2], (rows, 128))
    return jnp.where(low_lanes((rows, 128)), first, second)


def attend_kernel(pairs, coef, q_ref, k_ref, v_ref, w_ref, aux_ref, ob_ref, den_ref, state_ref, num, *rest):
    rows = q_ref.shape[0]
    half = rows // 2
    width = pairs * 128 + 128
    ex = Exchange(coef, *rest[:6], rest[6:8], False)
    greet(ex.partners())
    cos, sin = aux_ref[:, 0:1], aux_ref[:, 1:2]
    follow, tail = aux_ref[:, 2:3], aux_ref[:, 3:4]
    ones = jnp.ones((rows, 128), jnp.bfloat16)
    extras = [None, None]
    for p in range(pairs):
        kp = k_ref[:, pair_cols(p)].astype(jnp.float32) * tail
        rhs = jnp.concatenate([v_ref[:, pair_cols(p)], ones], axis=1)
        for kind, angle in enumerate((cos, sin)):
            block = mm((kp * angle).T.astype(jnp.bfloat16), rhs)
            extras[kind] = pack_state(ex.mine, p, kind, block, extras[kind])
    for kind in range(2):
        store_extra(ex.mine, kind, extras[kind], width)
    ex.scatter()

    def inner(p):
        kp = k_ref[:, pair_cols(p)]
        vp = v_ref[:, pair_cols(p)]
        low = low_lanes((rows, 128))
        zero = jnp.zeros((rows, 128), jnp.bfloat16)
        parts = []
        for e in range(2):
            h = 2 * p + e
            qh = jnp.where(low if e == 0 else ~low, q_ref[:, pair_cols(p)], zero)
            rhs = jnp.concatenate([vp, lane_is((rows, 128), h).astype(jnp.bfloat16)], axis=1)
            top = (mm_nt(qh[:half], kp[:half]) * w_ref[:half, :half]).astype(jnp.bfloat16)
            bottom = (mm_nt(qh[half:], kp) * w_ref[half:, :]).astype(jnp.bfloat16)
            parts.append(jnp.concatenate([mm(top, rhs[:half]), mm(bottom, rhs)], axis=0))
        num[:, pair_cols(p)] = jnp.where(low, parts[0][:, :128], parts[1][:, :128])
        dens = parts[0][:, 128:] + parts[1][:, 128:]
        if p == 0:
            den_ref[...] = dens
        else:
            den_ref[...] += dens

    third = max(1, pairs // 3)
    for p in range(third):
        inner(p)
    ex.across()
    for p in range(third, 2 * third):
        inner(p)
    ex.gather()
    for p in range(2 * third, pairs):
        inner(p)
    ex.finish()
    state_ref[...] = ex.result[...]
    den = den_ref[...]
    cf, sf = cos * follow, sin * follow
    for p in range(pairs):
        qp = q_ref[:, pair_cols(p)]
        extra = cf * mm(qp, unpack_state(ex.result, p, 0, width))
        extra += sf * mm(qp, unpack_state(ex.result, p, 1, width))
        num[:, pair_cols(p)] += extra[:, :128]
        den = den + extra[:, 128:]
    den_ref[...] = den
    inv = 1.0 / jnp.maximum(den, 1.0)
    for p in range(pairs):
        ob_ref[:, pair_cols(p)] = (num[:, pair_cols(p)] * spread(inv, p)).astype(jnp.bfloat16)


def attend(q, k, v, w, aux, coef):
    rows, model = q.shape
    pairs = model // 128
    width = model + 128
    vmem = pl.BlockSpec(memory_space=pltpu.VMEM)
    return pl.pallas_call(
        functools.partial(attend_kernel, pairs),
        out_shape=[
            jax.ShapeDtypeStruct((rows, model), jnp.bfloat16),
            jax.ShapeDtypeStruct((rows, 128), jnp.float32),
            jax.ShapeDtypeStruct((8, 16, width), jnp.bfloat16),
        ],
        in_specs=[pl.BlockSpec(memory_space=pltpu.SMEM)] + [vmem] * 5,
        out_specs=[vmem] * 3,
        scratch_shapes=[pltpu.VMEM((rows, model), jnp.float32)] + exchange_scratch(width),
        compiler_params=pltpu.CompilerParams(
            collective_id=2, has_side_effects=True, vmem_limit_bytes=48 * 2**20
        ),
        name="attend",
    )(coef, q, k, v, w, aux)


def attend_back_kernel(
    pairs, coef, q_ref, k_ref, v_ref, dob_ref, ob_ref, den_ref, state_ref, w_ref, aux_ref,
    out_ref, dn_ref, dd_ref, *rest,
):
    rows = q_ref.shape[0]
    half = rows // 2
    model = pairs * 128
    width = model + 128
    ex = Exchange(coef, *rest[:6], rest[6:8], True)
    greet(ex.partners())
    cos, sin = aux_ref[:, 0:1], aux_ref[:, 1:2]
    follow, tail = aux_ref[:, 2:3], aux_ref[:, 3:4]
    low = low_lanes((rows, 128))
    zero = jnp.zeros((rows, 128), jnp.bfloat16)
    den = den_ref[...]
    inv = 1.0 / jnp.maximum(den, 1.0)
    dots = jnp.zeros((rows, 128), jnp.float32)
    for p in range(pairs):
        dob = dob_ref[:, pair_cols(p)].astype(jnp.float32)
        dn_ref[:, pair_cols(p)] = (dob * spread(inv, p)).astype(jnp.bfloat16)
        both = dob * ob_ref[:, pair_cols(p)].astype(jnp.float32)
        first = jnp.sum(jnp.where(low, both, 0.0), axis=1, keepdims=True)
        second = jnp.sum(jnp.where(low, 0.0, both), axis=1, keepdims=True)
        dots = dots + jnp.where(lane_is((rows, 128), 2 * p), first, 0.0)
        dots = dots + jnp.where(lane_is((rows, 128), 2 * p + 1), second, 0.0)
    dden = jnp.where(den > 1.0, -dots * inv, 0.0)
    dd_ref[...] = dden
    dden_low = dden.astype(jnp.bfloat16)
    cf, sf = cos * follow, sin * follow
    extras = [None, None]
    for p in range(pairs):
        qp = q_ref[:, pair_cols(p)].astype(jnp.float32)
        rhs = jnp.concatenate([dn_ref[:, pair_cols(p)], dden_low], axis=1)
        for kind, angle in enumerate((cf, sf)):
            block = mm((qp * angle).T.astype(jnp.bfloat16), rhs)
            extras[kind] = pack_state(ex.mine, p, kind, block, extras[kind])
    for kind in range(2):
        store_extra(ex.mine, kind, extras[kind], width)
    ex.scatter()

    def inner(p):
        qp, kp, vp = q_ref[:, pair_cols(p)], k_ref[:, pair_cols(p)], v_ref[:, pair_cols(p)]
        dob = dob_ref[:, pair_cols(p)]
        dnp = dn_ref[:, pair_cols(p)]
        q_t = qp.astype(jnp.float32).T.astype(jnp.bfloat16)
        dn_t = dnp.astype(jnp.float32).T.astype(jnp.bfloat16)
        dq_parts, dk_parts, dv_parts = [], [], []
        for e in range(2):
            h = 2 * p + e
            mask = low if e == 0 else ~low
            span = slice(e * HD, (e + 1) * HD)
            qh = jnp.where(mask, qp, zero)
            doh = jnp.where(mask, dob, zero)
            scale, shift = inv[:, h : h + 1], dd_ref[:, h : h + 1]

            def tile(at_rows, at_cols):
                weight = w_ref[at_rows, at_cols]
                s = (mm_nt(qh[at_rows], kp[at_cols]) * weight).astype(jnp.bfloat16)
                t = mm_nt(doh[at_rows], vp[at_cols])
                ds = (t * scale[at_rows] + shift[at_rows]).astype(jnp.bfloat16)
                g = (ds.astype(jnp.float32) * weight).astype(jnp.bfloat16)
                return s, g

            up, down, every = slice(0, half), slice(half, rows), slice(0, rows)
            s_top, g_top = tile(up, up)
            s_low, g_low = tile(down, every)
            dq_parts.append(jnp.concatenate([mm(g_top, kp[:half]), mm(g_low, kp)], axis=0))

            def turned(left, top, bottom):
                whole = mm(left[span, half:], bottom)
                first = whole[:, :half] + mm(left[span, :half], top)
                return jnp.concatenate([first, whole[:, half:]], axis=1)

            dk_parts.append(turned(q_t, g_top, g_low))
            dv_parts.append(turned(dn_t, s_top, s_low))
        base = p * 128
        dq = jnp.where(low, dq_parts[0], dq_parts[1])
        right = jnp.concatenate([dnp, dden_low], axis=1)
        dq += cf * mm_nt(right, unpack_state(state_ref, p, 0, width))
        dq += sf * mm_nt(right, unpack_state(state_ref, p, 1, width))
        out_ref[:, base : base + 128] = dq.astype(jnp.bfloat16)
        keep[0][:, base : base + 128] = jnp.concatenate(dk_parts, axis=0).T
        keep[1][:, base : base + 128] = jnp.concatenate(dv_parts, axis=0).T

    keep = rest[8:10]
    dden_low = dd_ref[...].astype(jnp.bfloat16)
    third = max(1, pairs // 3)
    for p in range(third):
        inner(p)
    ex.across()
    for p in range(third, 2 * third):
        inner(p)
    ex.gather()
    for p in range(2 * third, pairs):
        inner(p)
    ex.finish()
    ct, st, valid = cos * tail, sin * tail, aux_ref[:, 4:5]
    ones = jnp.ones((rows, 128), jnp.bfloat16)
    for p in range(pairs):
        base = p * 128
        dsc, dss = unpack_state(ex.result, p, 0, width), unpack_state(ex.result, p, 1, width)
        right = jnp.concatenate([v_ref[:, pair_cols(p)], ones], axis=1)
        dk = keep[0][:, base : base + 128] + ct * mm_nt(right, dsc) + st * mm_nt(right, dss)
        kp = k_ref[:, pair_cols(p)]
        dv = keep[1][:, base : base + 128] + ct * mm(kp, dsc[:, :128]) + st * mm(kp, dss[:, :128])
        out_ref[:, model + base : model + base + 128] = (dk * valid).astype(jnp.bfloat16)
        out_ref[:, 2 * model + base : 2 * model + base + 128] = dv.astype(jnp.bfloat16)


def attend_back(q, k, v, dob, ob, den, state, w, aux, coef):
    rows, model = q.shape
    pairs = model // 128
    width = model + 128
    vmem = pl.BlockSpec(memory_space=pltpu.VMEM)
    return pl.pallas_call(
        functools.partial(attend_back_kernel, pairs),
        out_shape=jax.ShapeDtypeStruct((rows, 3 * model), jnp.bfloat16),
        in_specs=[pl.BlockSpec(memory_space=pltpu.SMEM)] + [vmem] * 9,
        out_specs=vmem,
        scratch_shapes=[
            pltpu.VMEM((rows, model), jnp.bfloat16),
            pltpu.VMEM((rows, 128), jnp.float32),
        ]
        + exchange_scratch(width)
        + [pltpu.VMEM((rows, model), jnp.float32)] * 2,
        compiler_params=pltpu.CompilerParams(
            collective_id=3, has_side_effects=True, vmem_limit_bytes=48 * 2**20
        ),
        name="attend_back",
    )(coef, q, k, v, dob, ob, den, state, w, aux)


def stream_meta(lengths, row_ids):
    seq_count = lengths.shape[0]
    seq_ends = jnp.cumsum(lengths, dtype=jnp.int32)
    seq_starts = seq_ends - lengths
    begun = seq_starts[None, :] <= row_ids[:, None]
    seg_raw = jnp.sum(begun.astype(jnp.int32), axis=1, dtype=jnp.int32) - 1
    seg_start = jnp.max(jnp.where(begun, seq_starts[None, :], 0), axis=1)
    inside = row_ids < seq_ends[seq_count - 1]
    seg_ids = jnp.where(inside, seg_raw, seq_count)
    offsets = jnp.where(inside, row_ids - seg_start, 0).astype(jnp.float32)
    angles = offsets * (0.5 * math.pi / LONGEST)
    return (seg_ids, jnp.cos(angles), jnp.sin(angles), inside.astype(jnp.float32))


def layer_norm(inputs_row, gain_row, shift_row):
    mean_row = jnp.mean(inputs_row, axis=-1, keepdims=True)
    centered = inputs_row - mean_row
    variance = jnp.mean(centered * centered, axis=-1, keepdims=True)
    return centered * lax.rsqrt(variance + norm_eps) * gain_row + shift_row


def gelu_exact(inner_pre):
    return jax.nn.gelu(inner_pre, approximate=False)


def contract_rows(left, right):
    return lax.dot_general(
        left, right, (((0,), (0,)), ((), ())), preferred_element_type=jnp.float32
    )


def contract_cols(left, right):
    return lax.dot_general(
        left, right, (((1,), (1,)), ((), ())), preferred_element_type=jnp.float32
    )


def adam_step(weight, first_old, second_old, gradient, factor, step_rate, decay_coef):
    clipped = gradient * factor
    first_new = beta_one * first_old + (1.0 - beta_one) * clipped
    second_new = beta_two * second_old + (1.0 - beta_two) * clipped * clipped
    first_hat = first_new / (1.0 - beta_one**step_fixed)
    second_hat = second_new / (1.0 - beta_two**step_fixed)
    weight_new = weight - step_rate * (
        first_hat / (jnp.sqrt(second_hat) + adam_eps) + decay_coef * weight
    )
    return (weight_new, first_new, second_new)


def other_core(array):
    return lax.ppermute(array, "head", [(0, 1), (1, 0), (2, 3), (3, 2)])


def gather_plan(w_qkv, w_out, w_up, w_down, norm_params):
    first = lax.axis_index("head") % 2 == 0
    low = [a.astype(jnp.bfloat16) for a in (w_qkv, w_out, w_up, w_down)]
    halves = [(a[:, : a.shape[1] // 2], a[:, a.shape[1] // 2 :]) for a in low]
    keep = [jnp.where(first, a, b) for a, b in halves]
    give = [jnp.where(first, b, a) for a, b in halves]
    wide = other_core(jnp.concatenate(give[:3], axis=2))
    got = jnp.split(wide, (keep[0].shape[2], keep[0].shape[2] + keep[1].shape[2]), axis=2)
    got.append(other_core(give[3]))
    pieces = [
        jnp.where(first, jnp.concatenate([a, b], axis=2), jnp.concatenate([b, a], axis=2))
        for a, b in zip(keep, got)
    ]
    layers, _, part = norm_params.shape
    pieces.append(
        jnp.pad(
            norm_params.astype(jnp.bfloat16).reshape(1, layers, part),
            ((0, 0), (0, 16 - layers), (0, 128 - part)),
        )
    )
    fulls = gather_all(pieces, [False] * 5, layers)
    norm = fulls[4].reshape(8, 2, 16, 2, 128)[:, :, :layers, :, :part]
    norm = norm.transpose(2, 3, 1, 0, 4).reshape(layers, 4, 8 * part)
    return fulls[:4], norm


def reduce_plan(grads, norm_grad):
    first = lax.axis_index("head") % 2 == 0
    layers = len(grads)
    flat = []
    for layer in range(layers):
        for g in grads[layer]:
            flat.append(g.reshape(8, 2, g.shape[0] // 16, g.shape[1]))
    part = norm_grad.shape[2] // 8
    norm = norm_grad.astype(jnp.bfloat16).reshape(layers, 2, 2, 8, part).transpose(3, 2, 0, 1, 4)
    norm = jnp.pad(norm, ((0, 0), (0, 0), (0, 16 - layers), (0, 0), (0, 128 - part)))
    flat.append(norm.reshape(8, 2, 16, 256))
    *sums, norm_sum, squares = reduce_all(flat)
    kinds = len(grads[0])
    stacked = [jnp.stack([sums[l * kinds + i] for l in range(layers)]) for i in range(kinds)]
    halves = [(a[..., : a.shape[2] // 2], a[..., a.shape[2] // 2 :]) for a in stacked]
    keep = [jnp.where(first, a, b) for a, b in halves]
    give = [jnp.where(first, b, a) for a, b in halves]
    wide = other_core(jnp.concatenate(give[:3], axis=2))
    got = jnp.split(wide, (keep[0].shape[2], keep[0].shape[2] + keep[1].shape[2]), axis=2)
    got.append(other_core(give[3]))
    whole = [
        jnp.where(first, jnp.concatenate([a, b], axis=1), jnp.concatenate([b, a], axis=1))
        for a, b in zip(keep, got)
    ]
    return whole, norm_sum[:layers, :part].reshape(layers, 1, part), jnp.sum(squares)


def exchange_plan(seg_last, seg_before, seg_plane, reverse):
    dp = lax.axis_index("dp")
    z = dp // 2
    last = lax.dynamic_slice(seg_last, (z * 8,), (8,))
    before = lax.dynamic_slice(seg_before, (z * 8,), (8,))
    order = jnp.arange(8)
    inside = (before[:, None] == last[None, :]) & (order[:, None] > order[None, :])
    ends = seg_last[7::8]
    planes = jnp.arange(4)
    to_end = last == ends[z]
    back = (before[:, None] == ends[None, :]) & (planes[None, :] < z)
    coef = jnp.zeros((16, 16), jnp.float32)
    shift = jnp.arange(1, 4)
    if reverse:
        coef = coef.at[:8, :8].set(inside.T.astype(jnp.float32))
        source = (z - shift) % 4
        coef = coef.at[:8, 8:11].set((to_end[:, None] & (source > z)[None, :]).astype(jnp.float32))
        target = (z + shift) % 4
        coef = coef.at[9:12, :8].set(back[:, target].T.astype(jnp.float32))
    else:
        coef = coef.at[:8, :8].set(inside.astype(jnp.float32))
        source = (z - shift) % 4
        coef = coef.at[:8, 8:11].set(back[:, source].astype(jnp.float32))
        coef = coef.at[9:12, :8].set(jnp.broadcast_to(to_end.astype(jnp.float32), (3, 8)))
    return coef


class LocalPlan:
    def __init__(self, lengths, rows):
        me = lax.axis_index("dp") * 4 + lax.axis_index("head")
        first_row = me * rows
        seg, cos, sin, valid = stream_meta(lengths, first_row + jnp.arange(rows, dtype=jnp.int32))
        starts = jnp.arange(32, dtype=jnp.int32) * rows
        before = stream_meta(lengths, starts - 1)[0]
        last = stream_meta(lengths, starts + rows - 1)[0]
        follow = (seg == before[me]).astype(jnp.float32)
        tail = (seg == last[me]).astype(jnp.float32)
        place_ids = jnp.arange(rows)
        allowed = (seg[:, None] == seg[None, :]) & (place_ids[None, :] <= place_ids[:, None])
        close = cos[:, None] * cos[None, :] + sin[:, None] * sin[None, :]
        self.valid = valid
        self.weights = jnp.where(allowed, close, 0.0)
        zero = jnp.zeros_like(cos)
        self.aux = jnp.stack([cos, sin, follow, tail, valid, zero, zero, zero], axis=1)
        self.ahead = exchange_plan(last, before, None, False)
        self.behind = exchange_plan(last, before, None, True)

    def attend(self, q, k, v):
        ob, den, state = attend(q, k, v, self.weights, self.aux, self.ahead)
        return ob, (q, k, v, ob, den, state)

    def attend_back(self, kept, dob):
        q, k, v, ob, den, state = kept
        return attend_back(q, k, v, dob, ob, den, state, self.weights, self.aux, self.behind)


def block_attention(queries, key_rows, value_rows, weights, aux):
    cos, sin, tail = aux[:, 0], aux[:, 1], aux[:, 3]
    raw = jnp.einsum("ihe,jhe->hij", queries, key_rows, preferred_element_type=jnp.float32)
    scores = (raw * weights[None]).astype(jnp.bfloat16)
    num = jnp.einsum("hij,jhe->ihe", scores, value_rows, preferred_element_type=jnp.float32)
    den = jnp.transpose(jnp.sum(scores.astype(jnp.float32), axis=2))
    out = []
    for angle in (cos, sin):
        turned = key_rows.astype(jnp.float32) * (angle * tail)[:, None, None]
        out.append(
            jnp.einsum(
                "jhe,jhf->hef", turned, value_rows.astype(jnp.float32), precision=exact_mode
            )
        )
        out.append(jnp.sum(turned, axis=0))
    return num, den, tuple(out)


def finish_rows(queries, num, den, state, aux):
    cos, sin, follow = aux[:, 0], aux[:, 1], aux[:, 2]
    for angle, kv, ks in ((cos, state[0], state[1]), (sin, state[2], state[3])):
        turned = queries.astype(jnp.float32) * (angle * follow)[:, None, None]
        num = num + jnp.einsum("ihe,hef->ihf", turned, kv, precision=exact_mode)
        den = den + jnp.einsum("ihe,he->ih", turned, ks, precision=exact_mode)
    return num / jnp.maximum(den, 1.0)[:, :, None]


class WidePlan(LocalPlan):
    def __init__(self, lengths, rows):
        parts = lax.axis_size("dp") * lax.axis_size("head")
        me = lax.axis_index("dp") * lax.axis_size("head") + lax.axis_index("head")
        seg, cos, sin, valid = stream_meta(
            lengths, me * rows + jnp.arange(rows, dtype=jnp.int32)
        )
        starts = jnp.arange(parts, dtype=jnp.int32) * rows
        before = stream_meta(lengths, starts - 1)[0]
        last = stream_meta(lengths, starts + rows - 1)[0]
        follow = (seg == before[me]).astype(jnp.float32)
        tail = (seg == last[me]).astype(jnp.float32)
        place_ids = jnp.arange(rows)
        allowed = (seg[:, None] == seg[None, :]) & (place_ids[None, :] <= place_ids[:, None])
        close = cos[:, None] * cos[None, :] + sin[:, None] * sin[None, :]
        self.valid = valid
        self.weights = jnp.where(allowed, close, 0.0)
        self.aux = jnp.stack([cos, sin, follow, tail, valid], axis=1)
        devices = jnp.arange(parts)
        self.ahead = ((last == before[me]) & (devices < me)).astype(jnp.float32)
        self.behind = ((before == last[me]) & (devices > me)).astype(jnp.float32)

    def masked(self, state, coef):
        def one(a):
            everything = lax.all_gather(a.astype(jnp.bfloat16), ("dp", "head"))
            return jnp.einsum(
                "d,d...->...",
                coef.astype(jnp.bfloat16),
                everything,
                preferred_element_type=jnp.float32,
            )

        return jax.tree.map(one, state)

    def attend(self, q, k, v):
        rows, model = q.shape
        split = lambda a: a.reshape(rows, HEADS, model // HEADS)
        local = lambda *a: block_attention(*a, self.weights, self.aux)
        (num, den, state), pull = jax.vjp(local, split(q), split(k), split(v))
        state = self.masked(state, self.ahead)
        finish = lambda *a: finish_rows(*a, self.aux)
        out, finish_pull = jax.vjp(finish, split(q), num, den, state)
        return out.astype(jnp.bfloat16).reshape(rows, model), (pull, finish_pull)

    def attend_back(self, kept, dob):
        pull, finish_pull = kept
        rows, model = dob.shape
        grad = dob.astype(jnp.float32).reshape(rows, HEADS, model // HEADS)
        dq_one, dnum, dden, dstate = finish_pull(grad)
        dstate = self.masked(dstate, self.behind)
        dq, dk, dv = pull((dnum, dden, dstate))
        dq = dq.astype(jnp.float32) + dq_one.astype(jnp.float32)
        dk = dk.astype(jnp.float32) * self.valid[:, None, None]
        out = [a.reshape(rows, model).astype(jnp.bfloat16) for a in (dq, dk, dv)]
        return jnp.concatenate(out, axis=1)


def wide_gather(w_qkv, w_out, w_up, w_down, norm_params):
    fulls = []
    for a in (w_qkv, w_out, w_up, w_down):
        part = lax.all_gather(a.astype(jnp.bfloat16), "dp", axis=1, tiled=True)
        fulls.append(lax.all_gather(part, "head", axis=2, tiled=True))
    norm = lax.all_gather(norm_params.astype(jnp.bfloat16), "dp", axis=2, tiled=True)
    return fulls, lax.all_gather(norm, "head", axis=1, tiled=True)


def wide_reduce(grads, norm_grad):
    def one(a):
        part = lax.psum_scatter(a, "head", scatter_dimension=1, tiled=True)
        part = lax.psum_scatter(part.astype(jnp.float32), "dp", scatter_dimension=0, tiled=True)
        return part

    whole = [jnp.stack([one(layer[i]) for layer in grads]) for i in range(len(grads[0]))]
    part = lax.psum_scatter(norm_grad, "head", scatter_dimension=1, tiled=True)
    norm = lax.psum_scatter(part, "dp", scatter_dimension=2, tiled=True)
    squares = sum([jnp.sum(a * a) for a in whole + [norm]])
    return whole, norm, lax.psum(squares, ("dp", "head"))


def body(
    inputs, cotangent, lengths,
    w_qkv, m_qkv, v_qkv, w_out, m_out, v_out, w_up, m_up, v_up, w_down, m_down, v_down,
    norm_params, m_norm, v_norm,
):
    rows, model = inputs.shape
    layers = w_qkv.shape[0]
    near = lax.axis_size("dp") == 8 and lax.axis_size("head") == 4 and rows == 512
    plan = (LocalPlan if near else WidePlan)(lengths, rows)
    fulls, norm_full = (gather_plan if near else wide_gather)(
        w_qkv, w_out, w_up, w_down, norm_params
    )
    norm_full = norm_full.astype(jnp.float32)
    hidden = inputs.astype(jnp.float32)
    kept = []
    for layer in range(layers):
        qkv_w, out_w, up_w, down_w = (a[layer] for a in fulls)
        gains = norm_full[layer]
        acts = hidden.astype(jnp.bfloat16)
        mixed = jnp.dot(acts, qkv_w, preferred_element_type=jnp.float32)
        soft = jax.nn.softplus(mixed[:, : 2 * model]).astype(jnp.bfloat16)
        q = soft[:, :model]
        k = soft[:, model:] * plan.valid[:, None].astype(jnp.bfloat16)
        v = mixed[:, 2 * model :].astype(jnp.bfloat16)
        attended, attend_kept = plan.attend(q, k, v)
        first_in = hidden + jnp.dot(attended, out_w, preferred_element_type=jnp.float32)
        first_out = layer_norm(first_in, gains[0], gains[1])
        first_low = first_out.astype(jnp.bfloat16)
        inner = jnp.dot(first_low, up_w, preferred_element_type=jnp.float32)
        act = gelu_exact(inner).astype(jnp.bfloat16)
        second_in = first_out + jnp.dot(act, down_w, preferred_element_type=jnp.float32)
        kept.append((acts, mixed, attend_kept, attended, first_in, first_low, inner, act, second_in))
        hidden = layer_norm(second_in, gains[2], gains[3])
    grad_hidden = cotangent.astype(jnp.float32)
    grads = [None] * layers
    norm_grads = [None] * layers
    for layer in reversed(range(layers)):
        acts, mixed, attend_kept, attended, first_in, first_low, inner, act, second_in = kept[layer]
        qkv_w, out_w, up_w, down_w = (a[layer] for a in fulls)
        gains = norm_full[layer]
        _, pull_two = jax.vjp(layer_norm, second_in, gains[2], gains[3])
        grad_second, dgain_two, dshift_two = pull_two(grad_hidden)
        branch_two = grad_second.astype(jnp.bfloat16)
        dw_down = contract_rows(act, branch_two).astype(jnp.bfloat16)
        grad_act = contract_cols(branch_two, down_w)
        _, gelu_pull = jax.vjp(gelu_exact, inner)
        grad_inner = gelu_pull(grad_act)[0].astype(jnp.bfloat16)
        dw_up = contract_rows(first_low, grad_inner).astype(jnp.bfloat16)
        grad_first = grad_second + contract_cols(grad_inner, up_w)
        _, pull_one = jax.vjp(layer_norm, first_in, gains[0], gains[1])
        grad_first_in, dgain_one, dshift_one = pull_one(grad_first)
        branch = grad_first_in.astype(jnp.bfloat16)
        dw_out = contract_rows(attended, branch).astype(jnp.bfloat16)
        dob = contract_cols(branch, out_w).astype(jnp.bfloat16)
        grad_mixed = plan.attend_back(attend_kept, dob)
        slope = jax.nn.sigmoid(mixed[:, : 2 * model])
        grad_soft = (grad_mixed[:, : 2 * model].astype(jnp.float32) * slope).astype(jnp.bfloat16)
        grad_pre = jnp.concatenate([grad_soft, grad_mixed[:, 2 * model :]], axis=1)
        dw_qkv = contract_rows(acts, grad_pre).astype(jnp.bfloat16)
        grad_hidden = grad_first_in + contract_cols(grad_pre, qkv_w)
        grads[layer] = (dw_qkv, dw_out, dw_up, dw_down)
        norm_grads[layer] = jnp.stack([dgain_one, dshift_one, dgain_two, dshift_two])
    whole, norm_sum, squares = (reduce_plan if near else wide_reduce)(grads, jnp.stack(norm_grads))
    grad_norm = jnp.sqrt(squares)
    factor = clip_limit / jnp.maximum(grad_norm, clip_limit)
    new_qkv = adam_step(w_qkv, m_qkv, v_qkv, whole[0], factor, rate_matrix, decay_rate)
    new_out = adam_step(w_out, m_out, v_out, whole[1], factor, rate_outproj, decay_rate)
    new_up = adam_step(w_up, m_up, v_up, whole[2], factor, rate_matrix, decay_rate)
    new_down = adam_step(w_down, m_down, v_down, whole[3], factor, rate_matrix, decay_rate)
    new_norm = adam_step(norm_params, m_norm, v_norm, norm_sum, factor, rate_norm, 0.0)
    return (
        (hidden, grad_hidden, grad_norm.reshape(1))
        + new_qkv + new_out + new_up + new_down + new_norm
    )


def solution(mesh):
    rows = P(("dp", "head"), None)
    weight = P(None, "dp", "head")
    norm = P(None, "head", "dp")
    in_specs = (rows, rows, P()) + (weight,) * 12 + (norm,) * 3
    out_specs = (rows, rows, P()) + (weight,) * 12 + (norm,) * 3
    return jax.shard_map(body, mesh=mesh, in_specs=in_specs, out_specs=out_specs, check_vma=False)
```

```python
import functools
import math
from typing import Any, NamedTuple

import jax
import jax.numpy as jnp
from jax import lax
from jax.experimental import pallas as pl
from jax.experimental.pallas import tpu as pltpu
from jax.sharding import PartitionSpec as P

HEADS = 12
LONGEST = 8192
HD = 64

exact_mode = lax.Precision.HIGHEST
beta_one = 0.9
beta_two = 0.999
adam_eps = 1e-08
decay_rate = 0.1
rate_matrix = 0.1
rate_outproj = 0.5
rate_norm = 0.5
clip_limit = 1.0
norm_eps = 1e-05
step_fixed = 10.0

MESH = pl.DeviceIdType.MESH
FIRST_X = (0, 3)
NORM, QKV, OUT, UP, DOWN = range(5)
MATRICES = (QKV, OUT, UP, DOWN)
BY_Z, BY_X, BY_Y, BY_CORE, BY_CORNER, ON_X, ON_Y, ON_CORNER = range(8)
CORE, ONE, TWO, LAST = range(4)


def place():
    dp, hd = lax.axis_index("dp"), lax.axis_index("head")
    return dp // 2, dp % 2, hd // 2, hd % 2


def at(z, x, y, c):
    return (z * 2 + x, y * 2 + c)


def flip(x, y, c, d):
    dx, dy, dc = d // 4, (d // 2) % 2, d % 2
    return 1 - x if dx else x, 1 - y if dy else y, 1 - c if dc else c


def partners():
    z, x, y, c = place()
    out = [at((z + d) % 4, x, y, c) for d in (1, 2, 3)]
    return out + [at(z, *flip(x, y, c, d)) for d in range(1, 8)]


def greet():
    barrier = pltpu.get_barrier_semaphore()
    devices = partners()
    for dev in devices:
        pl.semaphore_signal(barrier, inc=1, device_id=dev, device_id_type=MESH)
    pl.semaphore_wait(barrier, len(devices))


class Links:
    def __init__(self, send_sem, recv_sem):
        self.send_sem, self.recv_sem, self.copies = send_sem, recv_sem, []
        self.left = set()

    def send(self, src, dst, dev):
        k = len(self.copies)
        copy = pltpu.make_async_remote_copy(
            src_ref=src,
            dst_ref=dst,
            send_sem=self.send_sem.at[k],
            recv_sem=self.recv_sem.at[k],
            device_id=dev,
            device_id_type=MESH,
        )
        copy.start()
        self.copies.append(copy)
        self.left.add(k)
        copy.number = k
        return copy

    def sent(self, copy):
        copy.wait_send()
        self.left.discard(copy.number)

    def finish(self):
        for k in sorted(self.left):
            self.copies[k].wait_send()


class Moves:
    def __init__(self, sem):
        self.sem, self.copies = sem, []
        self.left = []

    def start(self, src, dst):
        copy = pltpu.make_async_copy(src, dst, self.sem.at[len(self.copies)])
        copy.start()
        self.copies.append(copy)
        self.left.append(copy)
        return copy

    def wait(self, copy):
        if any(copy is other for other in self.left):
            copy.wait()
        self.left = [other for other in self.left if other is not copy]

    def finish(self):
        for copy in self.left:
            copy.wait()
        self.left = []


def region(kind, rows, cols, z, x, y, c):
    strip, head = z * 2 + x, y * 2 + c
    if kind in (QKV, OUT, NORM):
        first, left = (strip * 2 + c) * rows, y * cols
    elif kind == UP:
        first, left = strip * rows, head * cols
    else:
        first, left = head * rows, strip * cols
    return (
        pl.ds(pl.multiple_of(first, rows), rows),
        pl.ds(pl.multiple_of(left, cols), cols),
    )


def whole_shape(kind, rows, cols):
    if kind in (QKV, OUT, NORM):
        return rows * 16, cols * 2
    if kind == UP:
        return rows * 8, cols * 4
    return rows * 4, cols * 8


class Kept(NamedTuple):
    acts: Any
    slope: Any
    soft: Any
    ob: Any
    den: Any
    state: Any
    xh1: Any
    xh2: Any
    rstd: Any
    n1b: Any
    gz: Any
    gu: Any


class Gather:
    def __init__(self, kind, piece, full, links, moves):
        self.kind, self.piece, self.full = kind, piece, full
        self.links, self.moves = links, moves
        self.z, self.x, self.y, self.c = place()
        self.copies = {}

    def spot(self, zz, xx, yy):
        rows, cols = self.piece.shape
        span = region(self.kind, rows, cols, zz, xx, yy, self.c)
        return self.full.at[span[0], span[1]]

    def origin(self, d):
        return (self.z + 4 - d) % 4 if d else self.z

    def begin(self, d):
        z, x, y, c = self.z, self.x, self.y, self.c
        if d:
            dev = at((z + d) % 4, x, y, c)
            self.copies[BY_Z, d] = self.links.send(self.piece, self.spot(z, x, y), dev)
        else:
            self.own = self.moves.start(self.piece, self.spot(z, x, y))

    def fan(self, d):
        z, x, y, c = self.z, self.x, self.y, self.c
        if d:
            self.copies[BY_Z, d].wait_recv()
        here = self.spot(self.origin(d), x, y)
        src = here if d else self.piece
        self.copies[BY_X, d] = self.links.send(src, here, at(z, 1 - x, y, c))
        self.copies[BY_Y, d] = self.links.send(src, here, at(z, x, 1 - y, c))
        self.copies[BY_CORE, d] = self.links.send(src, here, at(z, x, y, 1 - c))

    def second(self, d):
        z, x, y, c = self.z, self.x, self.y, self.c
        from_x, from_y = self.spot(self.origin(d), 1 - x, y), self.spot(self.origin(d), x, 1 - y)
        self.copies[BY_X, d].wait_recv()
        if d in FIRST_X:
            self.copies[BY_CORNER, d] = self.links.send(from_x, from_x, at(z, x, 1 - y, c))
        self.copies[ON_X, d] = self.links.send(from_x, from_x, at(z, x, y, 1 - c))
        self.copies[BY_Y, d].wait_recv()
        if d not in FIRST_X:
            self.copies[BY_CORNER, d] = self.links.send(from_y, from_y, at(z, 1 - x, y, c))
        self.copies[ON_Y, d] = self.links.send(from_y, from_y, at(z, x, y, 1 - c))

    def third(self, d):
        z, x, y, c = self.z, self.x, self.y, self.c
        block = self.spot(self.origin(d), 1 - x, 1 - y)
        self.copies[BY_CORNER, d].wait_recv()
        self.copies[ON_CORNER, d] = self.links.send(block, block, at(z, x, y, 1 - c))

    def ready(self):
        for key in (BY_CORE, ON_X, ON_Y, ON_CORNER):
            for d in range(4):
                self.copies[key, d].wait_recv()
        self.moves.wait(self.own)


class Exchange:
    def __init__(self, coef, refs, links, reverse):
        self.coef, self.reverse, self.links = coef, reverse, links
        self.mine, self.got, self.sums, self.got_z, self.back, self.result = refs
        self.z, self.x, self.y, self.c = place()
        self.index = self.x * 4 + self.y * 2 + self.c

    def scatter(self):
        self.got[self.index] = self.mine[self.index]
        self.first = []
        for d in range(1, 8):
            nx, ny, nc = flip(self.x, self.y, self.c, d)
            src = self.mine.at[nx * 4 + ny * 2 + nc]
            dev = at(self.z, nx, ny, nc)
            self.first.append(self.links.send(src, self.got.at[self.index], dev))

    def across(self):
        for copy in self.first:
            copy.wait_recv()
        self.planes = []
        for d in (1, 2, 3):
            total = jnp.zeros(self.got.shape[1:], jnp.float32)
            for j in range(8):
                total = total + self.coef[8 + d, j] * self.got[j].astype(jnp.float32)
            self.sums[d - 1] = total.astype(jnp.bfloat16)
            dev = at((self.z + d) % 4, self.x, self.y, self.c)
            self.planes.append(self.links.send(self.sums.at[d - 1], self.got_z.at[d - 1], dev))

    def gather(self):
        for copy in self.planes:
            copy.wait_recv()
        parts = [self.got[j].astype(jnp.float32) for j in range(8)]
        parts += [self.got_z[d].astype(jnp.float32) for d in range(3)]
        for i in range(8):
            total = jnp.zeros(self.got.shape[1:], jnp.float32)
            span = range(i + 1, 8) if self.reverse else range(i)
            for j in list(span) + [8, 9, 10]:
                total = total + self.coef[i, j] * parts[j]
            self.back[i] = total.astype(jnp.bfloat16)
        self.result[self.index] = self.back[self.index]
        self.last = []
        for d in range(1, 8):
            nx, ny, nc = flip(self.x, self.y, self.c, d)
            src = self.back.at[nx * 4 + ny * 2 + nc]
            dev = at(self.z, nx, ny, nc)
            self.last.append(self.links.send(src, self.result.at[self.index], dev))

    def finish(self):
        for copy in self.last:
            copy.wait_recv()


def exchange_scratch(width):
    counts = (8, 8, 3, 3, 8, 8)
    return [pltpu.VMEM((n, 16, width), jnp.bfloat16) for n in counts]


def mm(a, b):
    return lax.dot_general(a, b, (((1,), (0,)), ((), ())), preferred_element_type=jnp.float32)


def mm_nt(a, b):
    return lax.dot_general(a, b, (((1,), (1,)), ((), ())), preferred_element_type=jnp.float32)


def mm_tn(a, b):
    return lax.dot_general(a, b, (((0,), (0,)), ((), ())), preferred_element_type=jnp.float32)


def low_lanes(shape):
    return lax.broadcasted_iota(jnp.int32, shape, len(shape) - 1) < HD


def lane_is(shape, h):
    return lax.broadcasted_iota(jnp.int32, shape, len(shape) - 1) == h


def pair_cols(p):
    return slice(p * 128, (p + 1) * 128)


def pack_state(ref, p, kind, block, extra):
    low = low_lanes((64, 128))
    packed = jnp.where(low, block[:64, :128], block[64:, :128]).astype(jnp.bfloat16)
    for s in range(4):
        ref[kind * 4 + s, :, pair_cols(p)] = packed[s * 16 : (s + 1) * 16]
    if extra is None:
        extra = jnp.zeros((64, 128), jnp.float32)
    extra = extra + jnp.where(lane_is((64, 128), 2 * p), block[:64, 128:], 0.0)
    return extra + jnp.where(lane_is((64, 128), 2 * p + 1), block[64:, 128:], 0.0)


def store_extra(ref, kind, extra, width):
    extra = extra.astype(jnp.bfloat16)
    for s in range(4):
        ref[kind * 4 + s, :, width - 128 :] = extra[s * 16 : (s + 1) * 16]


def unpack_state(ref, p, kind, width):
    packed = jnp.concatenate([ref[kind * 4 + s, :, pair_cols(p)] for s in range(4)], axis=0)
    sums = jnp.concatenate([ref[kind * 4 + s, :, width - 128 :] for s in range(4)], axis=0)
    low = low_lanes((64, 128))
    zero = jnp.zeros((64, 128), jnp.bfloat16)
    top = jnp.concatenate(
        [jnp.where(low, packed, zero), jnp.where(lane_is((64, 128), 2 * p), sums, zero)], axis=1
    )
    bottom = jnp.concatenate(
        [jnp.where(low, zero, packed), jnp.where(lane_is((64, 128), 2 * p + 1), sums, zero)],
        axis=1,
    )
    return jnp.concatenate([top, bottom], axis=0)


def spread(values, p):
    rows = values.shape[0]
    first = jnp.broadcast_to(values[:, 2 * p : 2 * p + 1], (rows, 128))
    second = jnp.broadcast_to(values[:, 2 * p + 1 : 2 * p + 2], (rows, 128))
    return jnp.where(low_lanes((rows, 128)), first, second)


def assemble_gains(full, layers):
    spots = lax.broadcasted_iota(jnp.int32, (128, 768), 0)
    lanes = lax.broadcasted_iota(jnp.int32, (128, 768), 1)
    total = jnp.zeros((64, 768), jnp.float32)
    for dp in range(8):
        both = full[dp * 32 : (dp + 1) * 32, :]
        left = jnp.concatenate([both[:, :128], both[:, 128:]], axis=0)
        put = jnp.where((lanes == spots + dp * 96) & (spots < 96), 1.0, 0.0).astype(jnp.bfloat16)
        total = total + mm(left, put)
    return [
        jnp.concatenate([total[head * 16 + i : head * 16 + i + 1] for head in range(4)], axis=0)
        for i in range(layers)
    ]


AHEAD, SECOND, THIRD = 6, 4, 8
PUMP = 4


def forward_kernel(layers, pairs, coef, x_ref, w_ref, aux_ref, *refs):
    order = (NORM,) + MATRICES
    pieces = refs[:5]
    h_out, gains_out = refs[5:7]
    refs = refs[7:]
    full_out = [(None,) + refs[4 * i : 4 * i + 4] for i in range(layers)]
    refs = refs[4 * layers :]
    saved = [Kept(*refs[12 * i : 12 * i + 12]) for i in range(layers)]
    rest = refs[12 * layers :]
    full = [(rest[0],) + rest[1 + 4 * i : 5 + 4 * i] for i in range(layers)]
    rest = rest[1 + 4 * layers :]
    hold = Kept(*rest[:5], None, *rest[5:11])
    num, n1, h_mid = rest[11:14]
    ex_refs = [rest[14 + 6 * i : 20 + 6 * i] for i in range(layers)]
    send_sem, recv_sem, move_sem = rest[-3:]
    rows, model = x_ref.shape
    half = rows // 2
    width = model + 128
    links, moves = Links(send_sem, recv_sem), Moves(move_sem)
    greet()
    norms = Gather(NORM, pieces[NORM], full[0][NORM], links, moves)
    every = [
        [norms]
        + [Gather(k, pieces[k].at[i], full[i][k], links, moves) for k in MATRICES]
        for i in range(layers)
    ]

    steps = []

    done = [0]

    def pump(n):
        while n > 0 and done[0] < len(steps):
            steps[done[0]]()
            done[0] += 1
            n -= 1

    def until(mark):
        pump(mark - done[0])

    chain = [part for parts in every for part in parts[1:]]
    chain.insert(2, norms)
    line = [(part, d) for part in chain for d in (0, 1, 3, 2)]
    marks = {}
    for i in range(-AHEAD, len(line) + THIRD):
        for stage, lag in ((0, -AHEAD), (1, 0), (2, SECOND), (3, THIRD)):
            if 0 <= i - lag < len(line):
                part, d = line[i - lag]
                steps.append(functools.partial((part.begin, part.fan, part.second, part.third)[stage], d))
                marks[id(part)] = len(steps)

    cos, sin = aux_ref[:, 0:1], aux_ref[:, 1:2]
    follow, tail, valid = aux_ref[:, 2:3], aux_ref[:, 3:4], aux_ref[:, 4:5]
    soft = hold.soft

    def q_of(p):
        return soft[:, p * 128 : (p + 1) * 128]

    def k_of(p):
        return soft[:, model + p * 128 : model + (p + 1) * 128]

    def v_of(p):
        return soft[:, 2 * model + p * 128 : 2 * model + (p + 1) * 128]

    def one_layer(layer):
        parts, whole, keep = every[layer], full[layer], saved[layer]
        mark = [marks[id(part)] for part in parts]
        h_ref = h_mid if layer else x_ref
        h_next = h_out if layer == layers - 1 else h_mid
        ex = Exchange(coef, ex_refs[layer], links, False)
        hold.acts[...] = h_ref[...].astype(jnp.bfloat16)
        moves.start(hold.acts, keep.acts)
        until(mark[QKV])
        parts[QKV].ready()
        moves.start(whole[QKV], full_out[layer][QKV])
        acts = hold.acts[...]
        for j in range(3 * model // 256):
            span = slice(j * 256, (j + 1) * 256)
            p = mm(acts, whole[QKV][:, span])
            if j * 256 < 2 * model:
                t = jnp.exp(-jnp.abs(p))
                hold.slope[:, span] = (jnp.where(p >= 0, 1.0, t) / (1.0 + t)).astype(jnp.bfloat16)
                p = jnp.maximum(p, 0.0) + jnp.log1p(t)
                if j * 256 >= model:
                    p = p * valid
            soft[:, span] = p.astype(jnp.bfloat16)
            if j % 3 == 2:
                pump(1)
        moves.start(hold.slope, keep.slope)
        moves.start(soft, keep.soft)

        ones = jnp.ones((rows, 128), jnp.bfloat16)
        extras = [None, None]
        for p in range(pairs):
            kp = k_of(p).astype(jnp.float32) * tail
            rhs = jnp.concatenate([v_of(p), ones], axis=1)
            for kind, angle in enumerate((cos, sin)):
                block = mm_tn((kp * angle).astype(jnp.bfloat16), rhs)
                extras[kind] = pack_state(ex.mine, p, kind, block, extras[kind])
        for kind in range(2):
            store_extra(ex.mine, kind, extras[kind], width)
        ex.scatter()
        den_ref = hold.den

        def inner(p):
            kp, vp = k_of(p), v_of(p)
            low = low_lanes((rows, 128))
            zero = jnp.zeros((rows, 128), jnp.bfloat16)
            out = []
            for e in range(2):
                qh = jnp.where(low if e == 0 else ~low, q_of(p), zero)
                mark_head = lane_is((rows, 128), 2 * p + e).astype(jnp.bfloat16)
                rhs = jnp.concatenate([vp, mark_head], axis=1)
                top = mm_nt(qh[:half], kp[:half]) * w_ref[:half, :half]
                bottom = mm_nt(qh[half:], kp) * w_ref[half:, :]
                top, bottom = top.astype(jnp.bfloat16), bottom.astype(jnp.bfloat16)
                out.append(jnp.concatenate([mm(top, rhs[:half]), mm(bottom, rhs)], axis=0))
            num[:, pair_cols(p)] = jnp.where(low, out[0][:, :128], out[1][:, :128])
            dens = out[0][:, 128:] + out[1][:, 128:]
            if p == 0:
                den_ref[...] = dens
            else:
                den_ref[...] += dens

        for p in range(pairs):
            inner(p)
            if p == 1:
                ex.across()
            if p == 3:
                ex.gather()
            pump(PUMP)
        ex.finish()
        moves.start(ex.result, keep.state)
        den = den_ref[...]
        cf, sf = cos * follow, sin * follow
        for p in range(pairs):
            qp = q_of(p)
            extra = cf * mm(qp, unpack_state(ex.result, p, 0, width))
            extra += sf * mm(qp, unpack_state(ex.result, p, 1, width))
            num[:, pair_cols(p)] += extra[:, :128]
            den = den + extra[:, 128:]
        den_ref[...] = den
        moves.start(hold.den, keep.den)
        inv = 1.0 / jnp.maximum(den, 1.0)
        ob = hold.ob
        for p in range(pairs):
            ob[:, pair_cols(p)] = (num[:, pair_cols(p)] * spread(inv, p)).astype(jnp.bfloat16)
        moves.start(hold.ob, keep.ob)
        until(mark[OUT])
        parts[OUT].ready()
        moves.start(whole[OUT], full_out[layer][OUT])

        def norm(x_ref, which, low_ref, whole_ref):
            gain, shift = gains[2 * which], gains[2 * which + 1]
            for i in range(0, rows, 128):
                x = x_ref[i : i + 128, :]
                centered = x - jnp.mean(x, axis=1, keepdims=True)
                variance = jnp.mean(centered * centered, axis=1, keepdims=True)
                r = lax.rsqrt(variance + norm_eps)
                xh = centered * r
                x_ref[i : i + 128, :] = xh
                new = jnp.broadcast_to(r, (128, 128))
                if which:
                    new = jnp.where(low_lanes((128, 128)), hold.rstd[i : i + 128, :], new)
                hold.rstd[i : i + 128, :] = new
                y = xh * gain + shift
                whole_ref[i : i + 128, :] = y
                if low_ref is not None:
                    low_ref[i : i + 128, :] = y.astype(jnp.bfloat16)

        if layer == 0:
            until(mark[NORM])
            norms.ready()
            for i, lines in enumerate(assemble_gains(whole[NORM], layers)):
                gains_out[i, 0:4, :] = lines
                gains_out[i, 4:8, :] = jnp.zeros((4, model), jnp.float32)
        gains = [gains_out[layer, i : i + 1, :] for i in range(4)]
        attended = ob[...]
        for j in range(model // 256):
            span = slice(j * 256, (j + 1) * 256)
            first_in = h_ref[:, span].astype(jnp.float32)
            hold.xh1[:, span] = first_in + mm(attended, whole[OUT][:, span])
        norm(hold.xh1, 0, hold.n1b, n1)
        moves.start(hold.xh1, keep.xh1)
        moves.start(hold.n1b, keep.n1b)
        until(mark[UP])
        parts[UP].ready()
        moves.start(whole[UP], full_out[layer][UP])
        n1b = hold.n1b[...]
        hidden = whole[UP].shape[1]
        for j in range(hidden // 256):
            span = slice(j * 256, (j + 1) * 256)
            u = mm(n1b, whole[UP][:, span])
            phi = 0.5 * (1.0 + lax.erf(u * math.sqrt(0.5)))
            hold.gz[:, span] = (u * phi).astype(jnp.bfloat16)
            bell = jnp.exp(-0.5 * u * u) * (1.0 / math.sqrt(2.0 * math.pi))
            hold.gu[:, span] = (phi + u * bell).astype(jnp.bfloat16)
            pump(1)
        moves.start(hold.gz, keep.gz)
        moves.start(hold.gu, keep.gu)
        until(mark[DOWN])
        parts[DOWN].ready()
        moves.start(whole[DOWN], full_out[layer][DOWN])
        gz = hold.gz[...]
        for j in range(model // 256):
            span = slice(j * 256, (j + 1) * 256)
            hold.xh2[:, span] = n1[:, span] + mm_nt(gz, whole[DOWN][span, :])
        norm(hold.xh2, 1, None, h_next)
        moves.start(hold.xh2, keep.xh2)
        moves.start(hold.rstd, keep.rstd)
        moves.finish()

    for layer in range(layers):
        one_layer(layer)
    links.finish()


def forward(number, coef, inputs, weights, aux, pieces):
    rows, model = inputs.shape
    layers = pieces[1].shape[0]
    order = (NORM,) + MATRICES
    fulls = [whole_shape(k, *p.shape[-2:]) for k, p in zip(order, pieces)]
    hidden = fulls[UP][1]
    width = model + 128
    low, wide = jnp.bfloat16, jnp.float32
    kept = Kept(
        acts=((rows, model), low),
        slope=((rows, 2 * model), low),
        soft=((rows, 3 * model), low),
        ob=((rows, model), low),
        den=((rows, 128), wide),
        state=((8, 16, width), low),
        xh1=((rows, model), wide),
        xh2=((rows, model), wide),
        rstd=((rows, 128), wide),
        n1b=((rows, model), low),
        gz=((rows, hidden), low),
        gu=((rows, hidden), low),
    )
    vmem = pl.BlockSpec(memory_space=pltpu.VMEM)
    anywhere = pl.BlockSpec(memory_space=pl.ANY)
    scratch = [pltpu.VMEM(s, low) for s in fulls[:1] + fulls[1:] * layers]
    scratch += [pltpu.VMEM(*a) for a in kept[:5] + kept[6:]]
    scratch += [pltpu.VMEM((rows, model), wide)] * 3
    scratch += exchange_scratch(width) * layers
    scratch += [pltpu.SemaphoreType.DMA((layers * 141 + 31,))] * 2
    scratch += [pltpu.SemaphoreType.DMA((layers * 22,))]
    outs = pl.pallas_call(
        functools.partial(forward_kernel, layers, model // 128),
        out_shape=[
            jax.ShapeDtypeStruct((rows, model), wide),
            jax.ShapeDtypeStruct((layers, 8, model), wide),
        ]
        + [jax.ShapeDtypeStruct(s, low) for s in fulls[1:]] * layers
        + [jax.ShapeDtypeStruct(s, t) for s, t in kept] * layers,
        in_specs=[pl.BlockSpec(memory_space=pltpu.SMEM)] + [vmem] * 3 + [anywhere] * 5,
        out_specs=[vmem] * 2 + [anywhere] * (layers * (4 + len(kept))),
        scratch_shapes=scratch,
        compiler_params=pltpu.CompilerParams(
            collective_id=number, has_side_effects=True, vmem_limit_bytes=61 * 2**20
        ),
        name="forward_layers",
    )(coef, inputs, weights, aux, *pieces)
    outs, h_out, gains = outs[2:], outs[0], outs[1]
    held = []
    for i in range(layers):
        held.append((gains[i], outs[4 * i : 4 * i + 4], Kept(*outs[4 * layers + 12 * i :][:12])))
    return h_out, held


class Reduce:
    def __init__(self, own, core_in, one_y, one_x, two, from_z, links):
        self.own, self.core_in, self.links = own, core_in, links
        self.one_y, self.one_x, self.two, self.from_z = one_y, one_x, two, from_z
        self.z, self.x, self.y, self.c = place()
        self.rows, self.cols = two.shape[1], two.shape[2]
        self.copies = {}

    def plane(self, d):
        return (self.z + d) % 4 if d else self.z

    def side(self, yy):
        return pl.ds(pl.multiple_of(yy * self.cols, self.cols), self.cols)

    def strip(self, number, count=1):
        return pl.ds(pl.multiple_of(number * self.rows, self.rows), count * self.rows)

    def both(self, d):
        return self.strip(self.plane(d) * 2, 2)

    def give(self, ref, d):
        span = self.both(d)
        dev = at(self.z, self.x, self.y, 1 - self.c)
        copy = self.links.send(ref.at[span, pl.ds(0, 2 * self.cols)], self.core_in.at[span], dev)
        self.copies[CORE, d] = copy

    def given(self):
        for d in range(4):
            self.links.sent(self.copies[CORE, d])

    def release(self, free_sem):
        z, x, y, c = self.z, self.x, self.y, self.c
        for key, copy in self.copies.items():
            if copy.number in self.links.left:
                self.links.sent(copy)
        near = [at(z, 1 - x, y, c), at(z, x, 1 - y, c), at(z, x, y, 1 - c)]
        for dev in near + [at((z + d) % 4, x, y, c) for d in (1, 2, 3)]:
            pl.semaphore_signal(free_sem, inc=1, device_id=dev, device_id_type=MESH)

    def add(self, span, other):
        here = self.own[span].astype(jnp.float32)
        self.own[span] = (here + other.astype(jnp.float32)).astype(jnp.bfloat16)

    def one(self, d):
        z, x, y, c = self.z, self.x, self.y, self.c
        self.copies[CORE, d].wait_recv()
        self.add((self.both(d), slice(None)), self.core_in[self.both(d), :])
        if d in FIRST_X:
            src = self.own.at[self.both(d), self.side(1 - y)]
            dst, dev = self.one_y.at[FIRST_X.index(d)], at(z, x, 1 - y, c)
        else:
            src = self.own.at[self.strip(self.plane(d) * 2 + 1 - x)]
            dst, dev = self.one_x.at[d - 1], at(z, 1 - x, y, c)
        self.copies[ONE, d] = self.links.send(src, dst, dev)

    def second(self, d):
        z, x, y, c = self.z, self.x, self.y, self.c
        self.copies[ONE, d].wait_recv()
        self.links.sent(self.copies[ONE, d])
        near, far = self.strip(self.plane(d) * 2 + x), self.strip(self.plane(d) * 2 + 1 - x)
        if d in FIRST_X:
            self.add((self.both(d), self.side(y)), self.one_y[FIRST_X.index(d)])
            src, dev = self.own.at[far, self.side(y)], at(z, 1 - x, y, c)
        else:
            self.add((near, slice(None)), self.one_x[d - 1])
            src, dev = self.own.at[near, self.side(1 - y)], at(z, x, 1 - y, c)
        self.copies[TWO, d] = self.links.send(src, self.two.at[d], dev)

    def third(self, d):
        z, x, y, c = self.z, self.x, self.y, self.c
        self.copies[TWO, d].wait_recv()
        near = (self.strip(self.plane(d) * 2 + x), self.side(y))
        self.add(near, self.two[d])
        if d:
            src, dst = self.own.at[near[0], near[1]], self.from_z.at[d - 1]
            self.copies[LAST, d] = self.links.send(src, dst, at(self.plane(d), x, y, c))

    def last(self, out_ref, squares):
        value = self.own[self.strip(self.z * 2 + self.x), self.side(self.y)].astype(jnp.float32)
        for d in (1, 2, 3):
            self.copies[LAST, d].wait_recv()
            value = value + self.from_z[d - 1].astype(jnp.float32)
        out_ref[...] = value
        part = jnp.sum((value * value).reshape(self.rows // 8, 8, self.cols), axis=0)
        for j in range(self.cols // 128):
            squares[...] += part[:, j * 128 : (j + 1) * 128]


def backward_kernel(layers, pairs, coef, w_ref, aux_ref, dh_in, gains_ref, *refs):
    kept = [Kept(*refs[12 * i : 12 * i + 12]) for i in range(layers)]
    refs = refs[12 * layers :]
    weights = [(None,) + refs[4 * i : 4 * i + 4] for i in range(layers)]
    refs = refs[4 * layers :]
    dh = refs[0]
    sums = [(None,) + refs[1 + 4 * i : 5 + 4 * i] for i in range(layers)]
    norm_out, squares = refs[1 + 4 * layers : 3 + 4 * layers]
    rest = refs[3 + 4 * layers :]
    free_sem, send_sem, recv_sem, move_sem = rest[-4:]
    links, moves = Links(send_sem, recv_sem), Moves(move_sem)
    reds = [[None] + [Reduce(*rest[i:24:4], links) for i in range(4)] for _ in range(layers)]
    give_a, give_b, buf_a, buf_b, w_out = rest[24:29]
    hold = Kept(*rest[29:31], None, *rest[31:40])
    drb, turned, dd_ref = rest[40:43]
    ex_refs = [rest[43 + 6 * i : 49 + 6 * i] for i in range(layers)]
    rows, model = dh.shape
    half = rows // 2
    width = model + 128
    hidden = hold.gz.shape[1]
    z, x, y, c = place()
    even = c == 0

    loads = {}

    def load(number, src, dst):
        loads[number] = moves.start(src, dst)

    def need(*numbers):
        for number in numbers:
            moves.wait(loads[number])

    def load_early(layer):
        have = kept[layer]
        load(0, have.xh2, hold.xh2)
        load(1, have.rstd, hold.rstd)
        load(2, weights[layer][DOWN], buf_a)
        load(3, have.n1b, hold.n1b)
        load(4, have.xh1, hold.xh1)
        load(5, have.ob, hold.ob)
        load(6, have.den, hold.den)
        load(7, have.state, hold.state)
        load(8, have.slope, hold.slope)
        load(9, weights[layer][OUT], w_out)

    def load_late(layer):
        load(11, kept[layer].gu, hold.gu)
        load(12, weights[layer][UP], buf_b)

    steps, done, pushed, closed = [], [0], [], {}

    def pump(n):
        while n > 0 and done[0] < len(steps):
            steps[done[0]]()
            done[0] += 1
            n -= 1

    def until(mark):
        pump(mark - done[0])

    def later_stages(i):
        for stage in (1, 2, 3):
            if 0 <= i - stage < len(pushed):
                layer, kind = pushed[i - stage]
                red = reds[layer][kind]
                if stage < 3:
                    for d in (2, 3, 1, 0):
                        steps.append(functools.partial((red.second, red.third)[stage - 1], d))
                else:
                    steps.append(functools.partial(red.last, sums[layer][kind], squares))
                    if layer:
                        steps.append(functools.partial(red.release, free_sem.at[kind]))
                    closed[layer, kind] = len(steps)

    def take(layer, kind):
        if layer < layers - 1:
            until(closed[layer + 1, kind])

    def credit(layer, kind):
        if layer < layers - 1:
            pl.semaphore_wait(free_sem.at[kind], 6)

    def push(layer, kind, ref):
        red = reds[layer][kind]
        pump(len(steps))
        credit(layer, kind)
        for d in (2, 3, 1, 0):
            red.give(ref, d)
        pushed.append((layer, kind))
        for d in (2, 3, 1, 0):
            steps.append(functools.partial(red.one, d))
        later_stages(len(pushed) - 1)

    load(10, kept[layers - 1].gz, hold.gz)
    first_dh = moves.start(dh_in, dh)
    load_early(layers - 1)
    load_late(layers - 1)
    greet()
    squares[...] = jnp.zeros(squares.shape, jnp.float32)
    moves.wait(first_dh)

    cos, sin = aux_ref[:, 0:1], aux_ref[:, 1:2]
    follow, tail, valid = aux_ref[:, 2:3], aux_ref[:, 3:4], aux_ref[:, 4:5]
    low = low_lanes((rows, 128))
    zero = jnp.zeros((rows, 128), jnp.bfloat16)
    ones = jnp.ones((rows, 128), jnp.bfloat16)
    cf, sf = cos * follow, sin * follow
    ct, st = cos * tail, sin * tail

    def turn(ref):
        for i in range(0, model, 256):
            turned[i : i + 256, :] = ref[:, i : i + 256].astype(jnp.float32).T.astype(jnp.bfloat16)

    def choose(first, second):
        return jnp.where(even, first, second), jnp.where(even, second, first)

    def split_rows(block, mine_ref, theirs_ref, span):
        for strip in range(8):
            mine, theirs = choose(
                block[strip * 96 : strip * 96 + 48], block[strip * 96 + 48 : strip * 96 + 96]
            )
            mine_ref[strip * 48 : (strip + 1) * 48, span] = mine
            theirs_ref[strip * 48 : (strip + 1) * 48, span] = theirs

    def q_of(p):
        return buf_a[:rows, p * 128 : (p + 1) * 128]

    def k_of(p):
        return buf_a[:rows, model + p * 128 : model + (p + 1) * 128]

    def v_of(p):
        return buf_a[:rows, 2 * model + p * 128 : 2 * model + (p + 1) * 128]

    def one_layer(layer):
        red = reds[layer]
        down, up, out, qkv = red[DOWN], red[UP], red[OUT], red[QKV]
        ex = Exchange(coef, ex_refs[layer], links, True)

        def norm_back(xh_ref, which):
            gain = gains_ref[layer, 2 * which : 2 * which + 1, :]
            dg = jnp.zeros((8, model), jnp.float32)
            db = jnp.zeros((8, model), jnp.float32)
            for i in range(0, rows, 128):
                dy, xh = dh[i : i + 128, :], xh_ref[i : i + 128, :]
                r = hold.rstd[i : i + 128, which * 64 : which * 64 + 1]
                e = dy * gain
                both = dy * xh
                dx = e - jnp.mean(e, axis=1, keepdims=True)
                dx = r * (dx - xh * jnp.mean(e * xh, axis=1, keepdims=True))
                dg = dg + jnp.sum(both.reshape(16, 8, model), axis=0)
                db = db + jnp.sum(dy.reshape(16, 8, model), axis=0)
                dh[i : i + 128, :] = dx
                drb[i : i + 128, :] = dx.astype(jnp.bfloat16)
                pump(1)
            norm_out[layer, 2 * which : 2 * which + 1, :] = jnp.sum(dg, axis=0, keepdims=True)
            norm_out[layer, 2 * which + 1 : 2 * which + 2, :] = jnp.sum(db, axis=0, keepdims=True)

        norm_out[layer, 4:8, :] = jnp.zeros((4, model), jnp.float32)
        need(0, 1)
        norm_back(hold.xh2, 1)
        turn(drb)
        need(10)
        take(layer, DOWN)
        left = turned[...]
        for strip in range(8):
            block = mm(left, hold.gz[:, strip * 384 : (strip + 1) * 384]).astype(jnp.bfloat16)
            for yy in range(2):
                first = block[yy * 384 : yy * 384 + 192]
                second = block[yy * 384 + 192 : yy * 384 + 384]
                mine, theirs = choose(first, second)
                span = slice(strip * 192, (strip + 1) * 192)
                down.own[span, yy * 384 : (yy + 1) * 384] = mine
                give_a[span, yy * 384 : (yy + 1) * 384] = theirs
            pump(1)
        push(layer, DOWN, give_a)
        need(2, 11)
        low_grad = drb[...]
        for j in range(hidden // 256):
            span = slice(j * 256, (j + 1) * 256)
            t = mm(low_grad, buf_a[:, span]) * hold.gu[:, span].astype(jnp.float32)
            hold.gz[:, span] = t.astype(jnp.bfloat16)
            pump(1)
        du = hold.gz
        load(13, kept[layer].soft, buf_a.at[pl.ds(0, rows), pl.ds(0, 3 * model)])
        need(3)
        turn(hold.n1b)
        take(layer, UP)
        left = turned[...]
        for yy in range(2):
            for target, cc in ((give_b, 1 - c), (up.own, c)):
                for j in range(3):
                    cols = pl.ds(pl.multiple_of((yy * 2 + cc) * 768 + j * 256, 256), 256)
                    block = mm(left, du[:, cols]).astype(jnp.bfloat16)
                    target[:, yy * 768 + j * 256 : yy * 768 + (j + 1) * 256] = block
        push(layer, UP, give_b)
        need(12)
        for j in range(model // 256):
            span = slice(j * 256, (j + 1) * 256)
            dh[:, span] += mm_nt(du[...], buf_b[span, :])
            pump(2)
        load(14, weights[layer][QKV], buf_b.at[:, pl.ds(0, 3 * model)])
        load(15, kept[layer].acts, hold.acts)
        need(4)
        norm_back(hold.xh1, 0)
        need(5)
        turn(hold.ob)
        take(layer, OUT)
        down.given()
        left = turned[...]
        for j in range(model // 256):
            span = slice(j * 256, (j + 1) * 256)
            block = mm(left, drb[:, span]).astype(jnp.bfloat16)
            split_rows(block, out.own, give_a, span)
        push(layer, OUT, give_a)
        need(9)
        dob_ref = du.at[:, pl.ds(0, model)]
        dn_ref = du.at[:, pl.ds(model, model)]
        dob_ref[...] = mm_nt(drb[...], w_out[...]).astype(jnp.bfloat16)
        pump(2)

        need(13, 6, 7, 8)
        grad, state_ref = hold.gu, hold.state
        keep_k, keep_v = hold.xh2, hold.xh1
        den = hold.den[...]
        inv = 1.0 / jnp.maximum(den, 1.0)
        dots = jnp.zeros((rows, 128), jnp.float32)
        for p in range(pairs):
            dob = dob_ref[:, pair_cols(p)].astype(jnp.float32)
            dn_ref[:, pair_cols(p)] = (dob * spread(inv, p)).astype(jnp.bfloat16)
            both = dob * hold.ob[:, pair_cols(p)].astype(jnp.float32)
            first = jnp.sum(jnp.where(low, both, 0.0), axis=1, keepdims=True)
            second = jnp.sum(jnp.where(low, 0.0, both), axis=1, keepdims=True)
            dots = dots + jnp.where(lane_is((rows, 128), 2 * p), first, 0.0)
            dots = dots + jnp.where(lane_is((rows, 128), 2 * p + 1), second, 0.0)
        dden = jnp.where(den > 1.0, -dots * inv, 0.0)
        dd_ref[...] = dden
        dden_low = dden.astype(jnp.bfloat16)
        extras = [None, None]
        for p in range(pairs):
            qp = q_of(p).astype(jnp.float32)
            rhs = jnp.concatenate([dn_ref[:, pair_cols(p)], dden_low], axis=1)
            for kind, angle in enumerate((cf, sf)):
                block = mm_tn((qp * angle).astype(jnp.bfloat16), rhs)
                extras[kind] = pack_state(ex.mine, p, kind, block, extras[kind])
        for kind in range(2):
            store_extra(ex.mine, kind, extras[kind], width)
        ex.scatter()

        def inner(p):
            qp, kp, vp = q_of(p), k_of(p), v_of(p)
            dob, dnp = dob_ref[:, pair_cols(p)], dn_ref[:, pair_cols(p)]
            q_t = qp.astype(jnp.float32).T.astype(jnp.bfloat16)
            dn_t = dnp.astype(jnp.float32).T.astype(jnp.bfloat16)
            dq_parts, dk_parts, dv_parts = [], [], []
            for e in range(2):
                h = 2 * p + e
                mask = low if e == 0 else ~low
                span = slice(e * HD, (e + 1) * HD)
                qh = jnp.where(mask, qp, zero)
                doh = jnp.where(mask, dob, zero)
                scale, shift = inv[:, h : h + 1], dd_ref[:, h : h + 1]

                def tile(at_rows, at_cols):
                    weight = w_ref[at_rows, at_cols]
                    s = (mm_nt(qh[at_rows], kp[at_cols]) * weight).astype(jnp.bfloat16)
                    t = mm_nt(doh[at_rows], vp[at_cols])
                    ds = (t * scale[at_rows] + shift[at_rows]).astype(jnp.bfloat16)
                    g = (ds.astype(jnp.float32) * weight).astype(jnp.bfloat16)
                    return s, g

                above, below, every = slice(0, half), slice(half, rows), slice(0, rows)
                s_top, g_top = tile(above, above)
                s_low, g_low = tile(below, every)
                dq_parts.append(jnp.concatenate([mm(g_top, kp[:half]), mm(g_low, kp)], axis=0))

                def across(flat, top, bottom):
                    whole = mm(flat[span, half:], bottom)
                    first = whole[:, :half] + mm(flat[span, :half], top)
                    return jnp.concatenate([first, whole[:, half:]], axis=1)

                dk_parts.append(across(q_t, g_top, g_low))
                dv_parts.append(across(dn_t, s_top, s_low))
            base = slice(p * 128, (p + 1) * 128)
            dq = jnp.where(low, dq_parts[0], dq_parts[1])
            right = jnp.concatenate([dnp, dd_ref[...].astype(jnp.bfloat16)], axis=1)
            dq += cf * mm_nt(right, unpack_state(state_ref, p, 0, width))
            dq += sf * mm_nt(right, unpack_state(state_ref, p, 1, width))
            slope = hold.slope[:, base].astype(jnp.float32)
            grad[:, base] = (dq * slope).astype(jnp.bfloat16)
            keep_k[:, base] = jnp.concatenate(dk_parts, axis=0).T
            keep_v[:, base] = jnp.concatenate(dv_parts, axis=0).T

        for p in range(pairs):
            inner(p)
            if p == 1:
                ex.across()
            if p == 3:
                ex.gather()
            pump(3)
        ex.finish()
        for p in range(pairs):
            base = p * 128
            dsc, dss = unpack_state(ex.result, p, 0, width), unpack_state(ex.result, p, 1, width)
            right = jnp.concatenate([v_of(p), ones], axis=1)
            dk = keep_k[:, base : base + 128] + ct * mm_nt(right, dsc) + st * mm_nt(right, dss)
            kp = k_of(p)
            dv = ct * mm(kp, dsc[:, :128]) + st * mm(kp, dss[:, :128])
            dv = keep_v[:, base : base + 128] + dv
            slope = hold.slope[:, model + base : model + base + 128].astype(jnp.float32)
            grad[:, model + base : model + base + 128] = (dk * valid * slope).astype(jnp.bfloat16)
            grad[:, 2 * model + base : 2 * model + base + 128] = dv.astype(jnp.bfloat16)
        need(15)
        turn(hold.acts)
        if layer:
            load_early(layer - 1)
        take(layer, QKV)
        left = turned[...]
        for j in range(3 * model // 256):
            span = slice(j * 256, (j + 1) * 256)
            block = mm(left, grad[:, span]).astype(jnp.bfloat16)
            split_rows(block, qkv.own, hold.gz, span)
        push(layer, QKV, hold.gz)
        up.given()
        out.given()
        need(14)
        for j in range(model // 256):
            span = slice(j * 256, (j + 1) * 256)
            dh[:, span] += mm_nt(grad[:, : 3 * model], buf_b[span, : 3 * model])
            pump(2)
        qkv.given()
        if layer:
            load(10, kept[layer - 1].gz, hold.gz)
            load_late(layer - 1)

    for layer in reversed(range(layers)):
        one_layer(layer)
    for i in range(len(pushed), len(pushed) + 3):
        later_stages(i)
    pump(len(steps))
    moves.finish()
    links.finish()


def backward(number, coef, weights_map, aux, dh, held, dims):
    rows, model = dh.shape
    layers = len(held)
    gains = jnp.stack([h[0] for h in held])
    kept = held[0][2]
    hidden = kept.gz.shape[1]
    width = model + 128
    low, wide = jnp.bfloat16, jnp.float32
    vmem = pl.BlockSpec(memory_space=pltpu.VMEM)
    anywhere = pl.BlockSpec(memory_space=pl.ANY)
    sizes = dims[1:]
    scratch = [pltpu.VMEM((8 * r, 2 * w), low) for r, w in sizes] * 2
    scratch += [pltpu.VMEM((2, 2 * r, w), low) for r, w in sizes]
    scratch += [pltpu.VMEM((2, r, 2 * w), low) for r, w in sizes]
    scratch += [pltpu.VMEM((4, r, w), low) for r, w in sizes]
    scratch += [pltpu.VMEM((3, r, w), low) for r, w in sizes]
    for k in (DOWN, UP):
        scratch.append(pltpu.VMEM((8 * dims[k][0], 2 * dims[k][1]), low))
    scratch += [pltpu.VMEM((model, hidden), low)] * 2
    scratch.append(pltpu.VMEM((model, model), low))
    scratch += [pltpu.VMEM(a.shape, a.dtype) for a in kept[:2] + kept[3:]]
    scratch += [pltpu.VMEM((rows, model), low), pltpu.VMEM((model, rows), low)]
    scratch += [pltpu.VMEM((rows, 128), wide)]
    scratch += exchange_scratch(width) * layers
    scratch += [pltpu.SemaphoreType.REGULAR((5,))]
    scratch += [pltpu.SemaphoreType.DMA((layers * 80,))] * 2
    scratch += [pltpu.SemaphoreType.DMA((layers * 20,))]
    outs = pl.pallas_call(
        functools.partial(backward_kernel, layers, model // 128),
        out_shape=[jax.ShapeDtypeStruct((rows, model), wide)]
        + [jax.ShapeDtypeStruct(s, wide) for s in sizes] * layers
        + [
            jax.ShapeDtypeStruct((layers, 8, model), wide),
            jax.ShapeDtypeStruct((8, 128), wide),
        ],
        in_specs=[pl.BlockSpec(memory_space=pltpu.SMEM)]
        + [vmem, vmem, anywhere, vmem]
        + [anywhere] * (16 * layers),
        out_specs=[vmem] * (3 + 4 * layers),
        scratch_shapes=scratch,
        compiler_params=pltpu.CompilerParams(
            collective_id=number, has_side_effects=True, vmem_limit_bytes=63 * 2**20
        ),
        name="backward_layers",
    )(
        coef, weights_map, aux, dh, gains,
        *[a for h in held for a in h[2]],
        *[a for h in held for a in h[1]],
    )
    sums = [[None, *outs[1 + 4 * i : 5 + 4 * i]] for i in range(layers)]
    return outs[0], sums, outs[-2], outs[-1]


def stream_meta(lengths, row_ids):
    seq_count = lengths.shape[0]
    seq_ends = jnp.cumsum(lengths, dtype=jnp.int32)
    seq_starts = seq_ends - lengths
    begun = seq_starts[None, :] <= row_ids[:, None]
    seg_raw = jnp.sum(begun.astype(jnp.int32), axis=1, dtype=jnp.int32) - 1
    seg_start = jnp.max(jnp.where(begun, seq_starts[None, :], 0), axis=1)
    inside = row_ids < seq_ends[seq_count - 1]
    seg_ids = jnp.where(inside, seg_raw, seq_count)
    offsets = jnp.where(inside, row_ids - seg_start, 0).astype(jnp.float32)
    angles = offsets * (0.5 * math.pi / LONGEST)
    return (seg_ids, jnp.cos(angles), jnp.sin(angles), inside.astype(jnp.float32))


def adam_step(weight, first_old, second_old, gradient, factor, step_rate, decay_coef):
    clipped = gradient * factor
    first_new = beta_one * first_old + (1.0 - beta_one) * clipped
    second_new = beta_two * second_old + (1.0 - beta_two) * clipped * clipped
    first_hat = first_new / (1.0 - beta_one**step_fixed)
    second_hat = second_new / (1.0 - beta_two**step_fixed)
    weight_new = weight - step_rate * (
        first_hat / (jnp.sqrt(second_hat) + adam_eps) + decay_coef * weight
    )
    return (weight_new, first_new, second_new)


def other_core(array):
    return lax.ppermute(array, "head", [(0, 1), (1, 0), (2, 3), (3, 2)])


def weight_pieces(w_qkv, w_out, w_up, w_down, norm_params):
    first = lax.axis_index("head") % 2 == 0
    low = [a.astype(jnp.bfloat16) for a in (w_qkv, w_out)]
    halves = [(a[:, : a.shape[1] // 2], a[:, a.shape[1] // 2 :]) for a in low]
    keep = [jnp.where(first, a, b) for a, b in halves]
    give = [jnp.where(first, b, a) for a, b in halves]
    wide = other_core(jnp.concatenate(give, axis=2))
    got = jnp.split(wide, (keep[0].shape[2],), axis=2)
    pieces = [
        jnp.where(first, jnp.concatenate([a, b], axis=2), jnp.concatenate([b, a], axis=2))
        for a, b in zip(keep, got)
    ]
    pieces.append(w_up.astype(jnp.bfloat16))
    pieces.append(w_down.astype(jnp.bfloat16).transpose(0, 2, 1))
    layers, _, part = norm_params.shape
    norm = norm_params.astype(jnp.bfloat16).reshape(layers, part)
    return [jnp.pad(norm, ((0, 16 - layers), (0, 128 - part)))] + pieces


def exchange_plan(seg_last, seg_before, seg_plane, reverse):
    dp = lax.axis_index("dp")
    z = dp // 2
    last = lax.dynamic_slice(seg_last, (z * 8,), (8,))
    before = lax.dynamic_slice(seg_before, (z * 8,), (8,))
    order = jnp.arange(8)
    inside = (before[:, None] == last[None, :]) & (order[:, None] > order[None, :])
    ends = seg_last[7::8]
    planes = jnp.arange(4)
    to_end = last == ends[z]
    back = (before[:, None] == ends[None, :]) & (planes[None, :] < z)
    coef = jnp.zeros((16, 16), jnp.float32)
    shift = jnp.arange(1, 4)
    if reverse:
        coef = coef.at[:8, :8].set(inside.T.astype(jnp.float32))
        source = (z - shift) % 4
        coef = coef.at[:8, 8:11].set((to_end[:, None] & (source > z)[None, :]).astype(jnp.float32))
        target = (z + shift) % 4
        coef = coef.at[9:12, :8].set(back[:, target].T.astype(jnp.float32))
    else:
        coef = coef.at[:8, :8].set(inside.astype(jnp.float32))
        source = (z - shift) % 4
        coef = coef.at[:8, 8:11].set(back[:, source].astype(jnp.float32))
        coef = coef.at[9:12, :8].set(jnp.broadcast_to(to_end.astype(jnp.float32), (3, 8)))
    return coef


class LocalPlan:
    def __init__(self, lengths, rows):
        me = lax.axis_index("dp") * 4 + lax.axis_index("head")
        first_row = me * rows
        seg, cos, sin, valid = stream_meta(lengths, first_row + jnp.arange(rows, dtype=jnp.int32))
        starts = jnp.arange(32, dtype=jnp.int32) * rows
        before = stream_meta(lengths, starts - 1)[0]
        last = stream_meta(lengths, starts + rows - 1)[0]
        follow = (seg == before[me]).astype(jnp.float32)
        tail = (seg == last[me]).astype(jnp.float32)
        place_ids = jnp.arange(rows)
        allowed = (seg[:, None] == seg[None, :]) & (place_ids[None, :] <= place_ids[:, None])
        close = cos[:, None] * cos[None, :] + sin[:, None] * sin[None, :]
        self.valid = valid
        self.weights = jnp.where(allowed, close, 0.0)
        zero = jnp.zeros_like(cos)
        self.aux = jnp.stack([cos, sin, follow, tail, valid, zero, zero, zero], axis=1)
        self.ahead = exchange_plan(last, before, None, False)
        self.behind = exchange_plan(last, before, None, True)


def total_kernel(mine_ref, out_ref, sums, from_z, from_plane, send_sem, recv_sem):
    links = Links(send_sem, recv_sem)
    greet()
    devices = partners()
    copies = [links.send(mine_ref, from_z.at[i], devices[i]) for i in range(3)]
    total = mine_ref[...]
    for i in range(3):
        copies[i].wait_recv()
        total = total + from_z[i]
    sums[...] = total
    copies = [links.send(sums, from_plane.at[i], devices[3 + i]) for i in range(7)]
    for i in range(7):
        copies[i].wait_recv()
        total = total + from_plane[i]
    out_ref[...] = total
    links.finish()


def total_over_devices(number, mine):
    vmem = pl.BlockSpec(memory_space=pltpu.VMEM)
    return pl.pallas_call(
        total_kernel,
        out_shape=jax.ShapeDtypeStruct(mine.shape, mine.dtype),
        in_specs=[vmem],
        out_specs=vmem,
        scratch_shapes=[
            pltpu.VMEM(mine.shape, mine.dtype),
            pltpu.VMEM((3,) + mine.shape, mine.dtype),
            pltpu.VMEM((7,) + mine.shape, mine.dtype),
            pltpu.SemaphoreType.DMA((10,)),
            pltpu.SemaphoreType.DMA((10,)),
        ],
        compiler_params=pltpu.CompilerParams(
            collective_id=number, has_side_effects=True, vmem_limit_bytes=32 * 2**20
        ),
        name="total_over_devices",
    )(mine)


def own_columns(sums):
    first = lax.axis_index("head") % 2 == 0
    halves = [(a[..., : a.shape[2] // 2], a[..., a.shape[2] // 2 :]) for a in sums]
    keep = [jnp.where(first, a, b) for a, b in halves]
    give = [jnp.where(first, b, a) for a, b in halves]
    wide = other_core(jnp.concatenate(give, axis=2))
    got = jnp.split(wide, (keep[0].shape[2],), axis=2)
    return [
        jnp.where(first, jnp.concatenate([a, b], axis=1), jnp.concatenate([b, a], axis=1))
        for a, b in zip(keep, got)
    ]


def near_step(inputs, cotangent, lengths, w_qkv, w_out, w_up, w_down, norm_params):
    rows, model = inputs.shape
    layers, _, part = norm_params.shape
    plan = LocalPlan(lengths, rows)
    pieces = weight_pieces(w_qkv, w_out, w_up, w_down, norm_params)
    dims = [p.shape[-2:] for p in pieces]
    hidden, held = forward(0, plan.ahead, inputs, plan.weights, plan.aux, pieces)
    grad = cotangent.astype(jnp.float32)
    grad, sums, norms, squares = backward(
        1, plan.behind, plan.weights, plan.aux, grad, held, dims
    )
    norms = norms[:, :4].reshape(4 * layers, model)
    squares = jnp.pad(squares, ((0, 0), (0, model - 128)))
    totals = total_over_devices(2, jnp.concatenate([norms, squares], axis=0))
    norm_sum, squares = totals[: 4 * layers], totals[4 * layers :]
    squares = jnp.sum(squares) + jnp.sum(norm_sum * norm_sum)
    start = (0, lax.axis_index("head"), lax.axis_index("dp") * part)
    norm_sum = lax.dynamic_slice(norm_sum.reshape(layers, 4, model), start, (layers, 1, part))
    stacked = [None] + [jnp.stack([s[k] for s in sums]) for k in MATRICES]
    d_qkv, d_out = own_columns([stacked[QKV], stacked[OUT]])
    whole = [d_qkv, d_out, stacked[UP], stacked[DOWN].transpose(0, 2, 1)]
    return hidden, grad, whole, norm_sum, squares


def layer_norm(inputs_row, gain_row, shift_row):
    mean_row = jnp.mean(inputs_row, axis=-1, keepdims=True)
    centered = inputs_row - mean_row
    variance = jnp.mean(centered * centered, axis=-1, keepdims=True)
    return centered * lax.rsqrt(variance + norm_eps) * gain_row + shift_row


def gelu_exact(inner_pre):
    return jax.nn.gelu(inner_pre, approximate=False)


def contract_rows(left, right):
    return lax.dot_general(
        left, right, (((0,), (0,)), ((), ())), preferred_element_type=jnp.float32
    )


def contract_cols(left, right):
    return lax.dot_general(
        left, right, (((1,), (1,)), ((), ())), preferred_element_type=jnp.float32
    )


def block_attention(queries, key_rows, value_rows, weights, aux):
    cos, sin, tail = aux[:, 0], aux[:, 1], aux[:, 3]
    raw = jnp.einsum("ihe,jhe->hij", queries, key_rows, preferred_element_type=jnp.float32)
    scores = (raw * weights[None]).astype(jnp.bfloat16)
    num = jnp.einsum("hij,jhe->ihe", scores, value_rows, preferred_element_type=jnp.float32)
    den = jnp.transpose(jnp.sum(scores.astype(jnp.float32), axis=2))
    out = []
    for angle in (cos, sin):
        turned = key_rows.astype(jnp.float32) * (angle * tail)[:, None, None]
        out.append(
            jnp.einsum(
                "jhe,jhf->hef", turned, value_rows.astype(jnp.float32), precision=exact_mode
            )
        )
        out.append(jnp.sum(turned, axis=0))
    return num, den, tuple(out)


def finish_rows(queries, num, den, state, aux):
    cos, sin, follow = aux[:, 0], aux[:, 1], aux[:, 2]
    for angle, kv, ks in ((cos, state[0], state[1]), (sin, state[2], state[3])):
        turned = queries.astype(jnp.float32) * (angle * follow)[:, None, None]
        num = num + jnp.einsum("ihe,hef->ihf", turned, kv, precision=exact_mode)
        den = den + jnp.einsum("ihe,he->ih", turned, ks, precision=exact_mode)
    return num / jnp.maximum(den, 1.0)[:, :, None]


class WidePlan:
    def __init__(self, lengths, rows):
        parts = lax.axis_size("dp") * lax.axis_size("head")
        me = lax.axis_index("dp") * lax.axis_size("head") + lax.axis_index("head")
        seg, cos, sin, valid = stream_meta(
            lengths, me * rows + jnp.arange(rows, dtype=jnp.int32)
        )
        starts = jnp.arange(parts, dtype=jnp.int32) * rows
        before = stream_meta(lengths, starts - 1)[0]
        last = stream_meta(lengths, starts + rows - 1)[0]
        follow = (seg == before[me]).astype(jnp.float32)
        tail = (seg == last[me]).astype(jnp.float32)
        place_ids = jnp.arange(rows)
        allowed = (seg[:, None] == seg[None, :]) & (place_ids[None, :] <= place_ids[:, None])
        close = cos[:, None] * cos[None, :] + sin[:, None] * sin[None, :]
        self.valid = valid
        self.weights = jnp.where(allowed, close, 0.0)
        self.aux = jnp.stack([cos, sin, follow, tail, valid], axis=1)
        devices = jnp.arange(parts)
        self.ahead = ((last == before[me]) & (devices < me)).astype(jnp.float32)
        self.behind = ((before == last[me]) & (devices > me)).astype(jnp.float32)

    def masked(self, state, coef):
        def one(a):
            everything = lax.all_gather(a.astype(jnp.bfloat16), ("dp", "head"))
            return jnp.einsum(
                "d,d...->...",
                coef.astype(jnp.bfloat16),
                everything,
                preferred_element_type=jnp.float32,
            )

        return jax.tree.map(one, state)

    def attend(self, q, k, v):
        rows, model = q.shape
        split = lambda a: a.reshape(rows, HEADS, model // HEADS)
        local = lambda *a: block_attention(*a, self.weights, self.aux)
        (num, den, state), pull = jax.vjp(local, split(q), split(k), split(v))
        state = self.masked(state, self.ahead)
        finish = lambda *a: finish_rows(*a, self.aux)
        out, finish_pull = jax.vjp(finish, split(q), num, den, state)
        return out.astype(jnp.bfloat16).reshape(rows, model), (pull, finish_pull)

    def attend_back(self, kept, dob):
        pull, finish_pull = kept
        rows, model = dob.shape
        grad = dob.astype(jnp.float32).reshape(rows, HEADS, model // HEADS)
        dq_one, dnum, dden, dstate = finish_pull(grad)
        dstate = self.masked(dstate, self.behind)
        dq, dk, dv = pull((dnum, dden, dstate))
        dq = dq.astype(jnp.float32) + dq_one.astype(jnp.float32)
        dk = dk.astype(jnp.float32) * self.valid[:, None, None]
        out = [a.reshape(rows, model).astype(jnp.bfloat16) for a in (dq, dk, dv)]
        return jnp.concatenate(out, axis=1)


def wide_gather(w_qkv, w_out, w_up, w_down, norm_params):
    fulls = []
    for a in (w_qkv, w_out, w_up, w_down):
        part = lax.all_gather(a.astype(jnp.bfloat16), "dp", axis=1, tiled=True)
        fulls.append(lax.all_gather(part, "head", axis=2, tiled=True))
    norm = lax.all_gather(norm_params.astype(jnp.bfloat16), "dp", axis=2, tiled=True)
    return fulls, lax.all_gather(norm, "head", axis=1, tiled=True)


def wide_reduce(grads, norm_grad):
    def one(a):
        part = lax.psum_scatter(a, "head", scatter_dimension=1, tiled=True)
        part = lax.psum_scatter(part.astype(jnp.float32), "dp", scatter_dimension=0, tiled=True)
        return part

    whole = [jnp.stack([one(layer[i]) for layer in grads]) for i in range(len(grads[0]))]
    part = lax.psum_scatter(norm_grad, "head", scatter_dimension=1, tiled=True)
    norm = lax.psum_scatter(part, "dp", scatter_dimension=2, tiled=True)
    squares = sum([jnp.sum(a * a) for a in whole + [norm]])
    return whole, norm, lax.psum(squares, ("dp", "head"))


def wide_step(inputs, cotangent, lengths, w_qkv, w_out, w_up, w_down, norm_params):
    rows, model = inputs.shape
    layers = w_qkv.shape[0]
    plan = WidePlan(lengths, rows)
    fulls, norm_full = wide_gather(w_qkv, w_out, w_up, w_down, norm_params)
    norm_full = norm_full.astype(jnp.float32)
    hidden = inputs.astype(jnp.float32)
    kept = []
    for layer in range(layers):
        qkv_w, out_w, up_w, down_w = (a[layer] for a in fulls)
        gains = norm_full[layer]
        acts = hidden.astype(jnp.bfloat16)
        mixed = jnp.dot(acts, qkv_w, preferred_element_type=jnp.float32)
        soft = jax.nn.softplus(mixed[:, : 2 * model]).astype(jnp.bfloat16)
        q = soft[:, :model]
        k = soft[:, model:] * plan.valid[:, None].astype(jnp.bfloat16)
        v = mixed[:, 2 * model :].astype(jnp.bfloat16)
        attended, attend_kept = plan.attend(q, k, v)
        first_in = hidden + jnp.dot(attended, out_w, preferred_element_type=jnp.float32)
        first_out = layer_norm(first_in, gains[0], gains[1])
        first_low = first_out.astype(jnp.bfloat16)
        inner = jnp.dot(first_low, up_w, preferred_element_type=jnp.float32)
        act = gelu_exact(inner).astype(jnp.bfloat16)
        second_in = first_out + jnp.dot(act, down_w, preferred_element_type=jnp.float32)
        kept.append((acts, mixed, attend_kept, attended, first_in, first_low, inner, act, second_in))
        hidden = layer_norm(second_in, gains[2], gains[3])
    grad_hidden = cotangent.astype(jnp.float32)
    grads = [None] * layers
    norm_grads = [None] * layers
    for layer in reversed(range(layers)):
        acts, mixed, attend_kept, attended, first_in, first_low, inner, act, second_in = kept[layer]
        qkv_w, out_w, up_w, down_w = (a[layer] for a in fulls)
        gains = norm_full[layer]
        _, pull_two = jax.vjp(layer_norm, second_in, gains[2], gains[3])
        grad_second, dgain_two, dshift_two = pull_two(grad_hidden)
        branch_two = grad_second.astype(jnp.bfloat16)
        dw_down = contract_rows(act, branch_two).astype(jnp.bfloat16)
        grad_act = contract_cols(branch_two, down_w)
        _, gelu_pull = jax.vjp(gelu_exact, inner)
        grad_inner = gelu_pull(grad_act)[0].astype(jnp.bfloat16)
        dw_up = contract_rows(first_low, grad_inner).astype(jnp.bfloat16)
        grad_first = grad_second + contract_cols(grad_inner, up_w)
        _, pull_one = jax.vjp(layer_norm, first_in, gains[0], gains[1])
        grad_first_in, dgain_one, dshift_one = pull_one(grad_first)
        branch = grad_first_in.astype(jnp.bfloat16)
        dw_out = contract_rows(attended, branch).astype(jnp.bfloat16)
        dob = contract_cols(branch, out_w).astype(jnp.bfloat16)
        grad_mixed = plan.attend_back(attend_kept, dob)
        slope = jax.nn.sigmoid(mixed[:, : 2 * model])
        grad_soft = (grad_mixed[:, : 2 * model].astype(jnp.float32) * slope).astype(jnp.bfloat16)
        grad_pre = jnp.concatenate([grad_soft, grad_mixed[:, 2 * model :]], axis=1)
        dw_qkv = contract_rows(acts, grad_pre).astype(jnp.bfloat16)
        grad_hidden = grad_first_in + contract_cols(grad_pre, qkv_w)
        grads[layer] = (dw_qkv, dw_out, dw_up, dw_down)
        norm_grads[layer] = jnp.stack([dgain_one, dshift_one, dgain_two, dshift_two])
    whole, norm_sum, squares = wide_reduce(grads, jnp.stack(norm_grads))
    return hidden, grad_hidden, whole, norm_sum, squares


def body(
    inputs, cotangent, lengths,
    w_qkv, m_qkv, v_qkv, w_out, m_out, v_out, w_up, m_up, v_up, w_down, m_down, v_down,
    norm_params, m_norm, v_norm,
):
    rows = inputs.shape[0]
    near = lax.axis_size("dp") == 8 and lax.axis_size("head") == 4 and rows == 512
    hidden, grad_hidden, whole, norm_sum, squares = (near_step if near else wide_step)(
        inputs, cotangent, lengths, w_qkv, w_out, w_up, w_down, norm_params
    )
    grad_norm = jnp.sqrt(squares)
    factor = clip_limit / jnp.maximum(grad_norm, clip_limit)
    new_qkv = adam_step(w_qkv, m_qkv, v_qkv, whole[0], factor, rate_matrix, decay_rate)
    new_out = adam_step(w_out, m_out, v_out, whole[1], factor, rate_outproj, decay_rate)
    new_up = adam_step(w_up, m_up, v_up, whole[2], factor, rate_matrix, decay_rate)
    new_down = adam_step(w_down, m_down, v_down, whole[3], factor, rate_matrix, decay_rate)
    new_norm = adam_step(norm_params, m_norm, v_norm, norm_sum, factor, rate_norm, 0.0)
    return (
        (hidden, grad_hidden, grad_norm.reshape(1))
        + new_qkv + new_out + new_up + new_down + new_norm
    )


def solution(mesh):
    rows = P(("dp", "head"), None)
    weight = P(None, "dp", "head")
    norm = P(None, "head", "dp")
    in_specs = (rows, rows, P()) + (weight,) * 12 + (norm,) * 3
    out_specs = (rows, rows, P()) + (weight,) * 12 + (norm,) * 3
    return jax.shard_map(body, mesh=mesh, in_specs=in_specs, out_specs=out_specs, check_vma=False)
```

```python
import functools
import math
from typing import Any, NamedTuple

import jax
import jax.numpy as jnp
from jax import lax
from jax.experimental import pallas as pl
from jax.experimental.pallas import tpu as pltpu
from jax.sharding import PartitionSpec as P

HEADS = 12
LONGEST = 8192
HD = 64

exact_mode = lax.Precision.HIGHEST
beta_one = 0.9
beta_two = 0.999
adam_eps = 1e-08
decay_rate = 0.1
rate_matrix = 0.1
rate_outproj = 0.5
rate_norm = 0.5
clip_limit = 1.0
norm_eps = 1e-05
step_fixed = 10.0

MESH = pl.DeviceIdType.MESH
FIRST_X = (0, 3)
NORM, QKV, OUT, UP, DOWN = range(5)
MATRICES = (QKV, OUT, UP, DOWN)
BY_Z, BY_X, BY_Y, BY_CORE, BY_CORNER, ON_X, ON_Y, ON_CORNER = range(8)
CORE, ONE, TWO, LAST = range(4)


def place():
    dp, hd = lax.axis_index("dp"), lax.axis_index("head")
    return dp // 2, dp % 2, hd // 2, hd % 2


def at(z, x, y, c):
    return (z * 2 + x, y * 2 + c)


def flip(x, y, c, d):
    dx, dy, dc = d // 4, (d // 2) % 2, d % 2
    return 1 - x if dx else x, 1 - y if dy else y, 1 - c if dc else c


def partners():
    z, x, y, c = place()
    out = [at((z + d) % 4, x, y, c) for d in (1, 2, 3)]
    return out + [at(z, *flip(x, y, c, d)) for d in range(1, 8)]


def greet():
    barrier = pltpu.get_barrier_semaphore()
    devices = partners()
    for dev in devices:
        pl.semaphore_signal(barrier, inc=1, device_id=dev, device_id_type=MESH)
    pl.semaphore_wait(barrier, len(devices))


class Links:
    def __init__(self, send_sem, recv_sem):
        self.send_sem, self.recv_sem, self.copies = send_sem, recv_sem, []
        self.left = set()

    def send(self, src, dst, dev):
        k = len(self.copies)
        copy = pltpu.make_async_remote_copy(
            src_ref=src,
            dst_ref=dst,
            send_sem=self.send_sem.at[k],
            recv_sem=self.recv_sem.at[k],
            device_id=dev,
            device_id_type=MESH,
        )
        copy.start()
        self.copies.append(copy)
        self.left.add(k)
        copy.number = k
        return copy

    def sent(self, copy):
        copy.wait_send()
        self.left.discard(copy.number)

    def finish(self):
        for k in sorted(self.left):
            self.copies[k].wait_send()


class Moves:
    def __init__(self, sem):
        self.sem, self.copies = sem, []
        self.left = []

    def start(self, src, dst):
        copy = pltpu.make_async_copy(src, dst, self.sem.at[len(self.copies)])
        copy.start()
        self.copies.append(copy)
        self.left.append(copy)
        return copy

    def wait(self, copy):
        if any(copy is other for other in self.left):
            copy.wait()
        self.left = [other for other in self.left if other is not copy]

    def finish(self):
        for copy in self.left:
            copy.wait()
        self.left = []


def region(kind, rows, cols, z, x, y, c):
    strip, head = z * 2 + x, y * 2 + c
    if kind in (QKV, OUT, NORM):
        first, left = (strip * 2 + c) * rows, y * cols
    elif kind == UP:
        first, left = strip * rows, head * cols
    else:
        first, left = head * rows, strip * cols
    return (
        pl.ds(pl.multiple_of(first, rows), rows),
        pl.ds(pl.multiple_of(left, cols), cols),
    )


def whole_shape(kind, rows, cols):
    if kind in (QKV, OUT, NORM):
        return rows * 16, cols * 2
    if kind == UP:
        return rows * 8, cols * 4
    return rows * 4, cols * 8


class Kept(NamedTuple):
    acts: Any
    slope: Any
    soft: Any
    ob: Any
    den: Any
    state: Any
    xh1: Any
    xh2: Any
    rstd: Any
    n1b: Any
    gz: Any
    gu: Any


class Gather:
    def __init__(self, kind, piece, full, links, moves):
        self.kind, self.piece, self.full = kind, piece, full
        self.links, self.moves = links, moves
        self.z, self.x, self.y, self.c = place()
        self.copies = {}

    def spot(self, zz, xx, yy):
        rows, cols = self.piece.shape
        span = region(self.kind, rows, cols, zz, xx, yy, self.c)
        return self.full.at[span[0], span[1]]

    def origin(self, d):
        return (self.z + 4 - d) % 4 if d else self.z

    def begin(self, d):
        z, x, y, c = self.z, self.x, self.y, self.c
        if d:
            dev = at((z + d) % 4, x, y, c)
            self.copies[BY_Z, d] = self.links.send(self.piece, self.spot(z, x, y), dev)
        else:
            self.own = self.moves.start(self.piece, self.spot(z, x, y))

    def fan(self, d):
        z, x, y, c = self.z, self.x, self.y, self.c
        if d:
            self.copies[BY_Z, d].wait_recv()
        here = self.spot(self.origin(d), x, y)
        src = here if d else self.piece
        self.copies[BY_X, d] = self.links.send(src, here, at(z, 1 - x, y, c))
        self.copies[BY_Y, d] = self.links.send(src, here, at(z, x, 1 - y, c))
        self.copies[BY_CORE, d] = self.links.send(src, here, at(z, x, y, 1 - c))

    def second(self, d):
        z, x, y, c = self.z, self.x, self.y, self.c
        from_x, from_y = self.spot(self.origin(d), 1 - x, y), self.spot(self.origin(d), x, 1 - y)
        self.copies[BY_X, d].wait_recv()
        if d in FIRST_X:
            self.copies[BY_CORNER, d] = self.links.send(from_x, from_x, at(z, x, 1 - y, c))
        self.copies[ON_X, d] = self.links.send(from_x, from_x, at(z, x, y, 1 - c))
        self.copies[BY_Y, d].wait_recv()
        if d not in FIRST_X:
            self.copies[BY_CORNER, d] = self.links.send(from_y, from_y, at(z, 1 - x, y, c))
        self.copies[ON_Y, d] = self.links.send(from_y, from_y, at(z, x, y, 1 - c))

    def third(self, d):
        z, x, y, c = self.z, self.x, self.y, self.c
        block = self.spot(self.origin(d), 1 - x, 1 - y)
        self.copies[BY_CORNER, d].wait_recv()
        self.copies[ON_CORNER, d] = self.links.send(block, block, at(z, x, y, 1 - c))

    def ready(self):
        for key in (BY_CORE, ON_X, ON_Y, ON_CORNER):
            for d in range(4):
                self.copies[key, d].wait_recv()
        self.moves.wait(self.own)


class Exchange:
    def __init__(self, coef, refs, links, reverse):
        self.coef, self.reverse, self.links = coef, reverse, links
        self.mine, self.got, self.sums, self.got_z, self.back, self.result = refs
        self.z, self.x, self.y, self.c = place()
        self.index = self.x * 4 + self.y * 2 + self.c

    def scatter(self):
        self.got[self.index] = self.mine[self.index]
        self.first = []
        for d in range(1, 8):
            nx, ny, nc = flip(self.x, self.y, self.c, d)
            src = self.mine.at[nx * 4 + ny * 2 + nc]
            dev = at(self.z, nx, ny, nc)
            self.first.append(self.links.send(src, self.got.at[self.index], dev))

    def across(self):
        for copy in self.first:
            copy.wait_recv()
        self.planes = []
        for d in (1, 2, 3):
            total = jnp.zeros(self.got.shape[1:], jnp.float32)
            for j in range(8):
                factor = self.coef[8 + d : 9 + d, j : j + 1]
                total = total + factor * self.got[j].astype(jnp.float32)
            self.sums[d - 1] = total.astype(jnp.bfloat16)
            dev = at((self.z + d) % 4, self.x, self.y, self.c)
            self.planes.append(self.links.send(self.sums.at[d - 1], self.got_z.at[d - 1], dev))

    def gather(self):
        for copy in self.planes:
            copy.wait_recv()
        parts = [self.got[j].astype(jnp.float32) for j in range(8)]
        parts += [self.got_z[d].astype(jnp.float32) for d in range(3)]
        for i in range(8):
            total = jnp.zeros(self.got.shape[1:], jnp.float32)
            span = range(i + 1, 8) if self.reverse else range(i)
            for j in list(span) + [8, 9, 10]:
                total = total + self.coef[i : i + 1, j : j + 1] * parts[j]
            self.back[i] = total.astype(jnp.bfloat16)
        self.result[self.index] = self.back[self.index]
        self.last = []
        for d in range(1, 8):
            nx, ny, nc = flip(self.x, self.y, self.c, d)
            src = self.back.at[nx * 4 + ny * 2 + nc]
            dev = at(self.z, nx, ny, nc)
            self.last.append(self.links.send(src, self.result.at[self.index], dev))

    def finish(self):
        for copy in self.last:
            copy.wait_recv()
        for copy in self.first + self.planes + self.last:
            self.links.sent(copy)


def exchange_scratch(width, layers):
    counts = (8, 3, 8) + (8, 3, 8) * layers
    return [pltpu.VMEM((n, 16, width), jnp.bfloat16) for n in counts]


def exchange_refs(refs, layer):
    mine, sums, back = refs[:3]
    got, got_z, result = refs[3 + 3 * layer : 6 + 3 * layer]
    return mine, got, sums, got_z, back, result


def mm(a, b):
    return lax.dot_general(a, b, (((1,), (0,)), ((), ())), preferred_element_type=jnp.float32)


def mm_nt(a, b):
    return lax.dot_general(a, b, (((1,), (1,)), ((), ())), preferred_element_type=jnp.float32)


def mm_tn(a, b):
    return lax.dot_general(a, b, (((0,), (0,)), ((), ())), preferred_element_type=jnp.float32)


def low_lanes(shape):
    return lax.broadcasted_iota(jnp.int32, shape, len(shape) - 1) < HD


def lane_is(shape, h):
    return lax.broadcasted_iota(jnp.int32, shape, len(shape) - 1) == h


def pair_cols(p):
    return slice(p * 128, (p + 1) * 128)


def pack_state(ref, p, kind, block, extra):
    low = low_lanes((64, 128))
    packed = jnp.where(low, block[:64, :128], block[64:, :128]).astype(jnp.bfloat16)
    for s in range(4):
        ref[kind * 4 + s, :, pair_cols(p)] = packed[s * 16 : (s + 1) * 16]
    if extra is None:
        extra = jnp.zeros((64, 128), jnp.float32)
    extra = extra + jnp.where(lane_is((64, 128), 2 * p), block[:64, 128:], 0.0)
    return extra + jnp.where(lane_is((64, 128), 2 * p + 1), block[64:, 128:], 0.0)


def store_extra(ref, kind, extra, width):
    extra = extra.astype(jnp.bfloat16)
    for s in range(4):
        ref[kind * 4 + s, :, width - 128 :] = extra[s * 16 : (s + 1) * 16]


def unpack_state(ref, p, kind, width):
    packed = jnp.concatenate([ref[kind * 4 + s, :, pair_cols(p)] for s in range(4)], axis=0)
    sums = jnp.concatenate([ref[kind * 4 + s, :, width - 128 :] for s in range(4)], axis=0)
    low = low_lanes((64, 128))
    zero = jnp.zeros((64, 128), jnp.bfloat16)
    top = jnp.concatenate(
        [jnp.where(low, packed, zero), jnp.where(lane_is((64, 128), 2 * p), sums, zero)], axis=1
    )
    bottom = jnp.concatenate(
        [jnp.where(low, zero, packed), jnp.where(lane_is((64, 128), 2 * p + 1), sums, zero)],
        axis=1,
    )
    return jnp.concatenate([top, bottom], axis=0)


def spread(values, p):
    rows = values.shape[0]
    first = jnp.broadcast_to(values[:, 2 * p : 2 * p + 1], (rows, 128))
    second = jnp.broadcast_to(values[:, 2 * p + 1 : 2 * p + 2], (rows, 128))
    return jnp.where(low_lanes((rows, 128)), first, second)


def iota(shape, axis):
    return lax.broadcasted_iota(jnp.int32, shape, axis)


def stream_tables(lengths_ref, w_ref, aux_ref, ahead_ref, behind_ref):
    z, x, y, c = place()
    rows = w_ref.shape[0]
    count = lengths_ref.shape[1]
    me = z * 8 + x * 4 + y * 2 + c
    line, lane = iota((count, count), 0), iota((count, count), 1)
    lens = jnp.broadcast_to(lengths_ref[...].astype(jnp.float32), (count, count))
    total = jnp.sum(lens[:1], axis=1, keepdims=True)
    len_col = jnp.sum(jnp.where(line == lane, lens, 0.0), axis=1, keepdims=True)
    start_col = jnp.sum(jnp.where(lane < line, lens, 0.0), axis=1, keepdims=True)
    start_row = jnp.sum(jnp.where(line < lane, len_col, 0.0), axis=0, keepdims=True)

    def sequence(ids, axis):
        starts = start_row if axis else start_col
        begun = starts <= ids
        raw = jnp.sum(jnp.where(begun, 1.0, 0.0), axis=axis, keepdims=True) - 1.0
        first = jnp.max(jnp.where(begun, starts, 0.0), axis=axis, keepdims=True)
        inside = ids < total
        seg = jnp.where(inside, raw, 1.0 * count)
        angle = jnp.where(inside, ids - first, 0.0) * (0.5 * math.pi / LONGEST)
        return seg, angle, inside

    def ids_of(numbers):
        return numbers.astype(jnp.float32)

    seg_col, angle, inside = sequence(ids_of(me * rows + iota((rows, 1), 0)), 1)
    cos_col, sin_col = jnp.cos(angle), jnp.sin(angle)
    seg_row, angle, _ = sequence(ids_of(me * rows + iota((1, rows), 1)), 0)
    cos_row, sin_row = jnp.cos(angle), jnp.sin(angle)
    before = sequence(ids_of(me * rows - 1 + iota((1, 1), 0)), 1)[0]
    last = sequence(ids_of(me * rows + rows - 1 + iota((1, 1), 0)), 1)[0]
    spot = iota((rows, 128), 1)
    aux = jnp.where(spot == 0, cos_col, jnp.where(spot == 1, sin_col, 0.0))
    aux = aux + jnp.where((spot == 2) & (seg_col == before), 1.0, 0.0)
    aux = aux + jnp.where((spot == 3) & (seg_col == last), 1.0, 0.0)
    aux_ref[...] = aux + jnp.where((spot == 4) & inside, 1.0, 0.0)
    for i in range(0, rows, 128):
        part = slice(i, i + 128)
        close = cos_col[part] * cos_row + sin_col[part] * sin_row
        allowed = (seg_col[part] == seg_row) & (iota((128, rows), 1) <= iota((128, rows), 0) + i)
        w_ref[part, :] = jnp.where(allowed, close, 0.0)

    i, j = iota((8, 128), 0), iota((8, 128), 1)
    lane = iota((1, 128), 1)
    own = lane < 8
    source = (z + 11 - jnp.minimum(lane, 11)) % 4
    others = (lane >= 8) & (lane < 11)
    end = sequence(ids_of((z * 8 + 8) * rows - 1 + iota((1, 1), 0)), 1)[0]
    devices = z * 8 + iota((8, 1), 0)
    before_col = sequence(ids_of(devices * rows - 1), 1)[0]
    last_col = sequence(ids_of(devices * rows + rows - 1), 1)[0]
    at_lanes = jnp.where(own, z * 8 + lane + 1, source * 8 + 8)
    last_row = sequence(ids_of(at_lanes * rows - 1), 0)[0]
    before_row = sequence(ids_of((z * 8 + jnp.minimum(lane, 7)) * rows - 1), 0)[0]
    seen = ((own & (i > j)) | (others & (source < z))) & (before_col == last_row)
    ahead_ref[0:8, :] = jnp.where(seen, 1.0, 0.0)
    seen = own & (j > i) & (last_col == before_row)
    seen = seen | (others & (source > z) & (last_col == end))
    behind_ref[0:8, :] = jnp.where(seen, 1.0, 0.0)
    target = (z + i) % 4
    target_col = (z + iota((8, 1), 0)) % 4
    target_end = sequence(ids_of((target_col * 8 + 8) * rows - 1), 1)[0]
    given = own & (i >= 1) & (i <= 3)
    ahead_ref[8:16, :] = jnp.where(given & (last_row == end), 1.0, 0.0)
    given = given & (target < z) & (before_row == target_end)
    behind_ref[8:16, :] = jnp.where(given, 1.0, 0.0)


def assemble_gains(full, layers):
    spots = lax.broadcasted_iota(jnp.int32, (128, 768), 0)
    lanes = lax.broadcasted_iota(jnp.int32, (128, 768), 1)
    total = jnp.zeros((64, 768), jnp.float32)
    for dp in range(8):
        both = full[dp * 32 : (dp + 1) * 32, :]
        left = jnp.concatenate([both[:, :128], both[:, 128:]], axis=0)
        put = jnp.where((lanes == spots + dp * 96) & (spots < 96), 1.0, 0.0).astype(jnp.bfloat16)
        total = total + mm(left, put)
    return [
        jnp.concatenate([total[head * 16 + i : head * 16 + i + 1] for head in range(4)], axis=0)
        for i in range(layers)
    ]


AHEAD, SECOND, THIRD = 8, 8, 14
PUMP = 4


def forward_kernel(layers, pairs, lengths_ref, x_ref, *refs):
    order = (NORM,) + MATRICES
    pieces = refs[:5]
    h_out, gains_out, w_ref, aux_ref, behind_ref = refs[5:10]
    refs = refs[10:]
    full_out = [(None,) + refs[4 * i : 4 * i + 4] for i in range(layers)]
    refs = refs[4 * layers :]
    saved = [Kept(*refs[12 * i : 12 * i + 12]) for i in range(layers)]
    rest = refs[12 * layers :]
    full = [(rest[0],) + rest[1 + 4 * i : 5 + 4 * i] for i in range(layers)]
    rest = rest[1 + 4 * layers :]
    hold = Kept(*rest[:5], None, *rest[5:11])
    num, n1, h_mid = rest[11:14]
    ex_refs = [exchange_refs(rest[14:], i) for i in range(layers)]
    coef, send_sem, recv_sem, move_sem = rest[-4:]
    rows, model = x_ref.shape
    half = rows // 2
    width = model + 128
    links, moves = Links(send_sem, recv_sem), Moves(move_sem)
    greet()
    norms = Gather(NORM, pieces[NORM], full[0][NORM], links, moves)
    every = [
        [norms]
        + [Gather(k, pieces[k].at[i], full[i][k], links, moves) for k in MATRICES]
        for i in range(layers)
    ]

    steps = []

    done = [0]

    def pump(n):
        while n > 0 and done[0] < len(steps):
            steps[done[0]]()
            done[0] += 1
            n -= 1

    def until(mark):
        pump(mark - done[0])

    chain = [part for parts in every for part in parts[1:]]
    chain.insert(2, norms)
    line = [(part, d) for part in chain for d in (0, 1, 3, 2)]
    marks = {}
    for i in range(-AHEAD, len(line) + THIRD):
        for stage, lag in ((0, -AHEAD), (1, 0), (2, SECOND), (3, THIRD)):
            if 0 <= i - lag < len(line):
                part, d = line[i - lag]
                steps.append(functools.partial((part.begin, part.fan, part.second, part.third)[stage], d))
                marks[id(part)] = len(steps)

    pump(2 * AHEAD)
    stream_tables(lengths_ref, w_ref, aux_ref, coef, behind_ref)
    cos, sin = aux_ref[:, 0:1], aux_ref[:, 1:2]
    follow, tail, valid = aux_ref[:, 2:3], aux_ref[:, 3:4], aux_ref[:, 4:5]
    soft = hold.soft

    def q_of(p):
        return soft[:, p * 128 : (p + 1) * 128]

    def k_of(p):
        return soft[:, model + p * 128 : model + (p + 1) * 128]

    def v_of(p):
        return soft[:, 2 * model + p * 128 : 2 * model + (p + 1) * 128]

    def one_layer(layer):
        parts, whole, keep = every[layer], full[layer], saved[layer]
        mark = [marks[id(part)] for part in parts]
        h_ref = h_mid if layer else x_ref
        h_next = h_out if layer == layers - 1 else h_mid
        ex = Exchange(coef, ex_refs[layer], links, False)
        hold.acts[...] = h_ref[...].astype(jnp.bfloat16)
        moves.start(hold.acts, keep.acts)
        until(mark[QKV])
        parts[QKV].ready()
        moves.start(whole[QKV], full_out[layer][QKV])
        acts = hold.acts[...]
        for j in range(3 * model // 256):
            span = slice(j * 256, (j + 1) * 256)
            p = mm(acts, whole[QKV][:, span])
            if j * 256 < 2 * model:
                t = jnp.exp(-jnp.abs(p))
                hold.slope[:, span] = (jnp.where(p >= 0, 1.0, t) / (1.0 + t)).astype(jnp.bfloat16)
                p = jnp.maximum(p, 0.0) + jnp.log1p(t)
                if j * 256 >= model:
                    p = p * valid
            soft[:, span] = p.astype(jnp.bfloat16)
            if j % 3 == 2:
                pump(1)
        moves.start(hold.slope, keep.slope)
        moves.start(soft, keep.soft)

        ones = jnp.ones((rows, 128), jnp.bfloat16)
        extras = [None, None]
        for p in range(pairs):
            kp = k_of(p).astype(jnp.float32) * tail
            rhs = jnp.concatenate([v_of(p), ones], axis=1)
            for kind, angle in enumerate((cos, sin)):
                block = mm_tn((kp * angle).astype(jnp.bfloat16), rhs)
                extras[kind] = pack_state(ex.mine, p, kind, block, extras[kind])
        for kind in range(2):
            store_extra(ex.mine, kind, extras[kind], width)
        ex.scatter()
        den_ref = hold.den

        def inner(p):
            kp, vp = k_of(p), v_of(p)
            low = low_lanes((rows, 128))
            zero = jnp.zeros((rows, 128), jnp.bfloat16)
            out = []
            for e in range(2):
                qh = jnp.where(low if e == 0 else ~low, q_of(p), zero)
                mark_head = lane_is((rows, 128), 2 * p + e).astype(jnp.bfloat16)
                rhs = jnp.concatenate([vp, mark_head], axis=1)
                top = mm_nt(qh[:half], kp[:half]) * w_ref[:half, :half]
                bottom = mm_nt(qh[half:], kp) * w_ref[half:, :]
                top, bottom = top.astype(jnp.bfloat16), bottom.astype(jnp.bfloat16)
                out.append(jnp.concatenate([mm(top, rhs[:half]), mm(bottom, rhs)], axis=0))
            num[:, pair_cols(p)] = jnp.where(low, out[0][:, :128], out[1][:, :128])
            dens = out[0][:, 128:] + out[1][:, 128:]
            if p == 0:
                den_ref[...] = dens
            else:
                den_ref[...] += dens

        for p in range(pairs):
            inner(p)
            if p == 1:
                ex.across()
            if p == 3:
                ex.gather()
            pump(PUMP)
        ex.finish()
        moves.start(ex.result, keep.state)
        den = den_ref[...]
        cf, sf = cos * follow, sin * follow
        for p in range(pairs):
            qp = q_of(p)
            extra = cf * mm(qp, unpack_state(ex.result, p, 0, width))
            extra += sf * mm(qp, unpack_state(ex.result, p, 1, width))
            num[:, pair_cols(p)] += extra[:, :128]
            den = den + extra[:, 128:]
        den_ref[...] = den
        moves.start(hold.den, keep.den)
        inv = 1.0 / jnp.maximum(den, 1.0)
        ob = hold.ob
        for p in range(pairs):
            ob[:, pair_cols(p)] = (num[:, pair_cols(p)] * spread(inv, p)).astype(jnp.bfloat16)
        moves.start(hold.ob, keep.ob)
        until(mark[OUT])
        parts[OUT].ready()
        moves.start(whole[OUT], full_out[layer][OUT])

        def norm(x_ref, which, low_ref, whole_ref):
            gain, shift = gains[2 * which], gains[2 * which + 1]
            for i in range(0, rows, 128):
                x = x_ref[i : i + 128, :]
                centered = x - jnp.mean(x, axis=1, keepdims=True)
                variance = jnp.mean(centered * centered, axis=1, keepdims=True)
                r = lax.rsqrt(variance + norm_eps)
                xh = centered * r
                x_ref[i : i + 128, :] = xh
                new = jnp.broadcast_to(r, (128, 128))
                if which:
                    new = jnp.where(low_lanes((128, 128)), hold.rstd[i : i + 128, :], new)
                hold.rstd[i : i + 128, :] = new
                y = xh * gain + shift
                whole_ref[i : i + 128, :] = y
                if low_ref is not None:
                    low_ref[i : i + 128, :] = y.astype(jnp.bfloat16)

        if layer == 0:
            until(mark[NORM])
            norms.ready()
            for i, lines in enumerate(assemble_gains(whole[NORM], layers)):
                gains_out[i, 0:4, :] = lines
                gains_out[i, 4:8, :] = jnp.zeros((4, model), jnp.float32)
        gains = [gains_out[layer, i : i + 1, :] for i in range(4)]
        attended = ob[...]
        for j in range(model // 256):
            span = slice(j * 256, (j + 1) * 256)
            first_in = h_ref[:, span].astype(jnp.float32)
            hold.xh1[:, span] = first_in + mm(attended, whole[OUT][:, span])
        norm(hold.xh1, 0, hold.n1b, n1)
        moves.start(hold.xh1, keep.xh1)
        moves.start(hold.n1b, keep.n1b)
        until(mark[UP])
        parts[UP].ready()
        moves.start(whole[UP], full_out[layer][UP])
        n1b = hold.n1b[...]
        hidden = whole[UP].shape[1]
        for j in range(hidden // 256):
            span = slice(j * 256, (j + 1) * 256)
            u = mm(n1b, whole[UP][:, span])
            phi = 0.5 * (1.0 + lax.erf(u * math.sqrt(0.5)))
            hold.gz[:, span] = (u * phi).astype(jnp.bfloat16)
            bell = jnp.exp(-0.5 * u * u) * (1.0 / math.sqrt(2.0 * math.pi))
            hold.gu[:, span] = (phi + u * bell).astype(jnp.bfloat16)
            pump(1)
        moves.start(hold.gz, keep.gz)
        moves.start(hold.gu, keep.gu)
        until(mark[DOWN])
        parts[DOWN].ready()
        moves.start(whole[DOWN], full_out[layer][DOWN])
        gz = hold.gz[...]
        for j in range(model // 256):
            span = slice(j * 256, (j + 1) * 256)
            hold.xh2[:, span] = n1[:, span] + mm_nt(gz, whole[DOWN][span, :])
        norm(hold.xh2, 1, None, h_next)
        moves.start(hold.xh2, keep.xh2)
        moves.start(hold.rstd, keep.rstd)
        moves.finish()

    for layer in range(layers):
        one_layer(layer)
    links.finish()


def forward(number, lengths, inputs, pieces):
    rows, model = inputs.shape
    layers = pieces[1].shape[0]
    order = (NORM,) + MATRICES
    fulls = [whole_shape(k, *p.shape[-2:]) for k, p in zip(order, pieces)]
    hidden = fulls[UP][1]
    width = model + 128
    low, wide = jnp.bfloat16, jnp.float32
    kept = Kept(
        acts=((rows, model), low),
        slope=((rows, 2 * model), low),
        soft=((rows, 3 * model), low),
        ob=((rows, model), low),
        den=((rows, 128), wide),
        state=((8, 16, width), low),
        xh1=((rows, model), wide),
        xh2=((rows, model), wide),
        rstd=((rows, 128), wide),
        n1b=((rows, model), low),
        gz=((rows, hidden), low),
        gu=((rows, hidden), low),
    )
    vmem = pl.BlockSpec(memory_space=pltpu.VMEM)
    anywhere = pl.BlockSpec(memory_space=pl.ANY)
    scratch = [pltpu.VMEM(s, low) for s in fulls[:1] + fulls[1:] * layers]
    scratch += [pltpu.VMEM(*a) for a in kept[:5] + kept[6:]]
    scratch += [pltpu.VMEM((rows, model), wide)] * 3
    scratch += exchange_scratch(width, layers)
    scratch += [pltpu.VMEM((16, 128), wide)]
    scratch += [pltpu.SemaphoreType.DMA((layers * 141 + 31,))] * 2
    scratch += [pltpu.SemaphoreType.DMA((layers * 22,))]
    outs = pl.pallas_call(
        functools.partial(forward_kernel, layers, model // 128),
        out_shape=[
            jax.ShapeDtypeStruct((rows, model), wide),
            jax.ShapeDtypeStruct((layers, 8, model), wide),
            jax.ShapeDtypeStruct((rows, rows), wide),
            jax.ShapeDtypeStruct((rows, 128), wide),
            jax.ShapeDtypeStruct((16, 128), wide),
        ]
        + [jax.ShapeDtypeStruct(s, low) for s in fulls[1:]] * layers
        + [jax.ShapeDtypeStruct(s, t) for s, t in kept] * layers,
        in_specs=[vmem] * 2 + [anywhere] * 5,
        out_specs=[vmem] * 5 + [anywhere] * (layers * (4 + len(kept))),
        scratch_shapes=scratch,
        compiler_params=pltpu.CompilerParams(
            collective_id=number, has_side_effects=True, vmem_limit_bytes=61 * 2**20
        ),
        name="forward_layers",
    )(lengths.reshape(1, -1), inputs, *pieces)
    h_out, gains, tables, outs = outs[0], outs[1], outs[2:5], outs[5:]
    held = []
    for i in range(layers):
        held.append((outs[4 * i : 4 * i + 4], Kept(*outs[4 * layers + 12 * i :][:12])))
    return h_out, gains, tables, held


class Reduce:
    def __init__(self, own, core_in, one_y, one_x, two, from_z, links):
        self.own, self.core_in, self.links = own, core_in, links
        self.one_y, self.one_x, self.two, self.from_z = one_y, one_x, two, from_z
        self.z, self.x, self.y, self.c = place()
        self.rows, self.cols = two.shape[1], two.shape[2]
        self.copies = {}

    def plane(self, d):
        return (self.z + d) % 4 if d else self.z

    def side(self, yy):
        return pl.ds(pl.multiple_of(yy * self.cols, self.cols), self.cols)

    def strip(self, number, count=1):
        return pl.ds(pl.multiple_of(number * self.rows, self.rows), count * self.rows)

    def both(self, d):
        return self.strip(self.plane(d) * 2, 2)

    def give(self, ref, d):
        span = self.both(d)
        dev = at(self.z, self.x, self.y, 1 - self.c)
        copy = self.links.send(ref.at[span, pl.ds(0, 2 * self.cols)], self.core_in.at[span], dev)
        self.copies[CORE, d] = copy

    def given(self):
        for d in range(4):
            self.links.sent(self.copies[CORE, d])

    def release(self, free_sem):
        z, x, y, c = self.z, self.x, self.y, self.c
        for key, copy in self.copies.items():
            if copy.number in self.links.left:
                self.links.sent(copy)
        near = [at(z, 1 - x, y, c), at(z, x, 1 - y, c), at(z, x, y, 1 - c)]
        for dev in near + [at((z + d) % 4, x, y, c) for d in (1, 2, 3)]:
            pl.semaphore_signal(free_sem, inc=1, device_id=dev, device_id_type=MESH)

    def add(self, span, other):
        here = self.own[span].astype(jnp.float32)
        self.own[span] = (here + other.astype(jnp.float32)).astype(jnp.bfloat16)

    def one(self, d):
        z, x, y, c = self.z, self.x, self.y, self.c
        self.copies[CORE, d].wait_recv()
        self.add((self.both(d), slice(None)), self.core_in[self.both(d), :])
        if d in FIRST_X:
            src = self.own.at[self.both(d), self.side(1 - y)]
            dst, dev = self.one_y.at[FIRST_X.index(d)], at(z, x, 1 - y, c)
        else:
            src = self.own.at[self.strip(self.plane(d) * 2 + 1 - x)]
            dst, dev = self.one_x.at[d - 1], at(z, 1 - x, y, c)
        self.copies[ONE, d] = self.links.send(src, dst, dev)

    def second(self, d):
        z, x, y, c = self.z, self.x, self.y, self.c
        self.copies[ONE, d].wait_recv()
        self.links.sent(self.copies[ONE, d])
        near, far = self.strip(self.plane(d) * 2 + x), self.strip(self.plane(d) * 2 + 1 - x)
        if d in FIRST_X:
            self.add((self.both(d), self.side(y)), self.one_y[FIRST_X.index(d)])
            src, dev = self.own.at[far, self.side(y)], at(z, 1 - x, y, c)
        else:
            self.add((near, slice(None)), self.one_x[d - 1])
            src, dev = self.own.at[near, self.side(1 - y)], at(z, x, 1 - y, c)
        self.copies[TWO, d] = self.links.send(src, self.two.at[d], dev)

    def third(self, d):
        z, x, y, c = self.z, self.x, self.y, self.c
        self.copies[TWO, d].wait_recv()
        near = (self.strip(self.plane(d) * 2 + x), self.side(y))
        self.add(near, self.two[d])
        if d:
            src, dst = self.own.at[near[0], near[1]], self.from_z.at[d - 1]
            self.copies[LAST, d] = self.links.send(src, dst, at(self.plane(d), x, y, c))

    def last(self, out_ref, squares, swap=None):
        value = self.own[self.strip(self.z * 2 + self.x), self.side(self.y)].astype(jnp.float32)
        for d in (1, 2, 3):
            self.copies[LAST, d].wait_recv()
            value = value + self.from_z[d - 1].astype(jnp.float32)
        if swap is None:
            out_ref[...] = value
        else:
            half = self.cols // 2
            give_ref, got_ref = swap
            low, high = value[:, :half], value[:, half:]
            out_ref[...] = jnp.where(self.c == 0, low, high)
            give_ref[...] = jnp.where(self.c == 0, high, low)
            dev = at(self.z, self.x, self.y, 1 - self.c)
            self.swapped = self.links.send(give_ref, got_ref, dev)
        part = jnp.sum((value * value).reshape(self.rows // 8, 8, self.cols), axis=0)
        for j in range(self.cols // 128):
            squares[0] += part[:, j * 128 : (j + 1) * 128]


def backward_kernel(layers, pairs, coef, w_ref, aux_ref, dh_in, gains_ref, *refs):
    kept = [Kept(*refs[12 * i : 12 * i + 12]) for i in range(layers)]
    refs = refs[12 * layers :]
    weights = [(None,) + refs[4 * i : 4 * i + 4] for i in range(layers)]
    refs = refs[4 * layers :]
    dh = refs[0]
    sums = [(None,) + refs[1 + 4 * i : 5 + 4 * i] for i in range(layers)]
    gots = [refs[1 + 4 * layers + 2 * i :][:2] for i in range(layers)]
    norm_out, square_out = refs[1 + 6 * layers : 3 + 6 * layers]
    rest = refs[3 + 6 * layers :]
    free_sem, send_sem, recv_sem, move_sem = rest[-4:]
    norms, norm_z, norm_plane, squares, square_z, square_plane = rest[-10:-4]
    swaps = [rest[-10 - 2 * (i + 1) : -8 - 2 * (i + 1)] for i in range(layers)]
    links, moves = Links(send_sem, recv_sem), Moves(move_sem)
    reds = [[None] + [Reduce(*rest[i:24:4], links) for i in range(4)] for _ in range(layers)]
    give_a, give_b, buf_a, buf_b, w_out = rest[24:29]
    hold = Kept(*rest[29:31], None, *rest[31:40])
    drb, turned, dd_ref = rest[40:43]
    ex_refs = [exchange_refs(rest[43:], i) for i in range(layers)]
    rows, model = dh.shape
    half = rows // 2
    width = model + 128
    hidden = hold.gz.shape[1]
    z, x, y, c = place()
    even = c == 0

    loads = {}

    def load(number, src, dst):
        loads[number] = moves.start(src, dst)

    def need(*numbers):
        for number in numbers:
            moves.wait(loads[number])

    def load_early(layer):
        have = kept[layer]
        load(0, have.xh2, hold.xh2)
        load(1, have.rstd, hold.rstd)
        load(2, weights[layer][DOWN], buf_a)
        load(3, have.n1b, hold.n1b)
        load(4, have.xh1, hold.xh1)
        load(5, have.ob, hold.ob)
        load(6, have.den, hold.den)
        load(7, have.state, hold.state)
        load(8, have.slope, hold.slope)
        load(9, weights[layer][OUT], w_out)

    def load_late(layer):
        load(11, kept[layer].gu, hold.gu)
        load(12, weights[layer][UP], buf_b)

    steps, done, pushed, closed = [], [0], [], {}

    def pump(n):
        while n > 0 and done[0] < len(steps):
            steps[done[0]]()
            done[0] += 1
            n -= 1

    def until(mark):
        pump(mark - done[0])

    def later_stages(i):
        for stage in (1, 2, 3):
            if 0 <= i - stage < len(pushed):
                layer, kind = pushed[i - stage]
                red = reds[layer][kind]
                if stage < 3:
                    for d in (2, 3, 1, 0):
                        steps.append(functools.partial((red.second, red.third)[stage - 1], d))
                else:
                    swap = None
                    if kind in (QKV, OUT):
                        swap = (swaps[layer][kind - 1], gots[layer][kind - 1])
                    steps.append(functools.partial(red.last, sums[layer][kind], squares, swap))
                    if layer:
                        steps.append(functools.partial(red.release, free_sem.at[kind]))
                    closed[layer, kind] = len(steps)

    def take(layer, kind):
        if layer < layers - 1:
            until(closed[layer + 1, kind])

    def credit(layer, kind):
        if layer < layers - 1:
            pl.semaphore_wait(free_sem.at[kind], 6)

    def push(layer, kind, ref):
        red = reds[layer][kind]
        credit(layer, kind)
        for d in (2, 3, 1, 0):
            red.give(ref, d)
        pushed.append((layer, kind))
        for d in (2, 3, 1, 0):
            steps.append(functools.partial(red.one, d))
        later_stages(len(pushed) - 1)

    load(10, kept[layers - 1].gz, hold.gz)
    first_dh = moves.start(dh_in, dh)
    load_early(layers - 1)
    load_late(layers - 1)
    greet()
    squares[...] = jnp.zeros(squares.shape, jnp.float32)
    devices = partners()

    class Total:
        def __init__(self, mine, from_z, from_plane, out):
            self.refs = (mine, from_z, from_plane, out)

        def start(self):
            mine, from_z, _, _ = self.refs
            self.copies = [links.send(mine.at[0], from_z.at[i], devices[i]) for i in range(3)]

        def middle(self):
            mine, from_z, from_plane, _ = self.refs
            total = mine[0]
            for i in range(3):
                self.copies[i].wait_recv()
                total = total + from_z[i]
            mine[1] = total
            self.copies = [
                links.send(mine.at[1], from_plane.at[i], devices[3 + i]) for i in range(7)
            ]

        def end(self):
            mine, _, from_plane, out = self.refs
            total = mine[1]
            for i in range(7):
                self.copies[i].wait_recv()
                total = total + from_plane[i]
            out[...] = total

    norm_total = Total(norms, norm_z, norm_plane, norm_out)
    square_total = Total(squares, square_z, square_plane, square_out)
    moves.wait(first_dh)

    cos, sin = aux_ref[:, 0:1], aux_ref[:, 1:2]
    follow, tail, valid = aux_ref[:, 2:3], aux_ref[:, 3:4], aux_ref[:, 4:5]
    low = low_lanes((rows, 128))
    zero = jnp.zeros((rows, 128), jnp.bfloat16)
    ones = jnp.ones((rows, 128), jnp.bfloat16)
    cf, sf = cos * follow, sin * follow
    ct, st = cos * tail, sin * tail

    def turn(ref):
        for i in range(0, model, 256):
            turned[i : i + 256, :] = ref[:, i : i + 256].astype(jnp.float32).T.astype(jnp.bfloat16)

    def choose(first, second):
        return jnp.where(even, first, second), jnp.where(even, second, first)

    def split_rows(block, mine_ref, theirs_ref, span):
        for strip in range(8):
            mine, theirs = choose(
                block[strip * 96 : strip * 96 + 48], block[strip * 96 + 48 : strip * 96 + 96]
            )
            mine_ref[strip * 48 : (strip + 1) * 48, span] = mine
            theirs_ref[strip * 48 : (strip + 1) * 48, span] = theirs

    def q_of(p):
        return buf_a[:rows, p * 128 : (p + 1) * 128]

    def k_of(p):
        return buf_a[:rows, model + p * 128 : model + (p + 1) * 128]

    def v_of(p):
        return buf_a[:rows, 2 * model + p * 128 : 2 * model + (p + 1) * 128]

    def one_layer(layer):
        red = reds[layer]
        down, up, out, qkv = red[DOWN], red[UP], red[OUT], red[QKV]
        ex = Exchange(coef, ex_refs[layer], links, True)

        def norm_back(xh_ref, which):
            gain = gains_ref[layer, 2 * which : 2 * which + 1, :]
            dg = jnp.zeros((8, model), jnp.float32)
            db = jnp.zeros((8, model), jnp.float32)
            for i in range(0, rows, 128):
                dy, xh = dh[i : i + 128, :], xh_ref[i : i + 128, :]
                r = hold.rstd[i : i + 128, which * 64 : which * 64 + 1]
                e = dy * gain
                both = dy * xh
                dx = e - jnp.mean(e, axis=1, keepdims=True)
                dx = r * (dx - xh * jnp.mean(e * xh, axis=1, keepdims=True))
                dg = dg + jnp.sum(both.reshape(16, 8, model), axis=0)
                db = db + jnp.sum(dy.reshape(16, 8, model), axis=0)
                dh[i : i + 128, :] = dx
                drb[i : i + 128, :] = dx.astype(jnp.bfloat16)
                pump(1)
            at_line = 4 * layer + 2 * which
            norms[0, at_line : at_line + 1, :] = jnp.sum(dg, axis=0, keepdims=True)
            norms[0, at_line + 1 : at_line + 2, :] = jnp.sum(db, axis=0, keepdims=True)

        need(0, 1)
        norm_back(hold.xh2, 1)
        turn(drb)
        need(10)
        take(layer, DOWN)
        left = turned[...]
        for strip in range(8):
            block = mm(left, hold.gz[:, strip * 384 : (strip + 1) * 384]).astype(jnp.bfloat16)
            for yy in range(2):
                first = block[yy * 384 : yy * 384 + 192]
                second = block[yy * 384 + 192 : yy * 384 + 384]
                mine, theirs = choose(first, second)
                span = slice(strip * 192, (strip + 1) * 192)
                down.own[span, yy * 384 : (yy + 1) * 384] = mine
                give_a[span, yy * 384 : (yy + 1) * 384] = theirs
            pump(1)
        push(layer, DOWN, give_a)
        need(2, 11)
        low_grad = drb[...]
        for j in range(hidden // 256):
            span = slice(j * 256, (j + 1) * 256)
            t = mm(low_grad, buf_a[:, span]) * hold.gu[:, span].astype(jnp.float32)
            hold.gz[:, span] = t.astype(jnp.bfloat16)
            pump(1)
        du = hold.gz
        load(13, kept[layer].soft, buf_a.at[pl.ds(0, rows), pl.ds(0, 3 * model)])
        need(3)
        turn(hold.n1b)
        take(layer, UP)
        left = turned[...]
        for yy in range(2):
            for target, cc in ((give_b, 1 - c), (up.own, c)):
                for j in range(3):
                    cols = pl.ds(pl.multiple_of((yy * 2 + cc) * 768 + j * 256, 256), 256)
                    block = mm(left, du[:, cols]).astype(jnp.bfloat16)
                    target[:, yy * 768 + j * 256 : yy * 768 + (j + 1) * 256] = block
        push(layer, UP, give_b)
        need(12)
        for j in range(model // 256):
            span = slice(j * 256, (j + 1) * 256)
            dh[:, span] += mm_nt(du[...], buf_b[span, :])
            pump(2)
        load(14, weights[layer][QKV], buf_b.at[:, pl.ds(0, 3 * model)])
        load(15, kept[layer].acts, hold.acts)
        need(4)
        norm_back(hold.xh1, 0)
        need(9)
        dob_ref = du.at[:, pl.ds(0, model)]
        dn_ref = du.at[:, pl.ds(model, model)]
        dob_ref[...] = mm_nt(drb[...], w_out[...]).astype(jnp.bfloat16)
        need(13, 5, 6, 7, 8)
        grad, state_ref = hold.gu, hold.state
        keep_k, keep_v = hold.xh2, hold.xh1
        den = hold.den[...]
        inv = 1.0 / jnp.maximum(den, 1.0)
        dots = jnp.zeros((rows, 128), jnp.float32)
        for p in range(pairs):
            dob = dob_ref[:, pair_cols(p)].astype(jnp.float32)
            dn_ref[:, pair_cols(p)] = (dob * spread(inv, p)).astype(jnp.bfloat16)
            both = dob * hold.ob[:, pair_cols(p)].astype(jnp.float32)
            first = jnp.sum(jnp.where(low, both, 0.0), axis=1, keepdims=True)
            second = jnp.sum(jnp.where(low, 0.0, both), axis=1, keepdims=True)
            dots = dots + jnp.where(lane_is((rows, 128), 2 * p), first, 0.0)
            dots = dots + jnp.where(lane_is((rows, 128), 2 * p + 1), second, 0.0)
        dden = jnp.where(den > 1.0, -dots * inv, 0.0)
        dd_ref[...] = dden
        dden_low = dden.astype(jnp.bfloat16)
        extras = [None, None]
        for p in range(pairs):
            qp = q_of(p).astype(jnp.float32)
            rhs = jnp.concatenate([dn_ref[:, pair_cols(p)], dden_low], axis=1)
            for kind, angle in enumerate((cf, sf)):
                block = mm_tn((qp * angle).astype(jnp.bfloat16), rhs)
                extras[kind] = pack_state(ex.mine, p, kind, block, extras[kind])
        for kind in range(2):
            store_extra(ex.mine, kind, extras[kind], width)
        ex.scatter()

        if layer == 0:
            norm_total.start()
        turn(hold.ob)
        take(layer, OUT)
        down.given()
        left = turned[...]
        for j in range(model // 256):
            span = slice(j * 256, (j + 1) * 256)
            block = mm(left, drb[:, span]).astype(jnp.bfloat16)
            split_rows(block, out.own, give_a, span)
        push(layer, OUT, give_a)

        def inner(p):
            qp, kp, vp = q_of(p), k_of(p), v_of(p)
            dob, dnp = dob_ref[:, pair_cols(p)], dn_ref[:, pair_cols(p)]
            q_t = qp.astype(jnp.float32).T.astype(jnp.bfloat16)
            dn_t = dnp.astype(jnp.float32).T.astype(jnp.bfloat16)
            dq_parts, dk_parts, dv_parts = [], [], []
            for e in range(2):
                h = 2 * p + e
                mask = low if e == 0 else ~low
                span = slice(e * HD, (e + 1) * HD)
                qh = jnp.where(mask, qp, zero)
                doh = jnp.where(mask, dob, zero)
                scale, shift = inv[:, h : h + 1], dd_ref[:, h : h + 1]

                def tile(at_rows, at_cols):
                    weight = w_ref[at_rows, at_cols]
                    s = (mm_nt(qh[at_rows], kp[at_cols]) * weight).astype(jnp.bfloat16)
                    t = mm_nt(doh[at_rows], vp[at_cols])
                    ds = (t * scale[at_rows] + shift[at_rows]).astype(jnp.bfloat16)
                    g = (ds.astype(jnp.float32) * weight).astype(jnp.bfloat16)
                    return s, g

                above, below, every = slice(0, half), slice(half, rows), slice(0, rows)
                s_top, g_top = tile(above, above)
                s_low, g_low = tile(below, every)
                dq_parts.append(jnp.concatenate([mm(g_top, kp[:half]), mm(g_low, kp)], axis=0))

                def across(flat, top, bottom):
                    whole = mm(flat[span, half:], bottom)
                    first = whole[:, :half] + mm(flat[span, :half], top)
                    return jnp.concatenate([first, whole[:, half:]], axis=1)

                dk_parts.append(across(q_t, g_top, g_low))
                dv_parts.append(across(dn_t, s_top, s_low))
            base = slice(p * 128, (p + 1) * 128)
            dq = jnp.where(low, dq_parts[0], dq_parts[1])
            right = jnp.concatenate([dnp, dd_ref[...].astype(jnp.bfloat16)], axis=1)
            dq += cf * mm_nt(right, unpack_state(state_ref, p, 0, width))
            dq += sf * mm_nt(right, unpack_state(state_ref, p, 1, width))
            slope = hold.slope[:, base].astype(jnp.float32)
            grad[:, base] = (dq * slope).astype(jnp.bfloat16)
            keep_k[:, base] = jnp.concatenate(dk_parts, axis=0).T
            keep_v[:, base] = jnp.concatenate(dv_parts, axis=0).T

        for p in range(pairs):
            inner(p)
            if p == 1:
                ex.across()
            if p == 3:
                ex.gather()
            pump(3)
        ex.finish()
        for p in range(pairs):
            base = p * 128
            dsc, dss = unpack_state(ex.result, p, 0, width), unpack_state(ex.result, p, 1, width)
            right = jnp.concatenate([v_of(p), ones], axis=1)
            dk = keep_k[:, base : base + 128] + ct * mm_nt(right, dsc) + st * mm_nt(right, dss)
            kp = k_of(p)
            dv = ct * mm(kp, dsc[:, :128]) + st * mm(kp, dss[:, :128])
            dv = keep_v[:, base : base + 128] + dv
            slope = hold.slope[:, model + base : model + base + 128].astype(jnp.float32)
            grad[:, model + base : model + base + 128] = (dk * valid * slope).astype(jnp.bfloat16)
            grad[:, 2 * model + base : 2 * model + base + 128] = dv.astype(jnp.bfloat16)
        if layer == 0:
            norm_total.middle()
        need(15)
        turn(hold.acts)
        if layer:
            load_early(layer - 1)
        take(layer, QKV)
        left = turned[...]
        for j in range(3 * model // 256):
            span = slice(j * 256, (j + 1) * 256)
            block = mm(left, grad[:, span]).astype(jnp.bfloat16)
            split_rows(block, qkv.own, hold.gz, span)
        push(layer, QKV, hold.gz)
        up.given()
        out.given()
        need(14)
        for j in range(model // 256):
            span = slice(j * 256, (j + 1) * 256)
            dh[:, span] += mm_nt(grad[:, : 3 * model], buf_b[span, : 3 * model])
            pump(2)
        qkv.given()
        if layer:
            load(10, kept[layer - 1].gz, hold.gz)
            load_late(layer - 1)

    for layer in reversed(range(layers)):
        one_layer(layer)
    for i in range(len(pushed), len(pushed) + 3):
        later_stages(i)
    pump(len(steps))
    square_total.start()
    norm_total.end()
    square_total.middle()
    for red in reds:
        for kind in (QKV, OUT):
            red[kind].swapped.wait_recv()
    square_total.end()
    moves.finish()
    links.finish()


def backward(number, tables, gains, dh, held, dims):
    rows, model = dh.shape
    layers = len(held)
    weights_map, aux, coef = tables
    kept = held[0][1]
    hidden = kept.gz.shape[1]
    width = model + 128
    low, wide = jnp.bfloat16, jnp.float32
    vmem = pl.BlockSpec(memory_space=pltpu.VMEM)
    anywhere = pl.BlockSpec(memory_space=pl.ANY)
    sizes = dims[1:]
    scratch = [pltpu.VMEM((8 * r, 2 * w), low) for r, w in sizes] * 2
    scratch += [pltpu.VMEM((2, 2 * r, w), low) for r, w in sizes]
    scratch += [pltpu.VMEM((2, r, 2 * w), low) for r, w in sizes]
    scratch += [pltpu.VMEM((4, r, w), low) for r, w in sizes]
    scratch += [pltpu.VMEM((3, r, w), low) for r, w in sizes]
    for k in (DOWN, UP):
        scratch.append(pltpu.VMEM((8 * dims[k][0], 2 * dims[k][1]), low))
    scratch += [pltpu.VMEM((model, hidden), low)] * 2
    scratch.append(pltpu.VMEM((model, model), low))
    scratch += [pltpu.VMEM(a.shape, a.dtype) for a in kept[:2] + kept[3:]]
    scratch += [pltpu.VMEM((rows, model), low), pltpu.VMEM((model, rows), low)]
    scratch += [pltpu.VMEM((rows, 128), wide)]
    scratch += exchange_scratch(width, layers)
    halves = [(r, w // 2) for r, w in sizes[:2]]
    scratch += [pltpu.VMEM(s, wide) for s in halves] * layers
    for size in ((4 * layers, model), (8, 128)):
        scratch += [pltpu.VMEM((n,) + size, wide) for n in (2, 3, 7)]
    scratch += [pltpu.SemaphoreType.REGULAR((5,))]
    scratch += [pltpu.SemaphoreType.DMA((layers * 80 + 20,))] * 2
    scratch += [pltpu.SemaphoreType.DMA((layers * 20,))]
    outs = pl.pallas_call(
        functools.partial(backward_kernel, layers, model // 128),
        out_shape=[jax.ShapeDtypeStruct((rows, model), wide)]
        + [jax.ShapeDtypeStruct(s, wide) for s in halves + sizes[2:]] * layers
        + [jax.ShapeDtypeStruct(s, wide) for s in halves] * layers
        + [
            jax.ShapeDtypeStruct((4 * layers, model), wide),
            jax.ShapeDtypeStruct((8, 128), wide),
        ],
        in_specs=[vmem, vmem, vmem, anywhere, vmem]
        + [anywhere] * (16 * layers),
        out_specs=[vmem] * (3 + 6 * layers),
        scratch_shapes=scratch,
        compiler_params=pltpu.CompilerParams(
            collective_id=number, has_side_effects=True, vmem_limit_bytes=63 * 2**20
        ),
        name="backward_layers",
    )(
        coef, weights_map, aux, dh, gains,
        *[a for h in held for a in h[1]],
        *[a for h in held for a in h[0]],
    )
    sums = [outs[1 + 4 * i : 5 + 4 * i] for i in range(layers)]
    gots = [outs[1 + 4 * layers + 2 * i :][:2] for i in range(layers)]
    return outs[0], sums, gots, outs[-2], outs[-1]


def stream_meta(lengths, row_ids):
    seq_count = lengths.shape[0]
    seq_ends = jnp.cumsum(lengths, dtype=jnp.int32)
    seq_starts = seq_ends - lengths
    begun = seq_starts[None, :] <= row_ids[:, None]
    seg_raw = jnp.sum(begun.astype(jnp.int32), axis=1, dtype=jnp.int32) - 1
    seg_start = jnp.max(jnp.where(begun, seq_starts[None, :], 0), axis=1)
    inside = row_ids < seq_ends[seq_count - 1]
    seg_ids = jnp.where(inside, seg_raw, seq_count)
    offsets = jnp.where(inside, row_ids - seg_start, 0).astype(jnp.float32)
    angles = offsets * (0.5 * math.pi / LONGEST)
    return (seg_ids, jnp.cos(angles), jnp.sin(angles), inside.astype(jnp.float32))


def adam_step(weight, first_old, second_old, gradient, factor, step_rate, decay_coef):
    clipped = gradient * factor
    first_new = beta_one * first_old + (1.0 - beta_one) * clipped
    second_new = beta_two * second_old + (1.0 - beta_two) * clipped * clipped
    first_hat = first_new / (1.0 - beta_one**step_fixed)
    second_hat = second_new / (1.0 - beta_two**step_fixed)
    weight_new = weight - step_rate * (
        first_hat / (jnp.sqrt(second_hat) + adam_eps) + decay_coef * weight
    )
    return (weight_new, first_new, second_new)


def other_core(array):
    return lax.ppermute(array, "head", [(0, 1), (1, 0), (2, 3), (3, 2)])


def weight_pieces(w_qkv, w_out, w_up, w_down, norm_params):
    first = lax.axis_index("head") % 2 == 0
    low = [a.astype(jnp.bfloat16) for a in (w_qkv, w_out)]
    halves = [(a[:, : a.shape[1] // 2], a[:, a.shape[1] // 2 :]) for a in low]
    keep = [jnp.where(first, a, b) for a, b in halves]
    give = [jnp.where(first, b, a) for a, b in halves]
    wide = other_core(jnp.concatenate(give, axis=2))
    got = jnp.split(wide, (keep[0].shape[2],), axis=2)
    pieces = [
        jnp.where(first, jnp.concatenate([a, b], axis=2), jnp.concatenate([b, a], axis=2))
        for a, b in zip(keep, got)
    ]
    pieces.append(w_up.astype(jnp.bfloat16))
    pieces.append(w_down.astype(jnp.bfloat16).transpose(0, 2, 1))
    layers, _, part = norm_params.shape
    norm = norm_params.astype(jnp.bfloat16).reshape(layers, part)
    return [jnp.pad(norm, ((0, 16 - layers), (0, 128 - part)))] + pieces


def update_kernel(layers, count, *refs):
    out, norm_out = refs[count : count + 15], refs[count + 15]
    here, sem = refs[count + 16 : 2 * count + 16], refs[2 * count + 16]
    copies = [pltpu.make_async_copy(refs[i], here[i], sem.at[i]) for i in range(count)]
    for copy in copies:
        copy.start()
    sums = [here[4 * i : 4 * i + 4] for i in range(layers)]
    gots = [here[4 * layers + 2 * i :][:2] for i in range(layers)]
    norm_ref, square_ref = here[6 * layers : 6 * layers + 2]
    state = here[6 * layers + 2 :]
    z, x, y, c = place()
    dp, head = z * 2 + x, y * 2 + c
    for copy in copies:
        copy.wait()
    lines = norm_ref[...]
    total = jnp.sum(square_ref[...], axis=1, keepdims=True)
    total = jnp.sum(total, axis=0, keepdims=True)
    own = jnp.sum(lines * lines, axis=1, keepdims=True)
    total = total + jnp.sum(own, axis=0, keepdims=True)
    grad_norm = jnp.sqrt(total)
    factor = clip_limit / jnp.maximum(grad_norm, clip_limit)
    norm_out[...] = jnp.broadcast_to(grad_norm, norm_out.shape)

    def step(kind, layer, span, gradient, rate, decay):
        spot = (layer, span)
        old = [ref[spot] for ref in state[3 * kind : 3 * kind + 3]]
        new = adam_step(*old, gradient, factor, rate, decay)
        for ref, value in zip(out[3 * kind : 3 * kind + 3], new):
            ref[spot] = value

    for layer in range(layers):
        for kind, rate in ((0, rate_matrix), (1, rate_outproj)):
            mine, theirs = sums[layer][kind][...], gots[layer][kind][...]
            half = mine.shape[0]
            step(kind, layer, slice(0, half), jnp.where(c == 0, mine, theirs), rate, decay_rate)
            step(kind, layer, slice(half, 2 * half), jnp.where(c == 0, theirs, mine), rate, decay_rate)
        step(2, layer, slice(None), sums[layer][2][...], rate_matrix, decay_rate)
        step(3, layer, slice(None), sums[layer][3][...].T, rate_matrix, decay_rate)
        line = norm_ref[pl.ds(4 * layer + head, 1), :]
        part = state[12].shape[2]
        own = jnp.zeros((1, part), jnp.float32)
        for i in range(8):
            own = own + jnp.where(dp == i, line[:, i * part : (i + 1) * part], 0.0)
        step(4, layer, slice(None), own, rate_norm, 0.0)


def update(sums, gots, norm_sum, squares, state):
    vmem = pl.BlockSpec(memory_space=pltpu.VMEM)
    inputs = [a for s in sums for a in s] + [a for g in gots for a in g]
    inputs += [norm_sum, squares, *state]
    count = len(inputs)
    return pl.pallas_call(
        functools.partial(update_kernel, len(sums), count),
        out_shape=[jax.ShapeDtypeStruct(a.shape, a.dtype) for a in state]
        + [jax.ShapeDtypeStruct((8, 128), jnp.float32)],
        in_specs=[pl.BlockSpec(memory_space=pl.ANY)] * count,
        out_specs=[vmem] * (len(state) + 1),
        scratch_shapes=[pltpu.VMEM(a.shape, a.dtype) for a in inputs]
        + [pltpu.SemaphoreType.DMA((count,))],
        compiler_params=pltpu.CompilerParams(vmem_limit_bytes=56 * 2**20),
        name="update",
    )(*inputs)


def near_step(inputs, cotangent, lengths, state):
    w_qkv, w_out, w_up, w_down, norm_params = state[::3]
    pieces = weight_pieces(w_qkv, w_out, w_up, w_down, norm_params)
    dims = [p.shape[-2:] for p in pieces]
    hidden, gains, tables, held = forward(0, lengths, inputs, pieces)
    grad = cotangent.astype(jnp.float32)
    grad, sums, gots, norm_sum, squares = backward(1, tables, gains, grad, held, dims)
    *new, norm = update(sums, gots, norm_sum, squares, state)
    return (hidden, grad, norm[0, :1], *new)


def layer_norm(inputs_row, gain_row, shift_row):
    mean_row = jnp.mean(inputs_row, axis=-1, keepdims=True)
    centered = inputs_row - mean_row
    variance = jnp.mean(centered * centered, axis=-1, keepdims=True)
    return centered * lax.rsqrt(variance + norm_eps) * gain_row + shift_row


def gelu_exact(inner_pre):
    return jax.nn.gelu(inner_pre, approximate=False)


def contract_rows(left, right):
    return lax.dot_general(
        left, right, (((0,), (0,)), ((), ())), preferred_element_type=jnp.float32
    )


def contract_cols(left, right):
    return lax.dot_general(
        left, right, (((1,), (1,)), ((), ())), preferred_element_type=jnp.float32
    )


def block_attention(queries, key_rows, value_rows, weights, aux):
    cos, sin, tail = aux[:, 0], aux[:, 1], aux[:, 3]
    raw = jnp.einsum("ihe,jhe->hij", queries, key_rows, preferred_element_type=jnp.float32)
    scores = (raw * weights[None]).astype(jnp.bfloat16)
    num = jnp.einsum("hij,jhe->ihe", scores, value_rows, preferred_element_type=jnp.float32)
    den = jnp.transpose(jnp.sum(scores.astype(jnp.float32), axis=2))
    out = []
    for angle in (cos, sin):
        turned = key_rows.astype(jnp.float32) * (angle * tail)[:, None, None]
        out.append(
            jnp.einsum(
                "jhe,jhf->hef", turned, value_rows.astype(jnp.float32), precision=exact_mode
            )
        )
        out.append(jnp.sum(turned, axis=0))
    return num, den, tuple(out)


def finish_rows(queries, num, den, state, aux):
    cos, sin, follow = aux[:, 0], aux[:, 1], aux[:, 2]
    for angle, kv, ks in ((cos, state[0], state[1]), (sin, state[2], state[3])):
        turned = queries.astype(jnp.float32) * (angle * follow)[:, None, None]
        num = num + jnp.einsum("ihe,hef->ihf", turned, kv, precision=exact_mode)
        den = den + jnp.einsum("ihe,he->ih", turned, ks, precision=exact_mode)
    return num / jnp.maximum(den, 1.0)[:, :, None]


class WidePlan:
    def __init__(self, lengths, rows):
        parts = lax.axis_size("dp") * lax.axis_size("head")
        me = lax.axis_index("dp") * lax.axis_size("head") + lax.axis_index("head")
        seg, cos, sin, valid = stream_meta(
            lengths, me * rows + jnp.arange(rows, dtype=jnp.int32)
        )
        starts = jnp.arange(parts, dtype=jnp.int32) * rows
        before = stream_meta(lengths, starts - 1)[0]
        last = stream_meta(lengths, starts + rows - 1)[0]
        follow = (seg == before[me]).astype(jnp.float32)
        tail = (seg == last[me]).astype(jnp.float32)
        place_ids = jnp.arange(rows)
        allowed = (seg[:, None] == seg[None, :]) & (place_ids[None, :] <= place_ids[:, None])
        close = cos[:, None] * cos[None, :] + sin[:, None] * sin[None, :]
        self.valid = valid
        self.weights = jnp.where(allowed, close, 0.0)
        self.aux = jnp.stack([cos, sin, follow, tail, valid], axis=1)
        devices = jnp.arange(parts)
        self.ahead = ((last == before[me]) & (devices < me)).astype(jnp.float32)
        self.behind = ((before == last[me]) & (devices > me)).astype(jnp.float32)

    def masked(self, state, coef):
        def one(a):
            everything = lax.all_gather(a.astype(jnp.bfloat16), ("dp", "head"))
            return jnp.einsum(
                "d,d...->...",
                coef.astype(jnp.bfloat16),
                everything,
                preferred_element_type=jnp.float32,
            )

        return jax.tree.map(one, state)

    def attend(self, q, k, v):
        rows, model = q.shape
        split = lambda a: a.reshape(rows, HEADS, model // HEADS)
        local = lambda *a: block_attention(*a, self.weights, self.aux)
        (num, den, state), pull = jax.vjp(local, split(q), split(k), split(v))
        state = self.masked(state, self.ahead)
        finish = lambda *a: finish_rows(*a, self.aux)
        out, finish_pull = jax.vjp(finish, split(q), num, den, state)
        return out.astype(jnp.bfloat16).reshape(rows, model), (pull, finish_pull)

    def attend_back(self, kept, dob):
        pull, finish_pull = kept
        rows, model = dob.shape
        grad = dob.astype(jnp.float32).reshape(rows, HEADS, model // HEADS)
        dq_one, dnum, dden, dstate = finish_pull(grad)
        dstate = self.masked(dstate, self.behind)
        dq, dk, dv = pull((dnum, dden, dstate))
        dq = dq.astype(jnp.float32) + dq_one.astype(jnp.float32)
        dk = dk.astype(jnp.float32) * self.valid[:, None, None]
        out = [a.reshape(rows, model).astype(jnp.bfloat16) for a in (dq, dk, dv)]
        return jnp.concatenate(out, axis=1)


def wide_gather(w_qkv, w_out, w_up, w_down, norm_params):
    fulls = []
    for a in (w_qkv, w_out, w_up, w_down):
        part = lax.all_gather(a.astype(jnp.bfloat16), "dp", axis=1, tiled=True)
        fulls.append(lax.all_gather(part, "head", axis=2, tiled=True))
    norm = lax.all_gather(norm_params.astype(jnp.bfloat16), "dp", axis=2, tiled=True)
    return fulls, lax.all_gather(norm, "head", axis=1, tiled=True)


def wide_reduce(grads, norm_grad):
    def one(a):
        part = lax.psum_scatter(a, "head", scatter_dimension=1, tiled=True)
        part = lax.psum_scatter(part.astype(jnp.float32), "dp", scatter_dimension=0, tiled=True)
        return part

    whole = [jnp.stack([one(layer[i]) for layer in grads]) for i in range(len(grads[0]))]
    part = lax.psum_scatter(norm_grad, "head", scatter_dimension=1, tiled=True)
    norm = lax.psum_scatter(part, "dp", scatter_dimension=2, tiled=True)
    squares = sum([jnp.sum(a * a) for a in whole + [norm]])
    return whole, norm, lax.psum(squares, ("dp", "head"))


def wide_step(inputs, cotangent, lengths, state):
    w_qkv, w_out, w_up, w_down, norm_params = state[::3]
    rows, model = inputs.shape
    layers = w_qkv.shape[0]
    plan = WidePlan(lengths, rows)
    fulls, norm_full = wide_gather(w_qkv, w_out, w_up, w_down, norm_params)
    norm_full = norm_full.astype(jnp.float32)
    hidden = inputs.astype(jnp.float32)
    kept = []
    for layer in range(layers):
        qkv_w, out_w, up_w, down_w = (a[layer] for a in fulls)
        gains = norm_full[layer]
        acts = hidden.astype(jnp.bfloat16)
        mixed = jnp.dot(acts, qkv_w, preferred_element_type=jnp.float32)
        soft = jax.nn.softplus(mixed[:, : 2 * model]).astype(jnp.bfloat16)
        q = soft[:, :model]
        k = soft[:, model:] * plan.valid[:, None].astype(jnp.bfloat16)
        v = mixed[:, 2 * model :].astype(jnp.bfloat16)
        attended, attend_kept = plan.attend(q, k, v)
        first_in = hidden + jnp.dot(attended, out_w, preferred_element_type=jnp.float32)
        first_out = layer_norm(first_in, gains[0], gains[1])
        first_low = first_out.astype(jnp.bfloat16)
        inner = jnp.dot(first_low, up_w, preferred_element_type=jnp.float32)
        act = gelu_exact(inner).astype(jnp.bfloat16)
        second_in = first_out + jnp.dot(act, down_w, preferred_element_type=jnp.float32)
        kept.append((acts, mixed, attend_kept, attended, first_in, first_low, inner, act, second_in))
        hidden = layer_norm(second_in, gains[2], gains[3])
    grad_hidden = cotangent.astype(jnp.float32)
    grads = [None] * layers
    norm_grads = [None] * layers
    for layer in reversed(range(layers)):
        acts, mixed, attend_kept, attended, first_in, first_low, inner, act, second_in = kept[layer]
        qkv_w, out_w, up_w, down_w = (a[layer] for a in fulls)
        gains = norm_full[layer]
        _, pull_two = jax.vjp(layer_norm, second_in, gains[2], gains[3])
        grad_second, dgain_two, dshift_two = pull_two(grad_hidden)
        branch_two = grad_second.astype(jnp.bfloat16)
        dw_down = contract_rows(act, branch_two).astype(jnp.bfloat16)
        grad_act = contract_cols(branch_two, down_w)
        _, gelu_pull = jax.vjp(gelu_exact, inner)
        grad_inner = gelu_pull(grad_act)[0].astype(jnp.bfloat16)
        dw_up = contract_rows(first_low, grad_inner).astype(jnp.bfloat16)
        grad_first = grad_second + contract_cols(grad_inner, up_w)
        _, pull_one = jax.vjp(layer_norm, first_in, gains[0], gains[1])
        grad_first_in, dgain_one, dshift_one = pull_one(grad_first)
        branch = grad_first_in.astype(jnp.bfloat16)
        dw_out = contract_rows(attended, branch).astype(jnp.bfloat16)
        dob = contract_cols(branch, out_w).astype(jnp.bfloat16)
        grad_mixed = plan.attend_back(attend_kept, dob)
        slope = jax.nn.sigmoid(mixed[:, : 2 * model])
        grad_soft = (grad_mixed[:, : 2 * model].astype(jnp.float32) * slope).astype(jnp.bfloat16)
        grad_pre = jnp.concatenate([grad_soft, grad_mixed[:, 2 * model :]], axis=1)
        dw_qkv = contract_rows(acts, grad_pre).astype(jnp.bfloat16)
        grad_hidden = grad_first_in + contract_cols(grad_pre, qkv_w)
        grads[layer] = (dw_qkv, dw_out, dw_up, dw_down)
        norm_grads[layer] = jnp.stack([dgain_one, dshift_one, dgain_two, dshift_two])
    whole, norm_sum, squares = wide_reduce(grads, jnp.stack(norm_grads))
    grad_norm = jnp.sqrt(squares)
    factor = clip_limit / jnp.maximum(grad_norm, clip_limit)
    new = []
    rates = (rate_matrix, rate_outproj, rate_matrix, rate_matrix, rate_norm)
    for i, gradient in enumerate(whole + [norm_sum]):
        decay = decay_rate if i < 4 else 0.0
        new += adam_step(*state[3 * i : 3 * i + 3], gradient, factor, rates[i], decay)
    return (hidden, grad_hidden, grad_norm.reshape(1), *new)


def body(inputs, cotangent, lengths, *state):
    near = lax.axis_size("dp") == 8 and lax.axis_size("head") == 4 and inputs.shape[0] == 512
    return (near_step if near else wide_step)(inputs, cotangent, lengths, state)


def solution(mesh):
    rows = P(("dp", "head"), None)
    weight = P(None, "dp", "head")
    norm = P(None, "head", "dp")
    in_specs = (rows, rows, P()) + (weight,) * 12 + (norm,) * 3
    out_specs = (rows, rows, P()) + (weight,) * 12 + (norm,) * 3
    return jax.shard_map(body, mesh=mesh, in_specs=in_specs, out_specs=out_specs, check_vma=False)
```

```python
import functools
import math
from typing import Any, NamedTuple

import jax
import jax.numpy as jnp
from jax import lax
from jax.experimental import pallas as pl
from jax.experimental.pallas import tpu as pltpu
from jax.sharding import PartitionSpec as P

HEADS = 12
LONGEST = 8192
HD = 64

exact_mode = lax.Precision.HIGHEST
beta_one = 0.9
beta_two = 0.999
adam_eps = 1e-08
decay_rate = 0.1
rate_matrix = 0.1
rate_outproj = 0.5
rate_norm = 0.5
clip_limit = 1.0
norm_eps = 1e-05
step_fixed = 10.0

MESH = pl.DeviceIdType.MESH
FIRST_X = (0, 3)
NORM, QKV, OUT, UP, DOWN = range(5)
MATRICES = (QKV, OUT, UP, DOWN)
BY_Z, BY_X, BY_Y, BY_CORE, BY_CORNER, ON_X, ON_Y, ON_CORNER = range(8)
CORE, ONE, TWO, LAST = range(4)


def place():
    dp, hd = lax.axis_index("dp"), lax.axis_index("head")
    return dp // 2, dp % 2, hd // 2, hd % 2


def at(z, x, y, c):
    return (z * 2 + x, y * 2 + c)


def flip(x, y, c, d):
    dx, dy, dc = d // 4, (d // 2) % 2, d % 2
    return 1 - x if dx else x, 1 - y if dy else y, 1 - c if dc else c


def partners():
    z, x, y, c = place()
    out = [at((z + d) % 4, x, y, c) for d in (1, 2, 3)]
    return out + [at(z, *flip(x, y, c, d)) for d in range(1, 8)]


def greet():
    barrier = pltpu.get_barrier_semaphore()
    devices = partners()
    for dev in devices:
        pl.semaphore_signal(barrier, inc=1, device_id=dev, device_id_type=MESH)
    pl.semaphore_wait(barrier, len(devices))


class Links:
    def __init__(self, send_sem, recv_sem):
        self.send_sem, self.recv_sem, self.copies = send_sem, recv_sem, []
        self.left = set()

    def send(self, src, dst, dev):
        k = len(self.copies)
        copy = pltpu.make_async_remote_copy(
            src_ref=src,
            dst_ref=dst,
            send_sem=self.send_sem.at[k],
            recv_sem=self.recv_sem.at[k],
            device_id=dev,
            device_id_type=MESH,
        )
        copy.start()
        self.copies.append(copy)
        self.left.add(k)
        copy.number = k
        return copy

    def sent(self, copy):
        copy.wait_send()
        self.left.discard(copy.number)

    def finish(self):
        for k in sorted(self.left):
            self.copies[k].wait_send()


class Moves:
    def __init__(self, sem):
        self.sem, self.copies = sem, []
        self.left = []

    def start(self, src, dst):
        copy = pltpu.make_async_copy(src, dst, self.sem.at[len(self.copies)])
        copy.start()
        self.copies.append(copy)
        self.left.append(copy)
        return copy

    def wait(self, copy):
        if any(copy is other for other in self.left):
            copy.wait()
        self.left = [other for other in self.left if other is not copy]

    def finish(self):
        for copy in self.left:
            copy.wait()
        self.left = []


def region(kind, rows, cols, z, x, y, c):
    strip, head = z * 2 + x, y * 2 + c
    if kind in (QKV, OUT, NORM):
        first, left = (strip * 2 + c) * rows, y * cols
    elif kind == UP:
        first, left = strip * rows, head * cols
    else:
        first, left = head * rows, strip * cols
    return (
        pl.ds(pl.multiple_of(first, rows), rows),
        pl.ds(pl.multiple_of(left, cols), cols),
    )


def whole_shape(kind, rows, cols):
    if kind in (QKV, OUT, NORM):
        return rows * 16, cols * 2
    if kind == UP:
        return rows * 8, cols * 4
    return rows * 4, cols * 8


class Kept(NamedTuple):
    acts: Any
    slope: Any
    soft: Any
    ob: Any
    den: Any
    state: Any
    xh1: Any
    xh2: Any
    rstd: Any
    n1b: Any
    gz: Any
    gu: Any


class Gather:
    def __init__(self, kind, piece, full, links, moves):
        self.kind, self.piece, self.full = kind, piece, full
        self.links, self.moves = links, moves
        self.z, self.x, self.y, self.c = place()
        self.copies = {}

    def spot(self, zz, xx, yy):
        rows, cols = self.piece.shape
        span = region(self.kind, rows, cols, zz, xx, yy, self.c)
        return self.full.at[span[0], span[1]]

    def origin(self, d):
        return (self.z + 4 - d) % 4 if d else self.z

    def begin(self, d):
        z, x, y, c = self.z, self.x, self.y, self.c
        if d:
            dev = at((z + d) % 4, x, y, c)
            self.copies[BY_Z, d] = self.links.send(self.piece, self.spot(z, x, y), dev)
        else:
            self.own = self.moves.start(self.piece, self.spot(z, x, y))

    def fan(self, d):
        z, x, y, c = self.z, self.x, self.y, self.c
        if d:
            self.copies[BY_Z, d].wait_recv()
        here = self.spot(self.origin(d), x, y)
        src = here if d else self.piece
        self.copies[BY_X, d] = self.links.send(src, here, at(z, 1 - x, y, c))
        self.copies[BY_Y, d] = self.links.send(src, here, at(z, x, 1 - y, c))
        self.copies[BY_CORE, d] = self.links.send(src, here, at(z, x, y, 1 - c))

    def second(self, d):
        z, x, y, c = self.z, self.x, self.y, self.c
        from_x, from_y = self.spot(self.origin(d), 1 - x, y), self.spot(self.origin(d), x, 1 - y)
        self.copies[BY_X, d].wait_recv()
        if d in FIRST_X:
            self.copies[BY_CORNER, d] = self.links.send(from_x, from_x, at(z, x, 1 - y, c))
        self.copies[ON_X, d] = self.links.send(from_x, from_x, at(z, x, y, 1 - c))
        self.copies[BY_Y, d].wait_recv()
        if d not in FIRST_X:
            self.copies[BY_CORNER, d] = self.links.send(from_y, from_y, at(z, 1 - x, y, c))
        self.copies[ON_Y, d] = self.links.send(from_y, from_y, at(z, x, y, 1 - c))

    def third(self, d):
        z, x, y, c = self.z, self.x, self.y, self.c
        block = self.spot(self.origin(d), 1 - x, 1 - y)
        self.copies[BY_CORNER, d].wait_recv()
        self.copies[ON_CORNER, d] = self.links.send(block, block, at(z, x, y, 1 - c))

    def ready(self):
        for key in (BY_CORE, ON_X, ON_Y, ON_CORNER):
            for d in range(4):
                self.copies[key, d].wait_recv()
        self.moves.wait(self.own)


class GatherLate(Gather):
    def strip(self, zz, xx):
        rows, _ = self.piece.shape
        first = ((zz * 2 + xx) * 2 + self.c) * rows
        return self.full.at[pl.ds(pl.multiple_of(first, rows), rows)]

    def fan(self, d):
        if d == 0:
            super().fan(0)

    def second(self, d):
        if d == 0:
            super().second(0)

    def third(self, d):
        z, x, y, c = self.z, self.x, self.y, self.c
        if d == 0:
            super().third(0)
            self.moves.wait(self.own)
            for e in (1, 3, 2):
                for xx in range(2):
                    block, dev = self.strip(z, xx), at((z + e) % 4, x, y, c)
                    self.copies[BY_Z, e, xx] = self.links.send(block, block, dev)

    def fourth(self, d):
        for xx in range(2):
            self.copies[BY_Z, d, xx].wait_recv()
            block, dev = self.strip(self.origin(d), xx), at(self.z, self.x, self.y, 1 - self.c)
            self.copies[BY_CORE, d, xx] = self.links.send(block, block, dev)

    def begin(self, d):
        if d == 0:
            super().begin(0)

    def ready(self):
        for key in (BY_CORE, ON_X, ON_Y, ON_CORNER):
            self.copies[key, 0].wait_recv()
        for d in (1, 2, 3):
            for xx in range(2):
                self.copies[BY_CORE, d, xx].wait_recv()


class Exchange:
    def __init__(self, coef, refs, links, reverse):
        self.coef, self.reverse, self.links = coef, reverse, links
        self.mine, self.got, self.sums, self.got_z, self.back, self.result = refs
        self.z, self.x, self.y, self.c = place()
        self.index = self.x * 4 + self.y * 2 + self.c

    def scatter(self):
        self.got[self.index] = self.mine[self.index]
        self.first = []
        for d in range(1, 8):
            nx, ny, nc = flip(self.x, self.y, self.c, d)
            src = self.mine.at[nx * 4 + ny * 2 + nc]
            dev = at(self.z, nx, ny, nc)
            self.first.append(self.links.send(src, self.got.at[self.index], dev))

    def across(self):
        for copy in self.first:
            copy.wait_recv()
        self.planes = []
        for d in (1, 2, 3):
            total = jnp.zeros(self.got.shape[1:], jnp.float32)
            for j in range(8):
                factor = self.coef[8 + d : 9 + d, j : j + 1]
                total = total + factor * self.got[j].astype(jnp.float32)
            self.sums[d - 1] = total.astype(jnp.bfloat16)
            dev = at((self.z + d) % 4, self.x, self.y, self.c)
            self.planes.append(self.links.send(self.sums.at[d - 1], self.got_z.at[d - 1], dev))

    def gather(self):
        for copy in self.planes:
            copy.wait_recv()
        parts = [self.got[j].astype(jnp.float32) for j in range(8)]
        parts += [self.got_z[d].astype(jnp.float32) for d in range(3)]
        for i in range(8):
            total = jnp.zeros(self.got.shape[1:], jnp.float32)
            span = range(i + 1, 8) if self.reverse else range(i)
            for j in list(span) + [8, 9, 10]:
                total = total + self.coef[i : i + 1, j : j + 1] * parts[j]
            self.back[i] = total.astype(jnp.bfloat16)
        self.result[self.index] = self.back[self.index]
        self.last = []
        for d in range(1, 8):
            nx, ny, nc = flip(self.x, self.y, self.c, d)
            src = self.back.at[nx * 4 + ny * 2 + nc]
            dev = at(self.z, nx, ny, nc)
            self.last.append(self.links.send(src, self.result.at[self.index], dev))

    def finish(self):
        for copy in self.last:
            copy.wait_recv()
        for copy in self.first + self.planes + self.last:
            self.links.sent(copy)


def exchange_scratch(width, layers):
    counts = (8, 3, 8) + (8, 3, 8) * layers
    return [pltpu.VMEM((n, 16, width), jnp.bfloat16) for n in counts]


def exchange_refs(refs, layer):
    mine, sums, back = refs[:3]
    got, got_z, result = refs[3 + 3 * layer : 6 + 3 * layer]
    return mine, got, sums, got_z, back, result


def mm(a, b):
    return lax.dot_general(a, b, (((1,), (0,)), ((), ())), preferred_element_type=jnp.float32)


def mm_nt(a, b):
    return lax.dot_general(a, b, (((1,), (1,)), ((), ())), preferred_element_type=jnp.float32)


def mm_tn(a, b):
    return lax.dot_general(a, b, (((0,), (0,)), ((), ())), preferred_element_type=jnp.float32)


def low_lanes(shape):
    return lax.broadcasted_iota(jnp.int32, shape, len(shape) - 1) < HD


def lane_is(shape, h):
    return lax.broadcasted_iota(jnp.int32, shape, len(shape) - 1) == h


def pair_cols(p):
    return slice(p * 128, (p + 1) * 128)


def pack_state(ref, p, kind, block, extra):
    low = low_lanes((64, 128))
    packed = jnp.where(low, block[:64, :128], block[64:, :128]).astype(jnp.bfloat16)
    for s in range(4):
        ref[kind * 4 + s, :, pair_cols(p)] = packed[s * 16 : (s + 1) * 16]
    if extra is None:
        extra = jnp.zeros((64, 128), jnp.float32)
    extra = extra + jnp.where(lane_is((64, 128), 2 * p), block[:64, 128:], 0.0)
    return extra + jnp.where(lane_is((64, 128), 2 * p + 1), block[64:, 128:], 0.0)


def store_extra(ref, kind, extra, width):
    extra = extra.astype(jnp.bfloat16)
    for s in range(4):
        ref[kind * 4 + s, :, width - 128 :] = extra[s * 16 : (s + 1) * 16]


def unpack_state(ref, p, kind, width):
    packed = jnp.concatenate([ref[kind * 4 + s, :, pair_cols(p)] for s in range(4)], axis=0)
    sums = jnp.concatenate([ref[kind * 4 + s, :, width - 128 :] for s in range(4)], axis=0)
    low = low_lanes((64, 128))
    zero = jnp.zeros((64, 128), jnp.bfloat16)
    top = jnp.concatenate(
        [jnp.where(low, packed, zero), jnp.where(lane_is((64, 128), 2 * p), sums, zero)], axis=1
    )
    bottom = jnp.concatenate(
        [jnp.where(low, zero, packed), jnp.where(lane_is((64, 128), 2 * p + 1), sums, zero)],
        axis=1,
    )
    return jnp.concatenate([top, bottom], axis=0)


def spread(values, p):
    rows = values.shape[0]
    first = jnp.broadcast_to(values[:, 2 * p : 2 * p + 1], (rows, 128))
    second = jnp.broadcast_to(values[:, 2 * p + 1 : 2 * p + 2], (rows, 128))
    return jnp.where(low_lanes((rows, 128)), first, second)


def iota(shape, axis):
    return lax.broadcasted_iota(jnp.int32, shape, axis)


def stream_tables(lengths_ref, w_ref, aux_ref, ahead_ref, behind_ref):
    z, x, y, c = place()
    rows = w_ref.shape[0]
    count = lengths_ref.shape[1]
    me = z * 8 + x * 4 + y * 2 + c
    line, lane = iota((count, count), 0), iota((count, count), 1)
    lens = jnp.broadcast_to(lengths_ref[...].astype(jnp.float32), (count, count))
    total = jnp.sum(lens[:1], axis=1, keepdims=True)
    len_col = jnp.sum(jnp.where(line == lane, lens, 0.0), axis=1, keepdims=True)
    start_col = jnp.sum(jnp.where(lane < line, lens, 0.0), axis=1, keepdims=True)
    start_row = jnp.sum(jnp.where(line < lane, len_col, 0.0), axis=0, keepdims=True)

    def sequence(ids, axis):
        starts = start_row if axis else start_col
        begun = starts <= ids
        raw = jnp.sum(jnp.where(begun, 1.0, 0.0), axis=axis, keepdims=True) - 1.0
        first = jnp.max(jnp.where(begun, starts, 0.0), axis=axis, keepdims=True)
        inside = ids < total
        seg = jnp.where(inside, raw, 1.0 * count)
        angle = jnp.where(inside, ids - first, 0.0) * (0.5 * math.pi / LONGEST)
        return seg, angle, inside

    def ids_of(numbers):
        return numbers.astype(jnp.float32)

    seg_col, angle, inside = sequence(ids_of(me * rows + iota((rows, 1), 0)), 1)
    cos_col, sin_col = jnp.cos(angle), jnp.sin(angle)
    seg_row, angle, _ = sequence(ids_of(me * rows + iota((1, rows), 1)), 0)
    cos_row, sin_row = jnp.cos(angle), jnp.sin(angle)
    before = sequence(ids_of(me * rows - 1 + iota((1, 1), 0)), 1)[0]
    last = sequence(ids_of(me * rows + rows - 1 + iota((1, 1), 0)), 1)[0]
    spot = iota((rows, 128), 1)
    aux = jnp.where(spot == 0, cos_col, jnp.where(spot == 1, sin_col, 0.0))
    aux = aux + jnp.where((spot == 2) & (seg_col == before), 1.0, 0.0)
    aux = aux + jnp.where((spot == 3) & (seg_col == last), 1.0, 0.0)
    aux_ref[...] = aux + jnp.where((spot == 4) & inside, 1.0, 0.0)
    for i in range(0, rows, 128):
        part = slice(i, i + 128)
        close = cos_col[part] * cos_row + sin_col[part] * sin_row
        allowed = (seg_col[part] == seg_row) & (iota((128, rows), 1) <= iota((128, rows), 0) + i)
        w_ref[part, :] = jnp.where(allowed, close, 0.0)

    i, j = iota((8, 128), 0), iota((8, 128), 1)
    lane = iota((1, 128), 1)
    own = lane < 8
    source = (z + 11 - jnp.minimum(lane, 11)) % 4
    others = (lane >= 8) & (lane < 11)
    end = sequence(ids_of((z * 8 + 8) * rows - 1 + iota((1, 1), 0)), 1)[0]
    devices = z * 8 + iota((8, 1), 0)
    before_col = sequence(ids_of(devices * rows - 1), 1)[0]
    last_col = sequence(ids_of(devices * rows + rows - 1), 1)[0]
    at_lanes = jnp.where(own, z * 8 + lane + 1, source * 8 + 8)
    last_row = sequence(ids_of(at_lanes * rows - 1), 0)[0]
    before_row = sequence(ids_of((z * 8 + jnp.minimum(lane, 7)) * rows - 1), 0)[0]
    seen = ((own & (i > j)) | (others & (source < z))) & (before_col == last_row)
    ahead_ref[0:8, :] = jnp.where(seen, 1.0, 0.0)
    seen = own & (j > i) & (last_col == before_row)
    seen = seen | (others & (source > z) & (last_col == end))
    behind_ref[0:8, :] = jnp.where(seen, 1.0, 0.0)
    target = (z + i) % 4
    target_col = (z + iota((8, 1), 0)) % 4
    target_end = sequence(ids_of((target_col * 8 + 8) * rows - 1), 1)[0]
    given = own & (i >= 1) & (i <= 3)
    ahead_ref[8:16, :] = jnp.where(given & (last_row == end), 1.0, 0.0)
    given = given & (target < z) & (before_row == target_end)
    behind_ref[8:16, :] = jnp.where(given, 1.0, 0.0)


def assemble_gains(full, layers):
    spots = lax.broadcasted_iota(jnp.int32, (128, 768), 0)
    lanes = lax.broadcasted_iota(jnp.int32, (128, 768), 1)
    total = jnp.zeros((64, 768), jnp.float32)
    for dp in range(8):
        both = full[dp * 32 : (dp + 1) * 32, :]
        left = jnp.concatenate([both[:, :128], both[:, 128:]], axis=0)
        put = jnp.where((lanes == spots + dp * 96) & (spots < 96), 1.0, 0.0).astype(jnp.bfloat16)
        total = total + mm(left, put)
    return [
        jnp.concatenate([total[head * 16 + i : head * 16 + i + 1] for head in range(4)], axis=0)
        for i in range(layers)
    ]


AHEAD, SECOND, THIRD = 8, 8, 14
FOURTH = 18
PUMP = 4


def forward_kernel(layers, pairs, lengths_ref, x_ref, *refs):
    order = (NORM,) + MATRICES
    pieces = refs[:5]
    h_out, gains_out, w_ref, aux_ref, behind_ref = refs[5:10]
    refs = refs[10:]
    full_out = [(None,) + refs[4 * i : 4 * i + 4] for i in range(layers)]
    refs = refs[4 * layers :]
    saved = [Kept(*refs[12 * i : 12 * i + 12]) for i in range(layers)]
    rest = refs[12 * layers :]
    full = [(rest[0],) + rest[1 + 4 * i : 5 + 4 * i] for i in range(layers)]
    rest = rest[1 + 4 * layers :]
    hold = Kept(*rest[:5], None, *rest[5:11])
    num, n1, h_mid = rest[11:14]
    ex_refs = [exchange_refs(rest[14:], i) for i in range(layers)]
    coef, send_sem, recv_sem, move_sem = rest[-4:]
    rows, model = x_ref.shape
    half = rows // 2
    width = model + 128
    links, moves = Links(send_sem, recv_sem), Moves(move_sem)
    greet()
    norms = Gather(NORM, pieces[NORM], full[0][NORM], links, moves)
    every = [
        [norms]
        + [
            (GatherLate if k == OUT else Gather)(k, pieces[k].at[i], full[i][k], links, moves)
            for k in MATRICES
        ]
        for i in range(layers)
    ]

    steps = []

    done = [0]

    def pump(n):
        while n > 0 and done[0] < len(steps):
            steps[done[0]]()
            done[0] += 1
            n -= 1

    def until(mark):
        pump(mark - done[0])

    chain = [part for parts in every for part in parts[1:]]
    chain.insert(2, norms)
    line = [(part, d) for part in chain for d in (0, 1, 3, 2)]
    marks = {}
    for i in range(-AHEAD, len(line) + FOURTH):
        for stage, lag in ((0, -AHEAD), (1, 0), (2, SECOND), (3, THIRD)):
            if 0 <= i - lag < len(line):
                part, d = line[i - lag]
                stages = (part.begin, part.fan, part.second, part.third)
                steps.append(functools.partial(stages[stage], d))
                marks[id(part)] = len(steps)
        if 0 <= i - FOURTH < len(line):
            part, d = line[i - FOURTH]
            if d and isinstance(part, GatherLate):
                steps.append(functools.partial(part.fourth, d))
                marks[id(part)] = len(steps)

    pump(2 * AHEAD)
    stream_tables(lengths_ref, w_ref, aux_ref, coef, behind_ref)
    cos, sin = aux_ref[:, 0:1], aux_ref[:, 1:2]
    follow, tail, valid = aux_ref[:, 2:3], aux_ref[:, 3:4], aux_ref[:, 4:5]
    soft = hold.soft

    def q_of(p):
        return soft[:, p * 128 : (p + 1) * 128]

    def k_of(p):
        return soft[:, model + p * 128 : model + (p + 1) * 128]

    def v_of(p):
        return soft[:, 2 * model + p * 128 : 2 * model + (p + 1) * 128]

    def one_layer(layer):
        parts, whole, keep = every[layer], full[layer], saved[layer]
        mark = [marks[id(part)] for part in parts]
        h_ref = h_mid if layer else x_ref
        h_next = h_out if layer == layers - 1 else h_mid
        ex = Exchange(coef, ex_refs[layer], links, False)
        hold.acts[...] = h_ref[...].astype(jnp.bfloat16)
        moves.start(hold.acts, keep.acts)
        until(mark[QKV])
        parts[QKV].ready()
        moves.start(whole[QKV], full_out[layer][QKV])
        acts = hold.acts[...]
        for j in range(3 * model // 256):
            span = slice(j * 256, (j + 1) * 256)
            p = mm(acts, whole[QKV][:, span])
            if j * 256 < 2 * model:
                t = jnp.exp(-jnp.abs(p))
                hold.slope[:, span] = (jnp.where(p >= 0, 1.0, t) / (1.0 + t)).astype(jnp.bfloat16)
                p = jnp.maximum(p, 0.0) + jnp.log1p(t)
                if j * 256 >= model:
                    p = p * valid
            soft[:, span] = p.astype(jnp.bfloat16)
            if j % 3 == 2:
                pump(1)
        moves.start(hold.slope, keep.slope)
        moves.start(soft, keep.soft)

        ones = jnp.ones((rows, 128), jnp.bfloat16)
        extras = [None, None]
        for p in range(pairs):
            kp = k_of(p).astype(jnp.float32) * tail
            rhs = jnp.concatenate([v_of(p), ones], axis=1)
            for kind, angle in enumerate((cos, sin)):
                block = mm_tn((kp * angle).astype(jnp.bfloat16), rhs)
                extras[kind] = pack_state(ex.mine, p, kind, block, extras[kind])
        for kind in range(2):
            store_extra(ex.mine, kind, extras[kind], width)
        ex.scatter()
        den_ref = hold.den

        def inner(p):
            kp, vp = k_of(p), v_of(p)
            low = low_lanes((rows, 128))
            zero = jnp.zeros((rows, 128), jnp.bfloat16)
            out = []
            for e in range(2):
                qh = jnp.where(low if e == 0 else ~low, q_of(p), zero)
                mark_head = lane_is((rows, 128), 2 * p + e).astype(jnp.bfloat16)
                rhs = jnp.concatenate([vp, mark_head], axis=1)
                top = mm_nt(qh[:half], kp[:half]) * w_ref[:half, :half]
                bottom = mm_nt(qh[half:], kp) * w_ref[half:, :]
                top, bottom = top.astype(jnp.bfloat16), bottom.astype(jnp.bfloat16)
                out.append(jnp.concatenate([mm(top, rhs[:half]), mm(bottom, rhs)], axis=0))
            num[:, pair_cols(p)] = jnp.where(low, out[0][:, :128], out[1][:, :128])
            dens = out[0][:, 128:] + out[1][:, 128:]
            if p == 0:
                den_ref[...] = dens
            else:
                den_ref[...] += dens

        for p in range(pairs):
            inner(p)
            if p == 1:
                ex.across()
            if p == 3:
                ex.gather()
            pump(PUMP)
        ex.finish()
        moves.start(ex.result, keep.state)
        den = den_ref[...]
        cf, sf = cos * follow, sin * follow
        for p in range(pairs):
            qp = q_of(p)
            extra = cf * mm(qp, unpack_state(ex.result, p, 0, width))
            extra += sf * mm(qp, unpack_state(ex.result, p, 1, width))
            num[:, pair_cols(p)] += extra[:, :128]
            den = den + extra[:, 128:]
        den_ref[...] = den
        moves.start(hold.den, keep.den)
        inv = 1.0 / jnp.maximum(den, 1.0)
        ob = hold.ob
        for p in range(pairs):
            ob[:, pair_cols(p)] = (num[:, pair_cols(p)] * spread(inv, p)).astype(jnp.bfloat16)
        moves.start(hold.ob, keep.ob)
        until(mark[OUT])
        parts[OUT].ready()
        moves.start(whole[OUT], full_out[layer][OUT])

        def norm(x_ref, which, low_ref, whole_ref):
            gain, shift = gains[2 * which], gains[2 * which + 1]
            for i in range(0, rows, 128):
                x = x_ref[i : i + 128, :]
                centered = x - jnp.mean(x, axis=1, keepdims=True)
                variance = jnp.mean(centered * centered, axis=1, keepdims=True)
                r = lax.rsqrt(variance + norm_eps)
                xh = centered * r
                x_ref[i : i + 128, :] = xh
                new = jnp.broadcast_to(r, (128, 128))
                if which:
                    new = jnp.where(low_lanes((128, 128)), hold.rstd[i : i + 128, :], new)
                hold.rstd[i : i + 128, :] = new
                y = xh * gain + shift
                whole_ref[i : i + 128, :] = y
                if low_ref is not None:
                    low_ref[i : i + 128, :] = y.astype(jnp.bfloat16)

        if layer == 0:
            until(mark[NORM])
            norms.ready()
            for i, lines in enumerate(assemble_gains(whole[NORM], layers)):
                gains_out[i, 0:4, :] = lines
                gains_out[i, 4:8, :] = jnp.zeros((4, model), jnp.float32)
        gains = [gains_out[layer, i : i + 1, :] for i in range(4)]
        attended = ob[...]
        for j in range(model // 256):
            span = slice(j * 256, (j + 1) * 256)
            first_in = h_ref[:, span].astype(jnp.float32)
            hold.xh1[:, span] = first_in + mm(attended, whole[OUT][:, span])
        norm(hold.xh1, 0, hold.n1b, n1)
        moves.start(hold.xh1, keep.xh1)
        moves.start(hold.n1b, keep.n1b)
        until(mark[UP])
        parts[UP].ready()
        moves.start(whole[UP], full_out[layer][UP])
        n1b = hold.n1b[...]
        hidden = whole[UP].shape[1]
        for j in range(hidden // 256):
            span = slice(j * 256, (j + 1) * 256)
            u = mm(n1b, whole[UP][:, span])
            phi = 0.5 * (1.0 + lax.erf(u * math.sqrt(0.5)))
            hold.gz[:, span] = (u * phi).astype(jnp.bfloat16)
            bell = jnp.exp(-0.5 * u * u) * (1.0 / math.sqrt(2.0 * math.pi))
            hold.gu[:, span] = (phi + u * bell).astype(jnp.bfloat16)
            pump(1)
        moves.start(hold.gz, keep.gz)
        moves.start(hold.gu, keep.gu)
        until(mark[DOWN])
        parts[DOWN].ready()
        moves.start(whole[DOWN], full_out[layer][DOWN])
        gz = hold.gz[...]
        for j in range(model // 256):
            span = slice(j * 256, (j + 1) * 256)
            hold.xh2[:, span] = n1[:, span] + mm_nt(gz, whole[DOWN][span, :])
        norm(hold.xh2, 1, None, h_next)
        moves.start(hold.xh2, keep.xh2)
        moves.start(hold.rstd, keep.rstd)
        moves.finish()

    for layer in range(layers):
        one_layer(layer)
    links.finish()


def forward(number, lengths, inputs, pieces):
    rows, model = inputs.shape
    layers = pieces[1].shape[0]
    order = (NORM,) + MATRICES
    fulls = [whole_shape(k, *p.shape[-2:]) for k, p in zip(order, pieces)]
    hidden = fulls[UP][1]
    width = model + 128
    low, wide = jnp.bfloat16, jnp.float32
    kept = Kept(
        acts=((rows, model), low),
        slope=((rows, 2 * model), low),
        soft=((rows, 3 * model), low),
        ob=((rows, model), low),
        den=((rows, 128), wide),
        state=((8, 16, width), low),
        xh1=((rows, model), wide),
        xh2=((rows, model), wide),
        rstd=((rows, 128), wide),
        n1b=((rows, model), low),
        gz=((rows, hidden), low),
        gu=((rows, hidden), low),
    )
    vmem = pl.BlockSpec(memory_space=pltpu.VMEM)
    anywhere = pl.BlockSpec(memory_space=pl.ANY)
    scratch = [pltpu.VMEM(s, low) for s in fulls[:1] + fulls[1:] * layers]
    scratch += [pltpu.VMEM(*a) for a in kept[:5] + kept[6:]]
    scratch += [pltpu.VMEM((rows, model), wide)] * 3
    scratch += exchange_scratch(width, layers)
    scratch += [pltpu.VMEM((16, 128), wide)]
    scratch += [pltpu.SemaphoreType.DMA((layers * 141 + 31,))] * 2
    scratch += [pltpu.SemaphoreType.DMA((layers * 22,))]
    outs = pl.pallas_call(
        functools.partial(forward_kernel, layers, model // 128),
        out_shape=[
            jax.ShapeDtypeStruct((rows, model), wide),
            jax.ShapeDtypeStruct((layers, 8, model), wide),
            jax.ShapeDtypeStruct((rows, rows), wide),
            jax.ShapeDtypeStruct((rows, 128), wide),
            jax.ShapeDtypeStruct((16, 128), wide),
        ]
        + [jax.ShapeDtypeStruct(s, low) for s in fulls[1:]] * layers
        + [jax.ShapeDtypeStruct(s, t) for s, t in kept] * layers,
        in_specs=[vmem] * 2 + [anywhere] * 5,
        out_specs=[vmem] * 5 + [anywhere] * (layers * (4 + len(kept))),
        scratch_shapes=scratch,
        compiler_params=pltpu.CompilerParams(
            collective_id=number, has_side_effects=True, vmem_limit_bytes=61 * 2**20
        ),
        name="forward_layers",
    )(lengths.reshape(1, -1), inputs, *pieces)
    h_out, gains, tables, outs = outs[0], outs[1], outs[2:5], outs[5:]
    held = []
    for i in range(layers):
        held.append((outs[4 * i : 4 * i + 4], Kept(*outs[4 * layers + 12 * i :][:12])))
    return h_out, gains, tables, held


class Reduce:
    def __init__(self, own, core_in, one_y, one_x, two, from_z, links):
        self.own, self.core_in, self.links = own, core_in, links
        self.one_y, self.one_x, self.two, self.from_z = one_y, one_x, two, from_z
        self.z, self.x, self.y, self.c = place()
        self.rows, self.cols = two.shape[1], two.shape[2]
        self.copies = {}

    def plane(self, d):
        return (self.z + d) % 4 if d else self.z

    def side(self, yy):
        return pl.ds(pl.multiple_of(yy * self.cols, self.cols), self.cols)

    def strip(self, number, count=1):
        return pl.ds(pl.multiple_of(number * self.rows, self.rows), count * self.rows)

    def both(self, d):
        return self.strip(self.plane(d) * 2, 2)

    def give(self, ref, d):
        span = self.both(d)
        dev = at(self.z, self.x, self.y, 1 - self.c)
        copy = self.links.send(ref.at[span, pl.ds(0, 2 * self.cols)], self.core_in.at[span], dev)
        self.copies[CORE, d] = copy

    def given(self):
        for d in range(4):
            self.links.sent(self.copies[CORE, d])

    def release(self, free_sem):
        z, x, y, c = self.z, self.x, self.y, self.c
        for key, copy in self.copies.items():
            if copy.number in self.links.left:
                self.links.sent(copy)
        near = [at(z, 1 - x, y, c), at(z, x, 1 - y, c), at(z, x, y, 1 - c)]
        for dev in near + [at((z + d) % 4, x, y, c) for d in (1, 2, 3)]:
            pl.semaphore_signal(free_sem, inc=1, device_id=dev, device_id_type=MESH)

    def add(self, span, other):
        here = self.own[span].astype(jnp.float32)
        self.own[span] = (here + other.astype(jnp.float32)).astype(jnp.bfloat16)

    def one(self, d):
        z, x, y, c = self.z, self.x, self.y, self.c
        self.copies[CORE, d].wait_recv()
        self.add((self.both(d), slice(None)), self.core_in[self.both(d), :])
        if d in FIRST_X:
            src = self.own.at[self.both(d), self.side(1 - y)]
            dst, dev = self.one_y.at[FIRST_X.index(d)], at(z, x, 1 - y, c)
        else:
            src = self.own.at[self.strip(self.plane(d) * 2 + 1 - x)]
            dst, dev = self.one_x.at[d - 1], at(z, 1 - x, y, c)
        self.copies[ONE, d] = self.links.send(src, dst, dev)

    def second(self, d):
        z, x, y, c = self.z, self.x, self.y, self.c
        self.copies[ONE, d].wait_recv()
        self.links.sent(self.copies[ONE, d])
        near, far = self.strip(self.plane(d) * 2 + x), self.strip(self.plane(d) * 2 + 1 - x)
        if d in FIRST_X:
            self.add((self.both(d), self.side(y)), self.one_y[FIRST_X.index(d)])
            src, dev = self.own.at[far, self.side(y)], at(z, 1 - x, y, c)
        else:
            self.add((near, slice(None)), self.one_x[d - 1])
            src, dev = self.own.at[near, self.side(1 - y)], at(z, x, 1 - y, c)
        self.copies[TWO, d] = self.links.send(src, self.two.at[d], dev)

    def third(self, d):
        z, x, y, c = self.z, self.x, self.y, self.c
        self.copies[TWO, d].wait_recv()
        near = (self.strip(self.plane(d) * 2 + x), self.side(y))
        self.add(near, self.two[d])
        if d:
            src, dst = self.own.at[near[0], near[1]], self.from_z.at[d - 1]
            self.copies[LAST, d] = self.links.send(src, dst, at(self.plane(d), x, y, c))

    def whole(self):
        value = self.own[self.strip(self.z * 2 + self.x), self.side(self.y)].astype(jnp.float32)
        for d in (1, 2, 3):
            self.copies[LAST, d].wait_recv()
            value = value + self.from_z[d - 1].astype(jnp.float32)
        return value

    def last(self, out_ref, squares, swap=None):
        value = self.whole()
        if swap is None:
            out_ref[...] = value
        else:
            half = self.cols // 2
            give_ref, got_ref = swap
            low, high = value[:, :half], value[:, half:]
            out_ref[...] = jnp.where(self.c == 0, low, high)
            give_ref[...] = jnp.where(self.c == 0, high, low)
            dev = at(self.z, self.x, self.y, 1 - self.c)
            self.swapped = self.links.send(give_ref, got_ref, dev)
        part = jnp.sum((value * value).reshape(self.rows // 8, 8, self.cols), axis=0)
        for j in range(self.cols // 128):
            squares[0] += part[:, j * 128 : (j + 1) * 128]


class ReduceEarly(Reduce):
    def one(self, d):
        self.copies[CORE, d].wait_recv()
        self.add((self.both(d), slice(None)), self.core_in[self.both(d), :])
        if d:
            src, dst = self.own.at[self.both(d)], self.from_z.at[d - 1]
            dev = at(self.plane(d), self.x, self.y, self.c)
            self.copies[LAST, d] = self.links.send(src, dst, dev)

    def second(self, d):
        if d == 0:
            value = self.own[self.both(0), :].astype(jnp.float32)
            for e in (1, 2, 3):
                self.copies[LAST, e].wait_recv()
                value = value + self.from_z[e - 1].astype(jnp.float32)
            self.own[self.both(0), :] = value.astype(jnp.bfloat16)
            src = self.own.at[self.both(0), self.side(1 - self.y)]
            dev = at(self.z, self.x, 1 - self.y, self.c)
            self.copies[ONE, 0] = self.links.send(src, self.one_y.at[0], dev)

    def third(self, d):
        if d == 0:
            self.copies[ONE, 0].wait_recv()
            self.add((self.both(0), self.side(self.y)), self.one_y[0])
            src = self.own.at[self.strip(self.z * 2 + 1 - self.x), self.side(self.y)]
            dev = at(self.z, 1 - self.x, self.y, self.c)
            self.copies[TWO, 0] = self.links.send(src, self.two.at[0], dev)

    def whole(self):
        near = self.own[self.strip(self.z * 2 + self.x), self.side(self.y)]
        self.copies[TWO, 0].wait_recv()
        return near.astype(jnp.float32) + self.two[0].astype(jnp.float32)


def backward_kernel(layers, pairs, coef, w_ref, aux_ref, dh_in, gains_ref, *refs):
    kept = [Kept(*refs[12 * i : 12 * i + 12]) for i in range(layers)]
    refs = refs[12 * layers :]
    weights = [(None,) + refs[4 * i : 4 * i + 4] for i in range(layers)]
    refs = refs[4 * layers :]
    dh = refs[0]
    sums = [(None,) + refs[1 + 4 * i : 5 + 4 * i] for i in range(layers)]
    gots = [refs[1 + 4 * layers + 2 * i :][:2] for i in range(layers)]
    norm_out, square_out = refs[1 + 6 * layers : 3 + 6 * layers]
    rest = refs[3 + 6 * layers :]
    free_sem, send_sem, recv_sem, move_sem = rest[-4:]
    norms, norm_z, norm_plane, squares, square_z, square_plane = rest[-10:-4]
    swaps = [rest[-10 - 2 * (i + 1) : -8 - 2 * (i + 1)] for i in range(layers)]
    links, moves = Links(send_sem, recv_sem), Moves(move_sem)
    reds = [
        [None]
        + [
            (ReduceEarly if k == OUT else Reduce)(*rest[k - 1 : 24 : 4], links) for k in MATRICES
        ]
        for _ in range(layers)
    ]
    give_a, give_b, buf_a, buf_b, w_out = rest[24:29]
    hold = Kept(*rest[29:31], None, *rest[31:40])
    drb, turned, dd_ref = rest[40:43]
    ex_refs = [exchange_refs(rest[43:], i) for i in range(layers)]
    rows, model = dh.shape
    half = rows // 2
    width = model + 128
    hidden = hold.gz.shape[1]
    z, x, y, c = place()
    even = c == 0

    loads = {}

    def load(number, src, dst):
        loads[number] = moves.start(src, dst)

    def need(*numbers):
        for number in numbers:
            moves.wait(loads[number])

    def load_early(layer):
        have = kept[layer]
        load(0, have.xh2, hold.xh2)
        load(1, have.rstd, hold.rstd)
        load(2, weights[layer][DOWN], buf_a)
        load(3, have.n1b, hold.n1b)
        load(4, have.xh1, hold.xh1)
        load(5, have.ob, hold.ob)
        load(6, have.den, hold.den)
        load(7, have.state, hold.state)
        load(8, have.slope, hold.slope)
        load(9, weights[layer][OUT], w_out)

    def load_late(layer):
        load(11, kept[layer].gu, hold.gu)
        load(12, weights[layer][UP], buf_b)

    steps, done, pushed, closed = [], [0], [], {}

    def pump(n):
        while n > 0 and done[0] < len(steps):
            steps[done[0]]()
            done[0] += 1
            n -= 1

    def until(mark):
        pump(mark - done[0])

    def later_stages(i):
        for stage in (1, 2, 3):
            if 0 <= i - stage < len(pushed):
                layer, kind = pushed[i - stage]
                red = reds[layer][kind]
                if stage < 3:
                    for d in (2, 3, 1, 0):
                        steps.append(functools.partial((red.second, red.third)[stage - 1], d))
                else:
                    swap = None
                    if kind in (QKV, OUT):
                        swap = (swaps[layer][kind - 1], gots[layer][kind - 1])
                    steps.append(functools.partial(red.last, sums[layer][kind], squares, swap))
                    if layer:
                        steps.append(functools.partial(red.release, free_sem.at[kind]))
                    closed[layer, kind] = len(steps)

    def take(layer, kind):
        if layer < layers - 1:
            until(closed[layer + 1, kind])

    def credit(layer, kind):
        if layer < layers - 1:
            pl.semaphore_wait(free_sem.at[kind], 6)

    def push(layer, kind, ref):
        red = reds[layer][kind]
        credit(layer, kind)
        for d in (2, 3, 1, 0):
            red.give(ref, d)
        pushed.append((layer, kind))
        for d in (2, 3, 1, 0):
            steps.append(functools.partial(red.one, d))
        later_stages(len(pushed) - 1)

    load(10, kept[layers - 1].gz, hold.gz)
    first_dh = moves.start(dh_in, drb)
    load_early(layers - 1)
    load_late(layers - 1)
    greet()
    squares[...] = jnp.zeros(squares.shape, jnp.float32)
    devices = partners()

    class Total:
        def __init__(self, mine, from_z, from_plane, out):
            self.refs = (mine, from_z, from_plane, out)

        def start(self):
            mine, from_z, _, _ = self.refs
            self.copies = [links.send(mine.at[0], from_z.at[i], devices[i]) for i in range(3)]

        def middle(self):
            mine, from_z, from_plane, _ = self.refs
            total = mine[0]
            for i in range(3):
                self.copies[i].wait_recv()
                total = total + from_z[i]
            mine[1] = total
            self.copies = [
                links.send(mine.at[1], from_plane.at[i], devices[3 + i]) for i in range(7)
            ]

        def end(self):
            mine, _, from_plane, out = self.refs
            total = mine[1]
            for i in range(7):
                self.copies[i].wait_recv()
                total = total + from_plane[i]
            out[...] = total

    norm_total = Total(norms, norm_z, norm_plane, norm_out)
    square_total = Total(squares, square_z, square_plane, square_out)
    moves.wait(first_dh)
    dh[...] = drb[...].astype(jnp.float32)

    cos, sin = aux_ref[:, 0:1], aux_ref[:, 1:2]
    follow, tail, valid = aux_ref[:, 2:3], aux_ref[:, 3:4], aux_ref[:, 4:5]
    low = low_lanes((rows, 128))
    zero = jnp.zeros((rows, 128), jnp.bfloat16)
    ones = jnp.ones((rows, 128), jnp.bfloat16)
    cf, sf = cos * follow, sin * follow
    ct, st = cos * tail, sin * tail

    def turn(ref):
        for i in range(0, model, 256):
            turned[i : i + 256, :] = ref[:, i : i + 256].astype(jnp.float32).T.astype(jnp.bfloat16)

    def choose(first, second):
        return jnp.where(even, first, second), jnp.where(even, second, first)

    def split_rows(block, mine_ref, theirs_ref, span):
        for strip in range(8):
            mine, theirs = choose(
                block[strip * 96 : strip * 96 + 48], block[strip * 96 + 48 : strip * 96 + 96]
            )
            mine_ref[strip * 48 : (strip + 1) * 48, span] = mine
            theirs_ref[strip * 48 : (strip + 1) * 48, span] = theirs

    def q_of(p):
        return buf_a[:rows, p * 128 : (p + 1) * 128]

    def k_of(p):
        return buf_a[:rows, model + p * 128 : model + (p + 1) * 128]

    def v_of(p):
        return buf_a[:rows, 2 * model + p * 128 : 2 * model + (p + 1) * 128]

    def one_layer(layer):
        red = reds[layer]
        down, up, out, qkv = red[DOWN], red[UP], red[OUT], red[QKV]
        ex = Exchange(coef, ex_refs[layer], links, True)

        def norm_back(xh_ref, which):
            gain = gains_ref[layer, 2 * which : 2 * which + 1, :]
            dg = jnp.zeros((8, model), jnp.float32)
            db = jnp.zeros((8, model), jnp.float32)
            for i in range(0, rows, 128):
                dy, xh = dh[i : i + 128, :], xh_ref[i : i + 128, :]
                r = hold.rstd[i : i + 128, which * 64 : which * 64 + 1]
                e = dy * gain
                both = dy * xh
                dx = e - jnp.mean(e, axis=1, keepdims=True)
                dx = r * (dx - xh * jnp.mean(e * xh, axis=1, keepdims=True))
                dg = dg + jnp.sum(both.reshape(16, 8, model), axis=0)
                db = db + jnp.sum(dy.reshape(16, 8, model), axis=0)
                dh[i : i + 128, :] = dx
                drb[i : i + 128, :] = dx.astype(jnp.bfloat16)
                pump(1)
            at_line = 4 * layer + 2 * which
            norms[0, at_line : at_line + 1, :] = jnp.sum(dg, axis=0, keepdims=True)
            norms[0, at_line + 1 : at_line + 2, :] = jnp.sum(db, axis=0, keepdims=True)

        need(0, 1)
        norm_back(hold.xh2, 1)
        turn(drb)
        need(10)
        take(layer, DOWN)
        left = turned[...]
        for strip in range(8):
            block = mm(left, hold.gz[:, strip * 384 : (strip + 1) * 384]).astype(jnp.bfloat16)
            for yy in range(2):
                first = block[yy * 384 : yy * 384 + 192]
                second = block[yy * 384 + 192 : yy * 384 + 384]
                mine, theirs = choose(first, second)
                span = slice(strip * 192, (strip + 1) * 192)
                down.own[span, yy * 384 : (yy + 1) * 384] = mine
                give_a[span, yy * 384 : (yy + 1) * 384] = theirs
            pump(1)
        push(layer, DOWN, give_a)
        need(2, 11)
        low_grad = drb[...]
        for j in range(hidden // 256):
            span = slice(j * 256, (j + 1) * 256)
            t = mm(low_grad, buf_a[:, span]) * hold.gu[:, span].astype(jnp.float32)
            hold.gz[:, span] = t.astype(jnp.bfloat16)
            pump(1)
        du = hold.gz
        load(13, kept[layer].soft, buf_a.at[pl.ds(0, rows), pl.ds(0, 3 * model)])
        need(3)
        turn(hold.n1b)
        take(layer, UP)
        left = turned[...]
        for yy in range(2):
            for target, cc in ((give_b, 1 - c), (up.own, c)):
                for j in range(3):
                    cols = pl.ds(pl.multiple_of((yy * 2 + cc) * 768 + j * 256, 256), 256)
                    block = mm(left, du[:, cols]).astype(jnp.bfloat16)
                    target[:, yy * 768 + j * 256 : yy * 768 + (j + 1) * 256] = block
        push(layer, UP, give_b)
        need(12)
        for j in range(model // 256):
            span = slice(j * 256, (j + 1) * 256)
            dh[:, span] += mm_nt(du[...], buf_b[span, :])
            pump(2)
        load(14, weights[layer][QKV], buf_b.at[:, pl.ds(0, 3 * model)])
        load(15, kept[layer].acts, hold.acts)
        need(4)
        norm_back(hold.xh1, 0)
        need(9)
        dob_ref = du.at[:, pl.ds(0, model)]
        dn_ref = du.at[:, pl.ds(model, model)]
        dob_ref[...] = mm_nt(drb[...], w_out[...]).astype(jnp.bfloat16)
        need(13, 5, 6, 7, 8)
        grad, state_ref = hold.gu, hold.state
        keep_k, keep_v = hold.xh2, hold.xh1
        den = hold.den[...]
        inv = 1.0 / jnp.maximum(den, 1.0)
        dots = jnp.zeros((rows, 128), jnp.float32)
        for p in range(pairs):
            dob = dob_ref[:, pair_cols(p)].astype(jnp.float32)
            dn_ref[:, pair_cols(p)] = (dob * spread(inv, p)).astype(jnp.bfloat16)
            both = dob * hold.ob[:, pair_cols(p)].astype(jnp.float32)
            first = jnp.sum(jnp.where(low, both, 0.0), axis=1, keepdims=True)
            second = jnp.sum(jnp.where(low, 0.0, both), axis=1, keepdims=True)
            dots = dots + jnp.where(lane_is((rows, 128), 2 * p), first, 0.0)
            dots = dots + jnp.where(lane_is((rows, 128), 2 * p + 1), second, 0.0)
        dden = jnp.where(den > 1.0, -dots * inv, 0.0)
        dd_ref[...] = dden
        dden_low = dden.astype(jnp.bfloat16)
        extras = [None, None]
        for p in range(pairs):
            qp = q_of(p).astype(jnp.float32)
            rhs = jnp.concatenate([dn_ref[:, pair_cols(p)], dden_low], axis=1)
            for kind, angle in enumerate((cf, sf)):
                block = mm_tn((qp * angle).astype(jnp.bfloat16), rhs)
                extras[kind] = pack_state(ex.mine, p, kind, block, extras[kind])
        for kind in range(2):
            store_extra(ex.mine, kind, extras[kind], width)
        ex.scatter()

        if layer == 0:
            norm_total.start()
        turn(hold.ob)
        take(layer, OUT)
        down.given()
        left = turned[...]
        for j in range(model // 256):
            span = slice(j * 256, (j + 1) * 256)
            block = mm(left, drb[:, span]).astype(jnp.bfloat16)
            split_rows(block, out.own, give_a, span)
        push(layer, OUT, give_a)

        def inner(p):
            qp, kp, vp = q_of(p), k_of(p), v_of(p)
            dob, dnp = dob_ref[:, pair_cols(p)], dn_ref[:, pair_cols(p)]
            q_t = qp.astype(jnp.float32).T.astype(jnp.bfloat16)
            dn_t = dnp.astype(jnp.float32).T.astype(jnp.bfloat16)
            dq_parts, dk_parts, dv_parts = [], [], []
            for e in range(2):
                h = 2 * p + e
                mask = low if e == 0 else ~low
                span = slice(e * HD, (e + 1) * HD)
                qh = jnp.where(mask, qp, zero)
                doh = jnp.where(mask, dob, zero)
                scale, shift = inv[:, h : h + 1], dd_ref[:, h : h + 1]

                def tile(at_rows, at_cols):
                    weight = w_ref[at_rows, at_cols]
                    s = (mm_nt(qh[at_rows], kp[at_cols]) * weight).astype(jnp.bfloat16)
                    t = mm_nt(doh[at_rows], vp[at_cols])
                    ds = (t * scale[at_rows] + shift[at_rows]).astype(jnp.bfloat16)
                    g = (ds.astype(jnp.float32) * weight).astype(jnp.bfloat16)
                    return s, g

                above, below, every = slice(0, half), slice(half, rows), slice(0, rows)
                s_top, g_top = tile(above, above)
                s_low, g_low = tile(below, every)
                dq_parts.append(jnp.concatenate([mm(g_top, kp[:half]), mm(g_low, kp)], axis=0))

                def across(flat, top, bottom):
                    whole = mm(flat[span, half:], bottom)
                    first = whole[:, :half] + mm(flat[span, :half], top)
                    return jnp.concatenate([first, whole[:, half:]], axis=1)

                dk_parts.append(across(q_t, g_top, g_low))
                dv_parts.append(across(dn_t, s_top, s_low))
            base = slice(p * 128, (p + 1) * 128)
            dq = jnp.where(low, dq_parts[0], dq_parts[1])
            right = jnp.concatenate([dnp, dd_ref[...].astype(jnp.bfloat16)], axis=1)
            dq += cf * mm_nt(right, unpack_state(state_ref, p, 0, width))
            dq += sf * mm_nt(right, unpack_state(state_ref, p, 1, width))
            slope = hold.slope[:, base].astype(jnp.float32)
            grad[:, base] = (dq * slope).astype(jnp.bfloat16)
            keep_k[:, base] = jnp.concatenate(dk_parts, axis=0).T
            keep_v[:, base] = jnp.concatenate(dv_parts, axis=0).T

        for p in range(pairs):
            inner(p)
            if p == 1:
                ex.across()
            if p == 2:
                ex.gather()
            pump(3)
        ex.finish()
        for p in range(pairs):
            base = p * 128
            dsc, dss = unpack_state(ex.result, p, 0, width), unpack_state(ex.result, p, 1, width)
            right = jnp.concatenate([v_of(p), ones], axis=1)
            dk = keep_k[:, base : base + 128] + ct * mm_nt(right, dsc) + st * mm_nt(right, dss)
            kp = k_of(p)
            dv = ct * mm(kp, dsc[:, :128]) + st * mm(kp, dss[:, :128])
            dv = keep_v[:, base : base + 128] + dv
            slope = hold.slope[:, model + base : model + base + 128].astype(jnp.float32)
            grad[:, model + base : model + base + 128] = (dk * valid * slope).astype(jnp.bfloat16)
            grad[:, 2 * model + base : 2 * model + base + 128] = dv.astype(jnp.bfloat16)
        if layer == 0:
            norm_total.middle()
        need(15)
        turn(hold.acts)
        if layer:
            load_early(layer - 1)
        take(layer, QKV)
        left = turned[...]
        for j in range(3 * model // 256):
            span = slice(j * 256, (j + 1) * 256)
            block = mm(left, grad[:, span]).astype(jnp.bfloat16)
            split_rows(block, qkv.own, hold.gz, span)
        push(layer, QKV, hold.gz)
        up.given()
        out.given()
        need(14)
        for j in range(model // 256):
            span = slice(j * 256, (j + 1) * 256)
            dh[:, span] += mm_nt(grad[:, : 3 * model], buf_b[span, : 3 * model])
            pump(2)
        qkv.given()
        if layer:
            load(10, kept[layer - 1].gz, hold.gz)
            load_late(layer - 1)

    for layer in reversed(range(layers)):
        one_layer(layer)
    out, qkv = reds[0][OUT], reds[0][QKV]
    for step, d in (
        (qkv.second, 2), (out.third, 2), (qkv.second, 3), (qkv.third, 2), (out.third, 3),
        (out.third, 1), (qkv.second, 1), (qkv.third, 3), (out.third, 0), (qkv.second, 0),
        (qkv.third, 1), (qkv.third, 0),
    ):
        steps.append(functools.partial(step, d))
    pump(len(steps))
    reds[0][UP].last(sums[0][UP], squares)
    for kind in (OUT, QKV):
        reds[0][kind].last(sums[0][kind], squares, (swaps[0][kind - 1], gots[0][kind - 1]))
    square_total.start()
    norm_total.end()
    square_total.middle()
    for red in reds:
        for kind in (QKV, OUT):
            red[kind].swapped.wait_recv()
    square_total.end()
    moves.finish()
    links.finish()


def backward(number, tables, gains, dh, held, dims):
    rows, model = dh.shape
    layers = len(held)
    weights_map, aux, coef = tables
    kept = held[0][1]
    hidden = kept.gz.shape[1]
    width = model + 128
    low, wide = jnp.bfloat16, jnp.float32
    vmem = pl.BlockSpec(memory_space=pltpu.VMEM)
    anywhere = pl.BlockSpec(memory_space=pl.ANY)
    sizes = dims[1:]
    scratch = [pltpu.VMEM((8 * r, 2 * w), low) for r, w in sizes] * 2
    early = [k == OUT for k in MATRICES]
    scratch += [pltpu.VMEM((1 if e else 2, 2 * r, w), low) for (r, w), e in zip(sizes, early)]
    scratch += [pltpu.VMEM((1 if e else 2, r, 2 * w), low) for (r, w), e in zip(sizes, early)]
    scratch += [pltpu.VMEM((1 if e else 4, r, w), low) for (r, w), e in zip(sizes, early)]
    scratch += [
        pltpu.VMEM((3, 2 * r, 2 * w) if e else (3, r, w), low) for (r, w), e in zip(sizes, early)
    ]
    for k in (DOWN, UP):
        scratch.append(pltpu.VMEM((8 * dims[k][0], 2 * dims[k][1]), low))
    scratch += [pltpu.VMEM((model, hidden), low)] * 2
    scratch.append(pltpu.VMEM((model, model), low))
    scratch += [pltpu.VMEM(a.shape, a.dtype) for a in kept[:2] + kept[3:]]
    scratch += [pltpu.VMEM((rows, model), low), pltpu.VMEM((model, rows), low)]
    scratch += [pltpu.VMEM((rows, 128), wide)]
    scratch += exchange_scratch(width, layers)
    halves = [(r, w // 2) for r, w in sizes[:2]]
    scratch += [pltpu.VMEM(s, wide) for s in halves] * layers
    for size in ((4 * layers, model), (8, 128)):
        scratch += [pltpu.VMEM((n,) + size, wide) for n in (2, 3, 7)]
    scratch += [pltpu.SemaphoreType.REGULAR((5,))]
    scratch += [pltpu.SemaphoreType.DMA((layers * 80 + 20,))] * 2
    scratch += [pltpu.SemaphoreType.DMA((layers * 20,))]
    outs = pl.pallas_call(
        functools.partial(backward_kernel, layers, model // 128),
        out_shape=[jax.ShapeDtypeStruct((rows, model), wide)]
        + [jax.ShapeDtypeStruct(s, wide) for s in halves + sizes[2:]] * layers
        + [jax.ShapeDtypeStruct(s, wide) for s in halves] * layers
        + [
            jax.ShapeDtypeStruct((4 * layers, model), wide),
            jax.ShapeDtypeStruct((8, 128), wide),
        ],
        in_specs=[vmem, vmem, vmem, anywhere, vmem]
        + [anywhere] * (16 * layers),
        out_specs=[vmem] * (3 + 6 * layers),
        scratch_shapes=scratch,
        compiler_params=pltpu.CompilerParams(
            collective_id=number, has_side_effects=True, vmem_limit_bytes=63 * 2**20
        ),
        name="backward_layers",
    )(
        coef, weights_map, aux, dh, gains,
        *[a for h in held for a in h[1]],
        *[a for h in held for a in h[0]],
    )
    sums = [outs[1 + 4 * i : 5 + 4 * i] for i in range(layers)]
    gots = [outs[1 + 4 * layers + 2 * i :][:2] for i in range(layers)]
    return outs[0], sums, gots, outs[-2], outs[-1]


def stream_meta(lengths, row_ids):
    seq_count = lengths.shape[0]
    seq_ends = jnp.cumsum(lengths, dtype=jnp.int32)
    seq_starts = seq_ends - lengths
    begun = seq_starts[None, :] <= row_ids[:, None]
    seg_raw = jnp.sum(begun.astype(jnp.int32), axis=1, dtype=jnp.int32) - 1
    seg_start = jnp.max(jnp.where(begun, seq_starts[None, :], 0), axis=1)
    inside = row_ids < seq_ends[seq_count - 1]
    seg_ids = jnp.where(inside, seg_raw, seq_count)
    offsets = jnp.where(inside, row_ids - seg_start, 0).astype(jnp.float32)
    angles = offsets * (0.5 * math.pi / LONGEST)
    return (seg_ids, jnp.cos(angles), jnp.sin(angles), inside.astype(jnp.float32))


def adam_step(weight, first_old, second_old, gradient, factor, step_rate, decay_coef):
    clipped = gradient * factor
    first_new = beta_one * first_old + (1.0 - beta_one) * clipped
    second_new = beta_two * second_old + (1.0 - beta_two) * clipped * clipped
    first_hat = first_new / (1.0 - beta_one**step_fixed)
    second_hat = second_new / (1.0 - beta_two**step_fixed)
    weight_new = weight - step_rate * (
        first_hat / (jnp.sqrt(second_hat) + adam_eps) + decay_coef * weight
    )
    return (weight_new, first_new, second_new)


def other_core(array):
    return lax.ppermute(array, "head", [(0, 1), (1, 0), (2, 3), (3, 2)])


def weight_pieces(w_qkv, w_out, w_up, w_down, norm_params):
    first = lax.axis_index("head") % 2 == 0
    low = [a.astype(jnp.bfloat16) for a in (w_qkv, w_out)]
    halves = [(a[:, : a.shape[1] // 2], a[:, a.shape[1] // 2 :]) for a in low]
    keep = [jnp.where(first, a, b) for a, b in halves]
    give = [jnp.where(first, b, a) for a, b in halves]
    wide = other_core(jnp.concatenate(give, axis=2))
    got = jnp.split(wide, (keep[0].shape[2],), axis=2)
    pieces = [
        jnp.where(first, jnp.concatenate([a, b], axis=2), jnp.concatenate([b, a], axis=2))
        for a, b in zip(keep, got)
    ]
    pieces.append(w_up.astype(jnp.bfloat16))
    pieces.append(w_down.astype(jnp.bfloat16).transpose(0, 2, 1))
    layers, _, part = norm_params.shape
    norm = norm_params.astype(jnp.bfloat16).reshape(layers, part)
    return [jnp.pad(norm, ((0, 16 - layers), (0, 128 - part)))] + pieces


def update_kernel(layers, count, *refs):
    out, norm_out = refs[count + 2 : count + 17], refs[count + 17]
    here, sem = refs[count + 20 : 2 * count + 20], refs[2 * count + 20]
    kept = refs[2 * count + 21 : 2 * count + 23]
    rows = [pltpu.make_async_copy(refs[count + i], kept[i], sem.at[count + i]) for i in range(2)]
    for copy in rows:
        copy.start()
    copies = [pltpu.make_async_copy(refs[i], here[i], sem.at[i]) for i in range(count)]
    for copy in copies:
        copy.start()
    sums = [here[4 * i : 4 * i + 4] for i in range(layers)]
    gots = [here[4 * layers + 2 * i :][:2] for i in range(layers)]
    norm_ref, square_ref = here[6 * layers : 6 * layers + 2]
    state = here[6 * layers + 2 :]
    z, x, y, c = place()
    dp, head = z * 2 + x, y * 2 + c
    for copy in copies:
        copy.wait()
    for copy in rows:
        copy.wait()
    rows = [
        pltpu.make_async_copy(kept[i], refs[count + 18 + i], sem.at[count + i]) for i in range(2)
    ]
    for copy in rows:
        copy.start()
    lines = norm_ref[...]
    total = jnp.sum(square_ref[...], axis=1, keepdims=True)
    total = jnp.sum(total, axis=0, keepdims=True)
    own = jnp.sum(lines * lines, axis=1, keepdims=True)
    total = total + jnp.sum(own, axis=0, keepdims=True)
    grad_norm = jnp.sqrt(total)
    factor = clip_limit / jnp.maximum(grad_norm, clip_limit)
    norm_out[0] = jnp.sum(grad_norm)

    def step(kind, layer, span, gradient, rate, decay):
        spot = (layer, span)
        old = [ref[spot] for ref in state[3 * kind : 3 * kind + 3]]
        new = adam_step(*old, gradient, factor, rate, decay)
        for ref, value in zip(out[3 * kind : 3 * kind + 3], new):
            ref[spot] = value

    for layer in range(layers):
        for kind, rate in ((0, rate_matrix), (1, rate_outproj)):
            mine, theirs = sums[layer][kind][...], gots[layer][kind][...]
            half = mine.shape[0]
            step(kind, layer, slice(0, half), jnp.where(c == 0, mine, theirs), rate, decay_rate)
            step(kind, layer, slice(half, 2 * half), jnp.where(c == 0, theirs, mine), rate, decay_rate)
        step(2, layer, slice(None), sums[layer][2][...], rate_matrix, decay_rate)
        step(3, layer, slice(None), sums[layer][3][...], rate_matrix, decay_rate)
        line = norm_ref[pl.ds(4 * layer + head, 1), :]
        part = state[12].shape[2]
        own = jnp.zeros((1, part), jnp.float32)
        for i in range(8):
            own = own + jnp.where(dp == i, line[:, i * part : (i + 1) * part], 0.0)
        step(4, layer, slice(None), own, rate_norm, 0.0)
    for copy in rows:
        copy.wait()


def update(sums, gots, norm_sum, squares, state, rows):
    vmem = pl.BlockSpec(memory_space=pltpu.VMEM)
    anywhere = pl.BlockSpec(memory_space=pl.ANY)
    inputs = [a for s in sums for a in s] + [a for g in gots for a in g]
    inputs += [norm_sum, squares, *state]
    count = len(inputs)
    return pl.pallas_call(
        functools.partial(update_kernel, len(sums), count),
        out_shape=[jax.ShapeDtypeStruct(a.shape, a.dtype) for a in state]
        + [jax.ShapeDtypeStruct((1,), jnp.float32)]
        + [jax.ShapeDtypeStruct(a.shape, a.dtype) for a in rows],
        in_specs=[anywhere] * (count + 2),
        out_specs=[vmem] * len(state) + [pl.BlockSpec(memory_space=pltpu.SMEM)] + [anywhere] * 2,
        scratch_shapes=[pltpu.VMEM(a.shape, a.dtype) for a in inputs]
        + [pltpu.SemaphoreType.DMA((count + 2,))]
        + [pltpu.VMEM(a.shape, a.dtype) for a in rows],
        compiler_params=pltpu.CompilerParams(vmem_limit_bytes=56 * 2**20),
        name="update",
    )(*inputs, *rows)


def near_step(inputs, cotangent, lengths, state):
    w_qkv, w_out, w_up, w_down, norm_params = state[::3]
    pieces = weight_pieces(w_qkv, w_out, w_up, w_down, norm_params)
    dims = [p.shape[-2:] for p in pieces]
    hidden, gains, tables, held = forward(0, lengths, inputs, pieces)
    grad, sums, gots, norm_sum, squares = backward(1, tables, gains, cotangent, held, dims)
    turned = [a.transpose(0, 2, 1) if 9 <= i < 12 else a for i, a in enumerate(state)]
    *new, norm, hidden, grad = update(sums, gots, norm_sum, squares, turned, (hidden, grad))
    new = [a.transpose(0, 2, 1) if 9 <= i < 12 else a for i, a in enumerate(new)]
    return (hidden, grad, norm, *new)


def layer_norm(inputs_row, gain_row, shift_row):
    mean_row = jnp.mean(inputs_row, axis=-1, keepdims=True)
    centered = inputs_row - mean_row
    variance = jnp.mean(centered * centered, axis=-1, keepdims=True)
    return centered * lax.rsqrt(variance + norm_eps) * gain_row + shift_row


def gelu_exact(inner_pre):
    return jax.nn.gelu(inner_pre, approximate=False)


def contract_rows(left, right):
    return lax.dot_general(
        left, right, (((0,), (0,)), ((), ())), preferred_element_type=jnp.float32
    )


def contract_cols(left, right):
    return lax.dot_general(
        left, right, (((1,), (1,)), ((), ())), preferred_element_type=jnp.float32
    )


def block_attention(queries, key_rows, value_rows, weights, aux):
    cos, sin, tail = aux[:, 0], aux[:, 1], aux[:, 3]
    raw = jnp.einsum("ihe,jhe->hij", queries, key_rows, preferred_element_type=jnp.float32)
    scores = (raw * weights[None]).astype(jnp.bfloat16)
    num = jnp.einsum("hij,jhe->ihe", scores, value_rows, preferred_element_type=jnp.float32)
    den = jnp.transpose(jnp.sum(scores.astype(jnp.float32), axis=2))
    out = []
    for angle in (cos, sin):
        turned = key_rows.astype(jnp.float32) * (angle * tail)[:, None, None]
        out.append(
            jnp.einsum(
                "jhe,jhf->hef", turned, value_rows.astype(jnp.float32), precision=exact_mode
            )
        )
        out.append(jnp.sum(turned, axis=0))
    return num, den, tuple(out)


def finish_rows(queries, num, den, state, aux):
    cos, sin, follow = aux[:, 0], aux[:, 1], aux[:, 2]
    for angle, kv, ks in ((cos, state[0], state[1]), (sin, state[2], state[3])):
        turned = queries.astype(jnp.float32) * (angle * follow)[:, None, None]
        num = num + jnp.einsum("ihe,hef->ihf", turned, kv, precision=exact_mode)
        den = den + jnp.einsum("ihe,he->ih", turned, ks, precision=exact_mode)
    return num / jnp.maximum(den, 1.0)[:, :, None]


class WidePlan:
    def __init__(self, lengths, rows):
        parts = lax.axis_size("dp") * lax.axis_size("head")
        me = lax.axis_index("dp") * lax.axis_size("head") + lax.axis_index("head")
        seg, cos, sin, valid = stream_meta(
            lengths, me * rows + jnp.arange(rows, dtype=jnp.int32)
        )
        starts = jnp.arange(parts, dtype=jnp.int32) * rows
        before = stream_meta(lengths, starts - 1)[0]
        last = stream_meta(lengths, starts + rows - 1)[0]
        follow = (seg == before[me]).astype(jnp.float32)
        tail = (seg == last[me]).astype(jnp.float32)
        place_ids = jnp.arange(rows)
        allowed = (seg[:, None] == seg[None, :]) & (place_ids[None, :] <= place_ids[:, None])
        close = cos[:, None] * cos[None, :] + sin[:, None] * sin[None, :]
        self.valid = valid
        self.weights = jnp.where(allowed, close, 0.0)
        self.aux = jnp.stack([cos, sin, follow, tail, valid], axis=1)
        devices = jnp.arange(parts)
        self.ahead = ((last == before[me]) & (devices < me)).astype(jnp.float32)
        self.behind = ((before == last[me]) & (devices > me)).astype(jnp.float32)

    def masked(self, state, coef):
        def one(a):
            everything = lax.all_gather(a.astype(jnp.bfloat16), ("dp", "head"))
            return jnp.einsum(
                "d,d...->...",
                coef.astype(jnp.bfloat16),
                everything,
                preferred_element_type=jnp.float32,
            )

        return jax.tree.map(one, state)

    def attend(self, q, k, v):
        rows, model = q.shape
        split = lambda a: a.reshape(rows, HEADS, model // HEADS)
        local = lambda *a: block_attention(*a, self.weights, self.aux)
        (num, den, state), pull = jax.vjp(local, split(q), split(k), split(v))
        state = self.masked(state, self.ahead)
        finish = lambda *a: finish_rows(*a, self.aux)
        out, finish_pull = jax.vjp(finish, split(q), num, den, state)
        return out.astype(jnp.bfloat16).reshape(rows, model), (pull, finish_pull)

    def attend_back(self, kept, dob):
        pull, finish_pull = kept
        rows, model = dob.shape
        grad = dob.astype(jnp.float32).reshape(rows, HEADS, model // HEADS)
        dq_one, dnum, dden, dstate = finish_pull(grad)
        dstate = self.masked(dstate, self.behind)
        dq, dk, dv = pull((dnum, dden, dstate))
        dq = dq.astype(jnp.float32) + dq_one.astype(jnp.float32)
        dk = dk.astype(jnp.float32) * self.valid[:, None, None]
        out = [a.reshape(rows, model).astype(jnp.bfloat16) for a in (dq, dk, dv)]
        return jnp.concatenate(out, axis=1)


def wide_gather(w_qkv, w_out, w_up, w_down, norm_params):
    fulls = []
    for a in (w_qkv, w_out, w_up, w_down):
        part = lax.all_gather(a.astype(jnp.bfloat16), "dp", axis=1, tiled=True)
        fulls.append(lax.all_gather(part, "head", axis=2, tiled=True))
    norm = lax.all_gather(norm_params.astype(jnp.bfloat16), "dp", axis=2, tiled=True)
    return fulls, lax.all_gather(norm, "head", axis=1, tiled=True)


def wide_reduce(grads, norm_grad):
    def one(a):
        part = lax.psum_scatter(a, "head", scatter_dimension=1, tiled=True)
        part = lax.psum_scatter(part.astype(jnp.float32), "dp", scatter_dimension=0, tiled=True)
        return part

    whole = [jnp.stack([one(layer[i]) for layer in grads]) for i in range(len(grads[0]))]
    part = lax.psum_scatter(norm_grad, "head", scatter_dimension=1, tiled=True)
    norm = lax.psum_scatter(part, "dp", scatter_dimension=2, tiled=True)
    squares = sum([jnp.sum(a * a) for a in whole + [norm]])
    return whole, norm, lax.psum(squares, ("dp", "head"))


def wide_step(inputs, cotangent, lengths, state):
    w_qkv, w_out, w_up, w_down, norm_params = state[::3]
    rows, model = inputs.shape
    layers = w_qkv.shape[0]
    plan = WidePlan(lengths, rows)
    fulls, norm_full = wide_gather(w_qkv, w_out, w_up, w_down, norm_params)
    norm_full = norm_full.astype(jnp.float32)
    hidden = inputs.astype(jnp.float32)
    kept = []
    for layer in range(layers):
        qkv_w, out_w, up_w, down_w = (a[layer] for a in fulls)
        gains = norm_full[layer]
        acts = hidden.astype(jnp.bfloat16)
        mixed = jnp.dot(acts, qkv_w, preferred_element_type=jnp.float32)
        soft = jax.nn.softplus(mixed[:, : 2 * model]).astype(jnp.bfloat16)
        q = soft[:, :model]
        k = soft[:, model:] * plan.valid[:, None].astype(jnp.bfloat16)
        v = mixed[:, 2 * model :].astype(jnp.bfloat16)
        attended, attend_kept = plan.attend(q, k, v)
        first_in = hidden + jnp.dot(attended, out_w, preferred_element_type=jnp.float32)
        first_out = layer_norm(first_in, gains[0], gains[1])
        first_low = first_out.astype(jnp.bfloat16)
        inner = jnp.dot(first_low, up_w, preferred_element_type=jnp.float32)
        act = gelu_exact(inner).astype(jnp.bfloat16)
        second_in = first_out + jnp.dot(act, down_w, preferred_element_type=jnp.float32)
        kept.append((acts, mixed, attend_kept, attended, first_in, first_low, inner, act, second_in))
        hidden = layer_norm(second_in, gains[2], gains[3])
    grad_hidden = cotangent.astype(jnp.float32)
    grads = [None] * layers
    norm_grads = [None] * layers
    for layer in reversed(range(layers)):
        acts, mixed, attend_kept, attended, first_in, first_low, inner, act, second_in = kept[layer]
        qkv_w, out_w, up_w, down_w = (a[layer] for a in fulls)
        gains = norm_full[layer]
        _, pull_two = jax.vjp(layer_norm, second_in, gains[2], gains[3])
        grad_second, dgain_two, dshift_two = pull_two(grad_hidden)
        branch_two = grad_second.astype(jnp.bfloat16)
        dw_down = contract_rows(act, branch_two).astype(jnp.bfloat16)
        grad_act = contract_cols(branch_two, down_w)
        _, gelu_pull = jax.vjp(gelu_exact, inner)
        grad_inner = gelu_pull(grad_act)[0].astype(jnp.bfloat16)
        dw_up = contract_rows(first_low, grad_inner).astype(jnp.bfloat16)
        grad_first = grad_second + contract_cols(grad_inner, up_w)
        _, pull_one = jax.vjp(layer_norm, first_in, gains[0], gains[1])
        grad_first_in, dgain_one, dshift_one = pull_one(grad_first)
        branch = grad_first_in.astype(jnp.bfloat16)
        dw_out = contract_rows(attended, branch).astype(jnp.bfloat16)
        dob = contract_cols(branch, out_w).astype(jnp.bfloat16)
        grad_mixed = plan.attend_back(attend_kept, dob)
        slope = jax.nn.sigmoid(mixed[:, : 2 * model])
        grad_soft = (grad_mixed[:, : 2 * model].astype(jnp.float32) * slope).astype(jnp.bfloat16)
        grad_pre = jnp.concatenate([grad_soft, grad_mixed[:, 2 * model :]], axis=1)
        dw_qkv = contract_rows(acts, grad_pre).astype(jnp.bfloat16)
        grad_hidden = grad_first_in + contract_cols(grad_pre, qkv_w)
        grads[layer] = (dw_qkv, dw_out, dw_up, dw_down)
        norm_grads[layer] = jnp.stack([dgain_one, dshift_one, dgain_two, dshift_two])
    whole, norm_sum, squares = wide_reduce(grads, jnp.stack(norm_grads))
    grad_norm = jnp.sqrt(squares)
    factor = clip_limit / jnp.maximum(grad_norm, clip_limit)
    new = []
    rates = (rate_matrix, rate_outproj, rate_matrix, rate_matrix, rate_norm)
    for i, gradient in enumerate(whole + [norm_sum]):
        decay = decay_rate if i < 4 else 0.0
        new += adam_step(*state[3 * i : 3 * i + 3], gradient, factor, rates[i], decay)
    return (hidden, grad_hidden, grad_norm.reshape(1), *new)


def body(inputs, cotangent, lengths, *state):
    near = lax.axis_size("dp") == 8 and lax.axis_size("head") == 4 and inputs.shape[0] == 512
    return (near_step if near else wide_step)(inputs, cotangent, lengths, state)


def solution(mesh):
    rows = P(("dp", "head"), None)
    weight = P(None, "dp", "head")
    norm = P(None, "head", "dp")
    in_specs = (rows, rows, P()) + (weight,) * 12 + (norm,) * 3
    out_specs = (rows, rows, P()) + (weight,) * 12 + (norm,) * 3
    return jax.shard_map(body, mesh=mesh, in_specs=in_specs, out_specs=out_specs, check_vma=False)
```

```python
import functools
import math
from typing import Any, NamedTuple

import jax
import jax.numpy as jnp
from jax import lax
from jax.experimental import pallas as pl
from jax.experimental.pallas import tpu as pltpu
from jax.sharding import PartitionSpec as P

HEADS = 12
LONGEST = 8192
HD = 64

exact_mode = lax.Precision.HIGHEST
beta_one = 0.9
beta_two = 0.999
adam_eps = 1e-08
decay_rate = 0.1
rate_matrix = 0.1
rate_outproj = 0.5
rate_norm = 0.5
clip_limit = 1.0
norm_eps = 1e-05
step_fixed = 10.0

MESH = pl.DeviceIdType.MESH
FIRST_X = (0, 3)
NORM, QKV, OUT, UP, DOWN = range(5)
MATRICES = (QKV, OUT, UP, DOWN)
BY_Z, BY_X, BY_Y, BY_CORE, BY_CORNER, ON_X, ON_Y, ON_CORNER = range(8)
CORE, ONE, TWO, LAST = range(4)


def place():
    dp, hd = lax.axis_index("dp"), lax.axis_index("head")
    return dp // 2, dp % 2, hd // 2, hd % 2


def at(z, x, y, c):
    return (z * 2 + x, y * 2 + c)


def flip(x, y, c, d):
    dx, dy, dc = d // 4, (d // 2) % 2, d % 2
    return 1 - x if dx else x, 1 - y if dy else y, 1 - c if dc else c


def partners():
    z, x, y, c = place()
    out = [at((z + d) % 4, x, y, c) for d in (1, 2, 3)]
    return out + [at(z, *flip(x, y, c, d)) for d in range(1, 8)]


def greet():
    barrier = pltpu.get_barrier_semaphore()
    devices = partners()
    for dev in devices:
        pl.semaphore_signal(barrier, inc=1, device_id=dev, device_id_type=MESH)
    pl.semaphore_wait(barrier, len(devices))


class Links:
    def __init__(self, send_sem, recv_sem):
        self.send_sem, self.recv_sem, self.copies = send_sem, recv_sem, []
        self.left = set()

    def send(self, src, dst, dev):
        k = len(self.copies)
        copy = pltpu.make_async_remote_copy(
            src_ref=src,
            dst_ref=dst,
            send_sem=self.send_sem.at[k],
            recv_sem=self.recv_sem.at[k],
            device_id=dev,
            device_id_type=MESH,
        )
        copy.start()
        self.copies.append(copy)
        self.left.add(k)
        copy.number = k
        return copy

    def sent(self, copy):
        copy.wait_send()
        self.left.discard(copy.number)

    def finish(self):
        for k in sorted(self.left):
            self.copies[k].wait_send()


class Moves:
    def __init__(self, sem):
        self.sem, self.copies = sem, []
        self.left = []

    def start(self, src, dst):
        copy = pltpu.make_async_copy(src, dst, self.sem.at[len(self.copies)])
        copy.start()
        self.copies.append(copy)
        self.left.append(copy)
        return copy

    def wait(self, copy):
        if any(copy is other for other in self.left):
            copy.wait()
        self.left = [other for other in self.left if other is not copy]

    def finish(self):
        for copy in self.left:
            copy.wait()
        self.left = []


def region(kind, rows, cols, z, x, y, c):
    strip, head = z * 2 + x, y * 2 + c
    if kind in (QKV, OUT, NORM):
        first, left = (strip * 2 + c) * rows, y * cols
    elif kind == UP:
        first, left = strip * rows, head * cols
    else:
        first, left = head * rows, strip * cols
    return (
        pl.ds(pl.multiple_of(first, rows), rows),
        pl.ds(pl.multiple_of(left, cols), cols),
    )


def whole_shape(kind, rows, cols):
    if kind in (QKV, OUT, NORM):
        return rows * 16, cols * 2
    if kind == UP:
        return rows * 8, cols * 4
    return rows * 4, cols * 8


class Kept(NamedTuple):
    acts: Any
    slope: Any
    soft: Any
    ob: Any
    den: Any
    state: Any
    xh1: Any
    xh2: Any
    rstd: Any
    n1b: Any
    gz: Any
    gu: Any


class Gather:
    def __init__(self, kind, piece, full, links, moves):
        self.kind, self.piece, self.full = kind, piece, full
        self.links, self.moves = links, moves
        self.z, self.x, self.y, self.c = place()
        self.copies = {}

    def spot(self, zz, xx, yy):
        rows, cols = self.piece.shape
        span = region(self.kind, rows, cols, zz, xx, yy, self.c)
        return self.full.at[span[0], span[1]]

    def origin(self, d):
        return (self.z + 4 - d) % 4 if d else self.z

    def begin(self, d):
        z, x, y, c = self.z, self.x, self.y, self.c
        if d:
            dev = at((z + d) % 4, x, y, c)
            self.copies[BY_Z, d] = self.links.send(self.piece, self.spot(z, x, y), dev)
        else:
            self.own = self.moves.start(self.piece, self.spot(z, x, y))

    def fan(self, d):
        z, x, y, c = self.z, self.x, self.y, self.c
        if d:
            self.copies[BY_Z, d].wait_recv()
        here = self.spot(self.origin(d), x, y)
        src = here if d else self.piece
        self.copies[BY_X, d] = self.links.send(src, here, at(z, 1 - x, y, c))
        self.copies[BY_Y, d] = self.links.send(src, here, at(z, x, 1 - y, c))
        self.copies[BY_CORE, d] = self.links.send(src, here, at(z, x, y, 1 - c))

    def second(self, d):
        z, x, y, c = self.z, self.x, self.y, self.c
        from_x, from_y = self.spot(self.origin(d), 1 - x, y), self.spot(self.origin(d), x, 1 - y)
        self.copies[BY_X, d].wait_recv()
        if d in FIRST_X:
            self.copies[BY_CORNER, d] = self.links.send(from_x, from_x, at(z, x, 1 - y, c))
        self.copies[ON_X, d] = self.links.send(from_x, from_x, at(z, x, y, 1 - c))
        self.copies[BY_Y, d].wait_recv()
        if d not in FIRST_X:
            self.copies[BY_CORNER, d] = self.links.send(from_y, from_y, at(z, 1 - x, y, c))
        self.copies[ON_Y, d] = self.links.send(from_y, from_y, at(z, x, y, 1 - c))

    def third(self, d):
        z, x, y, c = self.z, self.x, self.y, self.c
        block = self.spot(self.origin(d), 1 - x, 1 - y)
        self.copies[BY_CORNER, d].wait_recv()
        self.copies[ON_CORNER, d] = self.links.send(block, block, at(z, x, y, 1 - c))

    def ready(self):
        for key in (BY_CORE, ON_X, ON_Y, ON_CORNER):
            for d in range(4):
                self.copies[key, d].wait_recv()
        self.moves.wait(self.own)


class GatherLate(Gather):
    def strip(self, zz, xx):
        rows, _ = self.piece.shape
        first = ((zz * 2 + xx) * 2 + self.c) * rows
        return self.full.at[pl.ds(pl.multiple_of(first, rows), rows)]

    def fan(self, d):
        if d == 0:
            super().fan(0)

    def second(self, d):
        if d == 0:
            super().second(0)

    def third(self, d):
        z, x, y, c = self.z, self.x, self.y, self.c
        if d == 0:
            super().third(0)
            self.moves.wait(self.own)
            for e in (1, 3, 2):
                for xx in range(2):
                    block, dev = self.strip(z, xx), at((z + e) % 4, x, y, c)
                    self.copies[BY_Z, e, xx] = self.links.send(block, block, dev)

    def fourth(self, d):
        for xx in range(2):
            self.copies[BY_Z, d, xx].wait_recv()
            block, dev = self.strip(self.origin(d), xx), at(self.z, self.x, self.y, 1 - self.c)
            self.copies[BY_CORE, d, xx] = self.links.send(block, block, dev)

    def begin(self, d):
        if d == 0:
            super().begin(0)

    def ready(self):
        for key in (BY_CORE, ON_X, ON_Y, ON_CORNER):
            self.copies[key, 0].wait_recv()
        for d in (1, 2, 3):
            for xx in range(2):
                self.copies[BY_CORE, d, xx].wait_recv()


class Exchange:
    def __init__(self, coef, refs, links, reverse):
        self.coef, self.reverse, self.links = coef, reverse, links
        self.mine, self.got, self.sums, self.got_z, self.back, self.result = refs
        self.z, self.x, self.y, self.c = place()
        self.index = self.x * 4 + self.y * 2 + self.c

    def scatter(self):
        self.got[self.index] = self.mine[self.index]
        self.first = []
        for d in range(1, 8):
            nx, ny, nc = flip(self.x, self.y, self.c, d)
            src = self.mine.at[nx * 4 + ny * 2 + nc]
            dev = at(self.z, nx, ny, nc)
            self.first.append(self.links.send(src, self.got.at[self.index], dev))

    def across(self):
        for copy in self.first:
            copy.wait_recv()
        self.planes = []
        for d in (1, 2, 3):
            total = jnp.zeros(self.got.shape[1:], jnp.float32)
            for j in range(8):
                factor = self.coef[8 + d : 9 + d, j : j + 1]
                total = total + factor * self.got[j].astype(jnp.float32)
            self.sums[d - 1] = total.astype(jnp.bfloat16)
            dev = at((self.z + d) % 4, self.x, self.y, self.c)
            self.planes.append(self.links.send(self.sums.at[d - 1], self.got_z.at[d - 1], dev))

    def gather(self):
        for copy in self.planes:
            copy.wait_recv()
        parts = [self.got[j].astype(jnp.float32) for j in range(8)]
        parts += [self.got_z[d].astype(jnp.float32) for d in range(3)]
        for i in range(8):
            total = jnp.zeros(self.got.shape[1:], jnp.float32)
            span = range(i + 1, 8) if self.reverse else range(i)
            for j in list(span) + [8, 9, 10]:
                total = total + self.coef[i : i + 1, j : j + 1] * parts[j]
            self.back[i] = total.astype(jnp.bfloat16)
        self.result[self.index] = self.back[self.index]
        self.last = []
        for d in range(1, 8):
            nx, ny, nc = flip(self.x, self.y, self.c, d)
            src = self.back.at[nx * 4 + ny * 2 + nc]
            dev = at(self.z, nx, ny, nc)
            self.last.append(self.links.send(src, self.result.at[self.index], dev))

    def finish(self):
        for copy in self.last:
            copy.wait_recv()
        for copy in self.first + self.planes + self.last:
            self.links.sent(copy)


def exchange_scratch(width, layers):
    counts = (8, 3, 8) + (8, 3, 8) * layers
    return [pltpu.VMEM((n, 16, width), jnp.bfloat16) for n in counts]


def exchange_refs(refs, layer):
    mine, sums, back = refs[:3]
    got, got_z, result = refs[3 + 3 * layer : 6 + 3 * layer]
    return mine, got, sums, got_z, back, result


def mm(a, b):
    return lax.dot_general(a, b, (((1,), (0,)), ((), ())), preferred_element_type=jnp.float32)


def mm_nt(a, b):
    return lax.dot_general(a, b, (((1,), (1,)), ((), ())), preferred_element_type=jnp.float32)


def mm_tn(a, b):
    return lax.dot_general(a, b, (((0,), (0,)), ((), ())), preferred_element_type=jnp.float32)


def low_lanes(shape):
    return lax.broadcasted_iota(jnp.int32, shape, len(shape) - 1) < HD


def lane_is(shape, h):
    return lax.broadcasted_iota(jnp.int32, shape, len(shape) - 1) == h


def pair_cols(p):
    return slice(p * 128, (p + 1) * 128)


def pack_state(ref, p, kind, block, extra):
    low = low_lanes((64, 128))
    packed = jnp.where(low, block[:64, :128], block[64:, :128]).astype(jnp.bfloat16)
    for s in range(4):
        ref[kind * 4 + s, :, pair_cols(p)] = packed[s * 16 : (s + 1) * 16]
    if extra is None:
        extra = jnp.zeros((64, 128), jnp.float32)
    extra = extra + jnp.where(lane_is((64, 128), 2 * p), block[:64, 128:], 0.0)
    return extra + jnp.where(lane_is((64, 128), 2 * p + 1), block[64:, 128:], 0.0)


def store_extra(ref, kind, extra, width):
    extra = extra.astype(jnp.bfloat16)
    for s in range(4):
        ref[kind * 4 + s, :, width - 128 :] = extra[s * 16 : (s + 1) * 16]


def unpack_state(ref, p, kind, width):
    packed = jnp.concatenate([ref[kind * 4 + s, :, pair_cols(p)] for s in range(4)], axis=0)
    sums = jnp.concatenate([ref[kind * 4 + s, :, width - 128 :] for s in range(4)], axis=0)
    low = low_lanes((64, 128))
    zero = jnp.zeros((64, 128), jnp.bfloat16)
    top = jnp.concatenate(
        [jnp.where(low, packed, zero), jnp.where(lane_is((64, 128), 2 * p), sums, zero)], axis=1
    )
    bottom = jnp.concatenate(
        [jnp.where(low, zero, packed), jnp.where(lane_is((64, 128), 2 * p + 1), sums, zero)],
        axis=1,
    )
    return jnp.concatenate([top, bottom], axis=0)


def spread(values, p):
    rows = values.shape[0]
    first = jnp.broadcast_to(values[:, 2 * p : 2 * p + 1], (rows, 128))
    second = jnp.broadcast_to(values[:, 2 * p + 1 : 2 * p + 2], (rows, 128))
    return jnp.where(low_lanes((rows, 128)), first, second)


def iota(shape, axis):
    return lax.broadcasted_iota(jnp.int32, shape, axis)


def stream_tables(lengths_ref, w_ref, aux_ref, ahead_ref, behind_ref):
    z, x, y, c = place()
    rows = w_ref.shape[0]
    count = lengths_ref.shape[1]
    me = z * 8 + x * 4 + y * 2 + c
    line, lane = iota((count, count), 0), iota((count, count), 1)
    lens = jnp.broadcast_to(lengths_ref[...].astype(jnp.float32), (count, count))
    total = jnp.sum(lens[:1], axis=1, keepdims=True)
    len_col = jnp.sum(jnp.where(line == lane, lens, 0.0), axis=1, keepdims=True)
    start_col = jnp.sum(jnp.where(lane < line, lens, 0.0), axis=1, keepdims=True)
    start_row = jnp.sum(jnp.where(line < lane, len_col, 0.0), axis=0, keepdims=True)

    def sequence(ids, axis):
        starts = start_row if axis else start_col
        begun = starts <= ids
        raw = jnp.sum(jnp.where(begun, 1.0, 0.0), axis=axis, keepdims=True) - 1.0
        first = jnp.max(jnp.where(begun, starts, 0.0), axis=axis, keepdims=True)
        inside = ids < total
        seg = jnp.where(inside, raw, 1.0 * count)
        angle = jnp.where(inside, ids - first, 0.0) * (0.5 * math.pi / LONGEST)
        return seg, angle, inside

    def ids_of(numbers):
        return numbers.astype(jnp.float32)

    seg_col, angle, inside = sequence(ids_of(me * rows + iota((rows, 1), 0)), 1)
    cos_col, sin_col = jnp.cos(angle), jnp.sin(angle)
    seg_row, angle, _ = sequence(ids_of(me * rows + iota((1, rows), 1)), 0)
    cos_row, sin_row = jnp.cos(angle), jnp.sin(angle)
    before = sequence(ids_of(me * rows - 1 + iota((1, 1), 0)), 1)[0]
    last = sequence(ids_of(me * rows + rows - 1 + iota((1, 1), 0)), 1)[0]
    spot = iota((rows, 128), 1)
    aux = jnp.where(spot == 0, cos_col, jnp.where(spot == 1, sin_col, 0.0))
    aux = aux + jnp.where((spot == 2) & (seg_col == before), 1.0, 0.0)
    aux = aux + jnp.where((spot == 3) & (seg_col == last), 1.0, 0.0)
    aux_ref[...] = aux + jnp.where((spot == 4) & inside, 1.0, 0.0)
    for i in range(0, rows, 128):
        part = slice(i, i + 128)
        close = cos_col[part] * cos_row + sin_col[part] * sin_row
        allowed = (seg_col[part] == seg_row) & (iota((128, rows), 1) <= iota((128, rows), 0) + i)
        w_ref[part, :] = jnp.where(allowed, close, 0.0)

    i, j = iota((8, 128), 0), iota((8, 128), 1)
    lane = iota((1, 128), 1)
    own = lane < 8
    source = (z + 11 - jnp.minimum(lane, 11)) % 4
    others = (lane >= 8) & (lane < 11)
    end = sequence(ids_of((z * 8 + 8) * rows - 1 + iota((1, 1), 0)), 1)[0]
    devices = z * 8 + iota((8, 1), 0)
    before_col = sequence(ids_of(devices * rows - 1), 1)[0]
    last_col = sequence(ids_of(devices * rows + rows - 1), 1)[0]
    at_lanes = jnp.where(own, z * 8 + lane + 1, source * 8 + 8)
    last_row = sequence(ids_of(at_lanes * rows - 1), 0)[0]
    before_row = sequence(ids_of((z * 8 + jnp.minimum(lane, 7)) * rows - 1), 0)[0]
    seen = ((own & (i > j)) | (others & (source < z))) & (before_col == last_row)
    ahead_ref[0:8, :] = jnp.where(seen, 1.0, 0.0)
    seen = own & (j > i) & (last_col == before_row)
    seen = seen | (others & (source > z) & (last_col == end))
    behind_ref[0:8, :] = jnp.where(seen, 1.0, 0.0)
    target = (z + i) % 4
    target_col = (z + iota((8, 1), 0)) % 4
    target_end = sequence(ids_of((target_col * 8 + 8) * rows - 1), 1)[0]
    given = own & (i >= 1) & (i <= 3)
    ahead_ref[8:16, :] = jnp.where(given & (last_row == end), 1.0, 0.0)
    given = given & (target < z) & (before_row == target_end)
    behind_ref[8:16, :] = jnp.where(given, 1.0, 0.0)


def assemble_gains(full, layers):
    spots = lax.broadcasted_iota(jnp.int32, (128, 768), 0)
    lanes = lax.broadcasted_iota(jnp.int32, (128, 768), 1)
    total = jnp.zeros((64, 768), jnp.float32)
    for dp in range(8):
        both = full[dp * 32 : (dp + 1) * 32, :]
        left = jnp.concatenate([both[:, :128], both[:, 128:]], axis=0)
        put = jnp.where((lanes == spots + dp * 96) & (spots < 96), 1.0, 0.0).astype(jnp.bfloat16)
        total = total + mm(left, put)
    return [
        jnp.concatenate([total[head * 16 + i : head * 16 + i + 1] for head in range(4)], axis=0)
        for i in range(layers)
    ]


AHEAD, SECOND, THIRD = 8, 8, 14
FOURTH = 18
PUMP = 4


def forward_kernel(layers, pairs, lengths_ref, x_ref, *refs):
    order = (NORM,) + MATRICES
    pieces = refs[:5]
    h_out, gains_out, w_ref, aux_ref, behind_ref = refs[5:10]
    refs = refs[10:]
    full_out = [(None,) + refs[4 * i : 4 * i + 4] for i in range(layers)]
    refs = refs[4 * layers :]
    saved = [Kept(*refs[12 * i : 12 * i + 12]) for i in range(layers)]
    rest = refs[12 * layers :]
    full = [(rest[0],) + rest[1 + 4 * i : 5 + 4 * i] for i in range(layers)]
    rest = rest[1 + 4 * layers :]
    hold = Kept(*rest[:5], None, *rest[5:11])
    num, n1, h_mid = rest[11:14]
    ex_refs = [exchange_refs(rest[14:], i) for i in range(layers)]
    coef, send_sem, recv_sem, move_sem = rest[-4:]
    rows, model = x_ref.shape
    half = rows // 2
    width = model + 128
    links, moves = Links(send_sem, recv_sem), Moves(move_sem)
    greet()
    norms = Gather(NORM, pieces[NORM], full[0][NORM], links, moves)
    every = [
        [norms]
        + [
            (GatherLate if k == OUT else Gather)(k, pieces[k].at[i], full[i][k], links, moves)
            for k in MATRICES
        ]
        for i in range(layers)
    ]

    steps = []

    done = [0]

    def pump(n):
        while n > 0 and done[0] < len(steps):
            steps[done[0]]()
            done[0] += 1
            n -= 1

    def until(mark):
        pump(mark - done[0])

    chain = [part for parts in every for part in parts[1:]]
    chain.insert(2, norms)
    line = [(part, d) for part in chain for d in (0, 1, 3, 2)]
    marks = {}
    for i in range(-AHEAD, len(line) + FOURTH):
        for stage, lag in ((0, -AHEAD), (1, 0), (2, SECOND), (3, THIRD)):
            if 0 <= i - lag < len(line):
                part, d = line[i - lag]
                stages = (part.begin, part.fan, part.second, part.third)
                steps.append(functools.partial(stages[stage], d))
                marks[id(part)] = len(steps)
        if 0 <= i - FOURTH < len(line):
            part, d = line[i - FOURTH]
            if d and isinstance(part, GatherLate):
                steps.append(functools.partial(part.fourth, d))
                marks[id(part)] = len(steps)

    pump(2 * AHEAD)
    stream_tables(lengths_ref, w_ref, aux_ref, coef, behind_ref)
    cos, sin = aux_ref[:, 0:1], aux_ref[:, 1:2]
    follow, tail, valid = aux_ref[:, 2:3], aux_ref[:, 3:4], aux_ref[:, 4:5]
    soft = hold.soft

    def q_of(p):
        return soft[:, p * 128 : (p + 1) * 128]

    def k_of(p):
        return soft[:, model + p * 128 : model + (p + 1) * 128]

    def v_of(p):
        return soft[:, 2 * model + p * 128 : 2 * model + (p + 1) * 128]

    def one_layer(layer):
        parts, whole, keep = every[layer], full[layer], saved[layer]
        mark = [marks[id(part)] for part in parts]
        h_ref = h_mid if layer else x_ref
        h_next = h_out if layer == layers - 1 else h_mid
        ex = Exchange(coef, ex_refs[layer], links, False)
        hold.acts[...] = h_ref[...].astype(jnp.bfloat16)
        moves.start(hold.acts, keep.acts)
        until(mark[QKV])
        parts[QKV].ready()
        moves.start(whole[QKV], full_out[layer][QKV])
        acts = hold.acts[...]
        for j in range(3 * model // 256):
            span = slice(j * 256, (j + 1) * 256)
            p = mm(acts, whole[QKV][:, span])
            if j * 256 < 2 * model:
                t = jnp.exp(-jnp.abs(p))
                hold.slope[:, span] = (jnp.where(p >= 0, 1.0, t) / (1.0 + t)).astype(jnp.bfloat16)
                p = jnp.maximum(p, 0.0) + jnp.log1p(t)
                if j * 256 >= model:
                    p = p * valid
            soft[:, span] = p.astype(jnp.bfloat16)
        moves.start(hold.slope, keep.slope)
        moves.start(soft, keep.soft)

        ones = jnp.ones((rows, 128), jnp.bfloat16)
        extras = [None, None]
        for p in range(pairs):
            kp = k_of(p).astype(jnp.float32) * tail
            rhs = jnp.concatenate([v_of(p), ones], axis=1)
            for kind, angle in enumerate((cos, sin)):
                block = mm_tn((kp * angle).astype(jnp.bfloat16), rhs)
                extras[kind] = pack_state(ex.mine, p, kind, block, extras[kind])
        for kind in range(2):
            store_extra(ex.mine, kind, extras[kind], width)
        ex.scatter()
        den_ref = hold.den

        def inner(p):
            kp, vp = k_of(p), v_of(p)
            low = low_lanes((rows, 128))
            zero = jnp.zeros((rows, 128), jnp.bfloat16)
            out = []
            for e in range(2):
                qh = jnp.where(low if e == 0 else ~low, q_of(p), zero)
                mark_head = lane_is((rows, 128), 2 * p + e).astype(jnp.bfloat16)
                rhs = jnp.concatenate([vp, mark_head], axis=1)
                top = mm_nt(qh[:half], kp[:half]) * w_ref[:half, :half]
                bottom = mm_nt(qh[half:], kp) * w_ref[half:, :]
                top, bottom = top.astype(jnp.bfloat16), bottom.astype(jnp.bfloat16)
                out.append(jnp.concatenate([mm(top, rhs[:half]), mm(bottom, rhs)], axis=0))
            num[:, pair_cols(p)] = jnp.where(low, out[0][:, :128], out[1][:, :128])
            dens = out[0][:, 128:] + out[1][:, 128:]
            if p == 0:
                den_ref[...] = dens
            else:
                den_ref[...] += dens

        for p in range(pairs):
            inner(p)
            if p == 1:
                ex.across()
            if p == 3:
                ex.gather()
            pump(PUMP)
        ex.finish()
        moves.start(ex.result, keep.state)
        den = den_ref[...]
        cf, sf = cos * follow, sin * follow
        for p in range(pairs):
            qp = q_of(p)
            extra = cf * mm(qp, unpack_state(ex.result, p, 0, width))
            extra += sf * mm(qp, unpack_state(ex.result, p, 1, width))
            num[:, pair_cols(p)] += extra[:, :128]
            den = den + extra[:, 128:]
        den_ref[...] = den
        moves.start(hold.den, keep.den)
        inv = 1.0 / jnp.maximum(den, 1.0)
        ob = hold.ob
        for p in range(pairs):
            ob[:, pair_cols(p)] = (num[:, pair_cols(p)] * spread(inv, p)).astype(jnp.bfloat16)
        moves.start(hold.ob, keep.ob)
        until(mark[OUT])
        parts[OUT].ready()
        moves.start(whole[OUT], full_out[layer][OUT])

        def norm(x_ref, which, low_ref, whole_ref):
            gain, shift = gains[2 * which], gains[2 * which + 1]
            for i in range(0, rows, 128):
                x = x_ref[i : i + 128, :]
                centered = x - jnp.mean(x, axis=1, keepdims=True)
                variance = jnp.mean(centered * centered, axis=1, keepdims=True)
                r = lax.rsqrt(variance + norm_eps)
                xh = centered * r
                x_ref[i : i + 128, :] = xh
                new = jnp.broadcast_to(r, (128, 128))
                if which:
                    new = jnp.where(low_lanes((128, 128)), hold.rstd[i : i + 128, :], new)
                hold.rstd[i : i + 128, :] = new
                y = xh * gain + shift
                whole_ref[i : i + 128, :] = y
                if low_ref is not None:
                    low_ref[i : i + 128, :] = y.astype(jnp.bfloat16)

        if layer == 0:
            until(mark[NORM])
            norms.ready()
            for i, lines in enumerate(assemble_gains(whole[NORM], layers)):
                gains_out[i, 0:4, :] = lines
                gains_out[i, 4:8, :] = jnp.zeros((4, model), jnp.float32)
        gains = [gains_out[layer, i : i + 1, :] for i in range(4)]
        attended = ob[...]
        for j in range(model // 256):
            span = slice(j * 256, (j + 1) * 256)
            first_in = h_ref[:, span].astype(jnp.float32)
            hold.xh1[:, span] = first_in + mm(attended, whole[OUT][:, span])
        norm(hold.xh1, 0, hold.n1b, n1)
        moves.start(hold.xh1, keep.xh1)
        moves.start(hold.n1b, keep.n1b)
        until(mark[UP])
        parts[UP].ready()
        moves.start(whole[UP], full_out[layer][UP])
        n1b = hold.n1b[...]
        hidden = whole[UP].shape[1]
        for j in range(hidden // 256):
            span = slice(j * 256, (j + 1) * 256)
            u = mm(n1b, whole[UP][:, span])
            phi = 0.5 * (1.0 + lax.erf(u * math.sqrt(0.5)))
            hold.gz[:, span] = (u * phi).astype(jnp.bfloat16)
            bell = jnp.exp(-0.5 * u * u) * (1.0 / math.sqrt(2.0 * math.pi))
            hold.gu[:, span] = (phi + u * bell).astype(jnp.bfloat16)
            pump(1)
        moves.start(hold.gz, keep.gz)
        moves.start(hold.gu, keep.gu)
        until(mark[DOWN])
        parts[DOWN].ready()
        moves.start(whole[DOWN], full_out[layer][DOWN])
        gz = hold.gz[...]
        for j in range(model // 256):
            span = slice(j * 256, (j + 1) * 256)
            hold.xh2[:, span] = n1[:, span] + mm_nt(gz, whole[DOWN][span, :])
        norm(hold.xh2, 1, None, h_next)
        moves.start(hold.xh2, keep.xh2)
        moves.start(hold.rstd, keep.rstd)
        moves.finish()

    for layer in range(layers):
        one_layer(layer)
    links.finish()


def forward(number, lengths, inputs, pieces):
    rows, model = inputs.shape
    layers = pieces[1].shape[0]
    order = (NORM,) + MATRICES
    fulls = [whole_shape(k, *p.shape[-2:]) for k, p in zip(order, pieces)]
    hidden = fulls[UP][1]
    width = model + 128
    low, wide = jnp.bfloat16, jnp.float32
    kept = Kept(
        acts=((rows, model), low),
        slope=((rows, 2 * model), low),
        soft=((rows, 3 * model), low),
        ob=((rows, model), low),
        den=((rows, 128), wide),
        state=((8, 16, width), low),
        xh1=((rows, model), wide),
        xh2=((rows, model), wide),
        rstd=((rows, 128), wide),
        n1b=((rows, model), low),
        gz=((rows, hidden), low),
        gu=((rows, hidden), low),
    )
    vmem = pl.BlockSpec(memory_space=pltpu.VMEM)
    anywhere = pl.BlockSpec(memory_space=pl.ANY)
    scratch = [pltpu.VMEM(s, low) for s in fulls[:1] + fulls[1:] * layers]
    scratch += [pltpu.VMEM(*a) for a in kept[:5] + kept[6:]]
    scratch += [pltpu.VMEM((rows, model), wide)] * 3
    scratch += exchange_scratch(width, layers)
    scratch += [pltpu.VMEM((16, 128), wide)]
    scratch += [pltpu.SemaphoreType.DMA((layers * 141 + 31,))] * 2
    scratch += [pltpu.SemaphoreType.DMA((layers * 22,))]
    outs = pl.pallas_call(
        functools.partial(forward_kernel, layers, model // 128),
        out_shape=[
            jax.ShapeDtypeStruct((rows, model), wide),
            jax.ShapeDtypeStruct((layers, 8, model), wide),
            jax.ShapeDtypeStruct((rows, rows), wide),
            jax.ShapeDtypeStruct((rows, 128), wide),
            jax.ShapeDtypeStruct((16, 128), wide),
        ]
        + [jax.ShapeDtypeStruct(s, low) for s in fulls[1:]] * layers
        + [jax.ShapeDtypeStruct(s, t) for s, t in kept] * layers,
        in_specs=[vmem] * 2 + [anywhere] * 5,
        out_specs=[vmem] * 5 + [anywhere] * (layers * (4 + len(kept))),
        scratch_shapes=scratch,
        compiler_params=pltpu.CompilerParams(
            collective_id=number, has_side_effects=True, vmem_limit_bytes=61 * 2**20
        ),
        name="forward_layers",
    )(lengths.reshape(1, -1), inputs, *pieces)
    h_out, gains, tables, outs = outs[0], outs[1], outs[2:5], outs[5:]
    held = []
    for i in range(layers):
        held.append((outs[4 * i : 4 * i + 4], Kept(*outs[4 * layers + 12 * i :][:12])))
    return h_out, gains, tables, held


class Reduce:
    def __init__(self, own, core_in, one_y, one_x, two, from_z, links):
        self.own, self.core_in, self.links = own, core_in, links
        self.one_y, self.one_x, self.two, self.from_z = one_y, one_x, two, from_z
        self.z, self.x, self.y, self.c = place()
        self.rows, self.cols = two.shape[1], two.shape[2]
        self.copies = {}

    def plane(self, d):
        return (self.z + d) % 4 if d else self.z

    def side(self, yy):
        return pl.ds(pl.multiple_of(yy * self.cols, self.cols), self.cols)

    def strip(self, number, count=1):
        return pl.ds(pl.multiple_of(number * self.rows, self.rows), count * self.rows)

    def both(self, d):
        return self.strip(self.plane(d) * 2, 2)

    def give(self, ref, d):
        span = self.both(d)
        dev = at(self.z, self.x, self.y, 1 - self.c)
        copy = self.links.send(ref.at[span, pl.ds(0, 2 * self.cols)], self.core_in.at[span], dev)
        self.copies[CORE, d] = copy

    def given(self):
        for d in range(4):
            self.links.sent(self.copies[CORE, d])

    def release(self, free_sem):
        z, x, y, c = self.z, self.x, self.y, self.c
        for key, copy in self.copies.items():
            if copy.number in self.links.left:
                self.links.sent(copy)
        near = [at(z, 1 - x, y, c), at(z, x, 1 - y, c), at(z, x, y, 1 - c)]
        for dev in near + [at((z + d) % 4, x, y, c) for d in (1, 2, 3)]:
            pl.semaphore_signal(free_sem, inc=1, device_id=dev, device_id_type=MESH)

    def add(self, span, other):
        here = self.own[span].astype(jnp.float32)
        self.own[span] = (here + other.astype(jnp.float32)).astype(jnp.bfloat16)

    def one(self, d):
        z, x, y, c = self.z, self.x, self.y, self.c
        self.copies[CORE, d].wait_recv()
        self.add((self.both(d), slice(None)), self.core_in[self.both(d), :])
        if d in FIRST_X:
            src = self.own.at[self.both(d), self.side(1 - y)]
            dst, dev = self.one_y.at[FIRST_X.index(d)], at(z, x, 1 - y, c)
        else:
            src = self.own.at[self.strip(self.plane(d) * 2 + 1 - x)]
            dst, dev = self.one_x.at[d - 1], at(z, 1 - x, y, c)
        self.copies[ONE, d] = self.links.send(src, dst, dev)

    def second(self, d):
        z, x, y, c = self.z, self.x, self.y, self.c
        self.copies[ONE, d].wait_recv()
        self.links.sent(self.copies[ONE, d])
        near, far = self.strip(self.plane(d) * 2 + x), self.strip(self.plane(d) * 2 + 1 - x)
        if d in FIRST_X:
            self.add((self.both(d), self.side(y)), self.one_y[FIRST_X.index(d)])
            src, dev = self.own.at[far, self.side(y)], at(z, 1 - x, y, c)
        else:
            self.add((near, slice(None)), self.one_x[d - 1])
            src, dev = self.own.at[near, self.side(1 - y)], at(z, x, 1 - y, c)
        self.copies[TWO, d] = self.links.send(src, self.two.at[d], dev)

    def third(self, d):
        z, x, y, c = self.z, self.x, self.y, self.c
        self.copies[TWO, d].wait_recv()
        near = (self.strip(self.plane(d) * 2 + x), self.side(y))
        self.add(near, self.two[d])
        if d:
            src, dst = self.own.at[near[0], near[1]], self.from_z.at[d - 1]
            self.copies[LAST, d] = self.links.send(src, dst, at(self.plane(d), x, y, c))

    def whole(self):
        value = self.own[self.strip(self.z * 2 + self.x), self.side(self.y)].astype(jnp.float32)
        for d in (1, 2, 3):
            self.copies[LAST, d].wait_recv()
            value = value + self.from_z[d - 1].astype(jnp.float32)
        return value

    def last(self, out_ref, squares, swap=None):
        value = self.whole()
        if swap is None:
            out_ref[...] = value
        else:
            half = self.cols // 2
            give_ref, got_ref = swap
            low, high = value[:, :half], value[:, half:]
            out_ref[...] = jnp.where(self.c == 0, low, high)
            give_ref[...] = jnp.where(self.c == 0, high, low)
            dev = at(self.z, self.x, self.y, 1 - self.c)
            self.swapped = self.links.send(give_ref, got_ref, dev)
        part = jnp.sum((value * value).reshape(self.rows // 8, 8, self.cols), axis=0)
        for j in range(self.cols // 128):
            squares[0] += part[:, j * 128 : (j + 1) * 128]


class ReduceEarly(Reduce):
    def one(self, d):
        self.copies[CORE, d].wait_recv()
        self.add((self.both(d), slice(None)), self.core_in[self.both(d), :])
        if d:
            src, dst = self.own.at[self.both(d)], self.from_z.at[d - 1]
            dev = at(self.plane(d), self.x, self.y, self.c)
            self.copies[LAST, d] = self.links.send(src, dst, dev)

    def second(self, d):
        if d == 0:
            value = self.own[self.both(0), :].astype(jnp.float32)
            for e in (1, 2, 3):
                self.copies[LAST, e].wait_recv()
                value = value + self.from_z[e - 1].astype(jnp.float32)
            self.own[self.both(0), :] = value.astype(jnp.bfloat16)
            src = self.own.at[self.both(0), self.side(1 - self.y)]
            dev = at(self.z, self.x, 1 - self.y, self.c)
            self.copies[ONE, 0] = self.links.send(src, self.one_y.at[0], dev)

    def third(self, d):
        if d == 0:
            self.copies[ONE, 0].wait_recv()
            self.add((self.both(0), self.side(self.y)), self.one_y[0])
            src = self.own.at[self.strip(self.z * 2 + 1 - self.x), self.side(self.y)]
            dev = at(self.z, 1 - self.x, self.y, self.c)
            self.copies[TWO, 0] = self.links.send(src, self.two.at[0], dev)

    def whole(self):
        near = self.own[self.strip(self.z * 2 + self.x), self.side(self.y)]
        self.copies[TWO, 0].wait_recv()
        return near.astype(jnp.float32) + self.two[0].astype(jnp.float32)


def backward_kernel(layers, pairs, coef, w_ref, aux_ref, dh_in, gains_ref, *refs):
    kept = [Kept(*refs[12 * i : 12 * i + 12]) for i in range(layers)]
    refs = refs[12 * layers :]
    weights = [(None,) + refs[4 * i : 4 * i + 4] for i in range(layers)]
    refs = refs[4 * layers :]
    dh = refs[0]
    sums = [(None,) + refs[1 + 4 * i : 5 + 4 * i] for i in range(layers)]
    gots = [refs[1 + 4 * layers + 2 * i :][:2] for i in range(layers)]
    norm_out, square_out = refs[1 + 6 * layers : 3 + 6 * layers]
    rest = refs[3 + 6 * layers :]
    free_sem, send_sem, recv_sem, move_sem = rest[-4:]
    norms, norm_z, norm_plane, squares, square_z, square_plane = rest[-10:-4]
    swaps = [rest[-10 - 2 * (i + 1) : -8 - 2 * (i + 1)] for i in range(layers)]
    links, moves = Links(send_sem, recv_sem), Moves(move_sem)
    reds = [
        [None]
        + [
            (ReduceEarly if k == OUT else Reduce)(*rest[k - 1 : 24 : 4], links) for k in MATRICES
        ]
        for _ in range(layers)
    ]
    give_a, give_b, buf_a, buf_b, w_out = rest[24:29]
    hold = Kept(*rest[29:31], None, *rest[31:40])
    drb, turned, dd_ref = rest[40:43]
    ex_refs = [exchange_refs(rest[43:], i) for i in range(layers)]
    rows, model = dh.shape
    half = rows // 2
    width = model + 128
    hidden = hold.gz.shape[1]
    z, x, y, c = place()
    even = c == 0

    loads = {}

    def load(number, src, dst):
        loads[number] = moves.start(src, dst)

    def need(*numbers):
        for number in numbers:
            moves.wait(loads[number])

    def load_early(layer):
        have = kept[layer]
        load(0, have.xh2, hold.xh2)
        load(1, have.rstd, hold.rstd)
        load(2, weights[layer][DOWN], buf_a)
        load(3, have.n1b, hold.n1b)
        load(4, have.xh1, hold.xh1)
        load(5, have.ob, hold.ob)
        load(6, have.den, hold.den)
        load(7, have.state, hold.state)
        load(8, have.slope, hold.slope)
        load(9, weights[layer][OUT], w_out)

    def load_late(layer):
        load(11, kept[layer].gu, hold.gu)
        load(12, weights[layer][UP], buf_b)

    steps, done, pushed, closed = [], [0], [], {}

    def pump(n):
        while n > 0 and done[0] < len(steps):
            steps[done[0]]()
            done[0] += 1
            n -= 1

    def until(mark):
        pump(mark - done[0])

    def later_stages(i):
        for stage in (1, 2, 3):
            if 0 <= i - stage < len(pushed):
                layer, kind = pushed[i - stage]
                red = reds[layer][kind]
                if stage < 3:
                    for d in (2, 3, 1, 0):
                        steps.append(functools.partial((red.second, red.third)[stage - 1], d))
                else:
                    swap = None
                    if kind in (QKV, OUT):
                        swap = (swaps[layer][kind - 1], gots[layer][kind - 1])
                    steps.append(functools.partial(red.last, sums[layer][kind], squares, swap))
                    if layer:
                        steps.append(functools.partial(red.release, free_sem.at[kind]))
                    closed[layer, kind] = len(steps)

    def take(layer, kind):
        if layer < layers - 1:
            until(closed[layer + 1, kind])

    def credit(layer, kind):
        if layer < layers - 1:
            pl.semaphore_wait(free_sem.at[kind], 6)

    def push(layer, kind, ref):
        red = reds[layer][kind]
        credit(layer, kind)
        for d in (2, 3, 1, 0):
            red.give(ref, d)
        pushed.append((layer, kind))
        for d in (2, 3, 1, 0):
            steps.append(functools.partial(red.one, d))
        later_stages(len(pushed) - 1)

    load(10, kept[layers - 1].gz, hold.gz)
    first_dh = moves.start(dh_in, drb)
    load_early(layers - 1)
    load_late(layers - 1)
    greet()
    squares[...] = jnp.zeros(squares.shape, jnp.float32)
    devices = partners()

    class Total:
        def __init__(self, mine, from_z, from_plane, out):
            self.refs = (mine, from_z, from_plane, out)

        def start(self):
            mine, from_z, _, _ = self.refs
            self.copies = [links.send(mine.at[0], from_z.at[i], devices[i]) for i in range(3)]

        def middle(self):
            mine, from_z, from_plane, _ = self.refs
            total = mine[0]
            for i in range(3):
                self.copies[i].wait_recv()
                total = total + from_z[i]
            mine[1] = total
            self.copies = [
                links.send(mine.at[1], from_plane.at[i], devices[3 + i]) for i in range(7)
            ]

        def end(self):
            mine, _, from_plane, out = self.refs
            total = mine[1]
            for i in range(7):
                self.copies[i].wait_recv()
                total = total + from_plane[i]
            out[...] = total

    norm_total = Total(norms, norm_z, norm_plane, norm_out)
    square_total = Total(squares, square_z, square_plane, square_out)
    moves.wait(first_dh)
    dh[...] = drb[...].astype(jnp.float32)

    cos, sin = aux_ref[:, 0:1], aux_ref[:, 1:2]
    follow, tail, valid = aux_ref[:, 2:3], aux_ref[:, 3:4], aux_ref[:, 4:5]
    low = low_lanes((rows, 128))
    zero = jnp.zeros((rows, 128), jnp.bfloat16)
    ones = jnp.ones((rows, 128), jnp.bfloat16)
    cf, sf = cos * follow, sin * follow
    ct, st = cos * tail, sin * tail

    def turn(ref):
        for i in range(0, model, 256):
            turned[i : i + 256, :] = ref[:, i : i + 256].astype(jnp.float32).T.astype(jnp.bfloat16)

    def choose(first, second):
        return jnp.where(even, first, second), jnp.where(even, second, first)

    def split_rows(block, mine_ref, theirs_ref, span):
        for strip in range(8):
            mine, theirs = choose(
                block[strip * 96 : strip * 96 + 48], block[strip * 96 + 48 : strip * 96 + 96]
            )
            mine_ref[strip * 48 : (strip + 1) * 48, span] = mine
            theirs_ref[strip * 48 : (strip + 1) * 48, span] = theirs

    def q_of(p):
        return buf_a[:rows, p * 128 : (p + 1) * 128]

    def k_of(p):
        return buf_a[:rows, model + p * 128 : model + (p + 1) * 128]

    def v_of(p):
        return buf_a[:rows, 2 * model + p * 128 : 2 * model + (p + 1) * 128]

    def one_layer(layer):
        red = reds[layer]
        down, up, out, qkv = red[DOWN], red[UP], red[OUT], red[QKV]
        ex = Exchange(coef, ex_refs[layer], links, True)

        def norm_back(xh_ref, which):
            gain = gains_ref[layer, 2 * which : 2 * which + 1, :]
            dg = jnp.zeros((8, model), jnp.float32)
            db = jnp.zeros((8, model), jnp.float32)
            for i in range(0, rows, 128):
                dy, xh = dh[i : i + 128, :], xh_ref[i : i + 128, :]
                r = hold.rstd[i : i + 128, which * 64 : which * 64 + 1]
                e = dy * gain
                both = dy * xh
                dx = e - jnp.mean(e, axis=1, keepdims=True)
                dx = r * (dx - xh * jnp.mean(e * xh, axis=1, keepdims=True))
                dg = dg + jnp.sum(both.reshape(16, 8, model), axis=0)
                db = db + jnp.sum(dy.reshape(16, 8, model), axis=0)
                dh[i : i + 128, :] = dx
                drb[i : i + 128, :] = dx.astype(jnp.bfloat16)
                pump(1)
            at_line = 4 * layer + 2 * which
            norms[0, at_line : at_line + 1, :] = jnp.sum(dg, axis=0, keepdims=True)
            norms[0, at_line + 1 : at_line + 2, :] = jnp.sum(db, axis=0, keepdims=True)

        need(0, 1)
        norm_back(hold.xh2, 1)
        turn(drb)
        need(10)
        take(layer, DOWN)
        left = turned[...]
        for strip in range(8):
            block = mm(left, hold.gz[:, strip * 384 : (strip + 1) * 384]).astype(jnp.bfloat16)
            for yy in range(2):
                first = block[yy * 384 : yy * 384 + 192]
                second = block[yy * 384 + 192 : yy * 384 + 384]
                mine, theirs = choose(first, second)
                span = slice(strip * 192, (strip + 1) * 192)
                down.own[span, yy * 384 : (yy + 1) * 384] = mine
                give_a[span, yy * 384 : (yy + 1) * 384] = theirs
            pump(1)
        push(layer, DOWN, give_a)
        need(2, 11)
        low_grad = drb[...]
        for j in range(hidden // 256):
            span = slice(j * 256, (j + 1) * 256)
            t = mm(low_grad, buf_a[:, span]) * hold.gu[:, span].astype(jnp.float32)
            hold.gz[:, span] = t.astype(jnp.bfloat16)
            pump(1)
        du = hold.gz
        load(13, kept[layer].soft, buf_a.at[pl.ds(0, rows), pl.ds(0, 3 * model)])
        need(3)
        turn(hold.n1b)
        take(layer, UP)
        left = turned[...]
        for yy in range(2):
            for target, cc in ((give_b, 1 - c), (up.own, c)):
                for j in range(3):
                    cols = pl.ds(pl.multiple_of((yy * 2 + cc) * 768 + j * 256, 256), 256)
                    block = mm(left, du[:, cols]).astype(jnp.bfloat16)
                    target[:, yy * 768 + j * 256 : yy * 768 + (j + 1) * 256] = block
        push(layer, UP, give_b)
        need(12)
        for j in range(model // 256):
            span = slice(j * 256, (j + 1) * 256)
            dh[:, span] += mm_nt(du[...], buf_b[span, :])
            pump(2)
        load(14, weights[layer][QKV], buf_b.at[:, pl.ds(0, 3 * model)])
        load(15, kept[layer].acts, hold.acts)
        need(4)
        norm_back(hold.xh1, 0)
        need(9)
        dob_ref = du.at[:, pl.ds(0, model)]
        dn_ref = du.at[:, pl.ds(model, model)]
        dob_ref[...] = mm_nt(drb[...], w_out[...]).astype(jnp.bfloat16)
        need(13, 5, 6, 7, 8)
        grad, state_ref = hold.gu, hold.state
        keep_k, keep_v = hold.xh2, hold.xh1
        den = hold.den[...]
        inv = 1.0 / jnp.maximum(den, 1.0)
        dots = jnp.zeros((rows, 128), jnp.float32)
        for p in range(pairs):
            dob = dob_ref[:, pair_cols(p)].astype(jnp.float32)
            dn_ref[:, pair_cols(p)] = (dob * spread(inv, p)).astype(jnp.bfloat16)
            both = dob * hold.ob[:, pair_cols(p)].astype(jnp.float32)
            first = jnp.sum(jnp.where(low, both, 0.0), axis=1, keepdims=True)
            second = jnp.sum(jnp.where(low, 0.0, both), axis=1, keepdims=True)
            dots = dots + jnp.where(lane_is((rows, 128), 2 * p), first, 0.0)
            dots = dots + jnp.where(lane_is((rows, 128), 2 * p + 1), second, 0.0)
        dden = jnp.where(den > 1.0, -dots * inv, 0.0)
        dd_ref[...] = dden
        dden_low = dden.astype(jnp.bfloat16)
        extras = [None, None]
        for p in range(pairs):
            qp = q_of(p).astype(jnp.float32)
            rhs = jnp.concatenate([dn_ref[:, pair_cols(p)], dden_low], axis=1)
            for kind, angle in enumerate((cf, sf)):
                block = mm_tn((qp * angle).astype(jnp.bfloat16), rhs)
                extras[kind] = pack_state(ex.mine, p, kind, block, extras[kind])
        for kind in range(2):
            store_extra(ex.mine, kind, extras[kind], width)
        ex.scatter()

        if layer == 0:
            norm_total.start()
        turn(hold.ob)
        take(layer, OUT)
        down.given()
        left = turned[...]
        for j in range(model // 256):
            span = slice(j * 256, (j + 1) * 256)
            block = mm(left, drb[:, span]).astype(jnp.bfloat16)
            split_rows(block, out.own, give_a, span)
        push(layer, OUT, give_a)

        def inner(p):
            qp, kp, vp = q_of(p), k_of(p), v_of(p)
            dob, dnp = dob_ref[:, pair_cols(p)], dn_ref[:, pair_cols(p)]
            q_t = qp.astype(jnp.float32).T.astype(jnp.bfloat16)
            dn_t = dnp.astype(jnp.float32).T.astype(jnp.bfloat16)
            dq_parts, dk_parts, dv_parts = [], [], []
            for e in range(2):
                h = 2 * p + e
                mask = low if e == 0 else ~low
                span = slice(e * HD, (e + 1) * HD)
                qh = jnp.where(mask, qp, zero)
                doh = jnp.where(mask, dob, zero)
                scale, shift = inv[:, h : h + 1], dd_ref[:, h : h + 1]

                def tile(at_rows, at_cols):
                    weight = w_ref[at_rows, at_cols]
                    s = (mm_nt(qh[at_rows], kp[at_cols]) * weight).astype(jnp.bfloat16)
                    t = mm_nt(doh[at_rows], vp[at_cols])
                    ds = (t * scale[at_rows] + shift[at_rows]).astype(jnp.bfloat16)
                    g = (ds.astype(jnp.float32) * weight).astype(jnp.bfloat16)
                    return s, g

                above, below, every = slice(0, half), slice(half, rows), slice(0, rows)
                s_top, g_top = tile(above, above)
                s_low, g_low = tile(below, every)
                dq_parts.append(jnp.concatenate([mm(g_top, kp[:half]), mm(g_low, kp)], axis=0))

                def across(flat, top, bottom):
                    whole = mm(flat[span, half:], bottom)
                    first = whole[:, :half] + mm(flat[span, :half], top)
                    return jnp.concatenate([first, whole[:, half:]], axis=1)

                dk_parts.append(across(q_t, g_top, g_low))
                dv_parts.append(across(dn_t, s_top, s_low))
            base = slice(p * 128, (p + 1) * 128)
            dq = jnp.where(low, dq_parts[0], dq_parts[1])
            right = jnp.concatenate([dnp, dd_ref[...].astype(jnp.bfloat16)], axis=1)
            dq += cf * mm_nt(right, unpack_state(state_ref, p, 0, width))
            dq += sf * mm_nt(right, unpack_state(state_ref, p, 1, width))
            slope = hold.slope[:, base].astype(jnp.float32)
            grad[:, base] = (dq * slope).astype(jnp.bfloat16)
            keep_k[:, base] = jnp.concatenate(dk_parts, axis=0).T
            keep_v[:, base] = jnp.concatenate(dv_parts, axis=0).T

        for p in range(pairs):
            inner(p)
            if p == 1:
                ex.across()
            if p == 2:
                ex.gather()
            pump(3)
        ex.finish()
        for p in range(pairs):
            base = p * 128
            dsc, dss = unpack_state(ex.result, p, 0, width), unpack_state(ex.result, p, 1, width)
            right = jnp.concatenate([v_of(p), ones], axis=1)
            dk = keep_k[:, base : base + 128] + ct * mm_nt(right, dsc) + st * mm_nt(right, dss)
            kp = k_of(p)
            dv = ct * mm(kp, dsc[:, :128]) + st * mm(kp, dss[:, :128])
            dv = keep_v[:, base : base + 128] + dv
            slope = hold.slope[:, model + base : model + base + 128].astype(jnp.float32)
            grad[:, model + base : model + base + 128] = (dk * valid * slope).astype(jnp.bfloat16)
            grad[:, 2 * model + base : 2 * model + base + 128] = dv.astype(jnp.bfloat16)
        if layer == 0:
            norm_total.middle()
        need(15)
        turn(hold.acts)
        if layer:
            load_early(layer - 1)
        take(layer, QKV)
        left = turned[...]
        for j in range(3 * model // 256):
            span = slice(j * 256, (j + 1) * 256)
            block = mm(left, grad[:, span]).astype(jnp.bfloat16)
            split_rows(block, qkv.own, hold.gz, span)
        push(layer, QKV, hold.gz)
        up.given()
        out.given()
        need(14)
        for j in range(model // 256):
            span = slice(j * 256, (j + 1) * 256)
            dh[:, span] += mm_nt(grad[:, : 3 * model], buf_b[span, : 3 * model])
            pump(2)
        qkv.given()
        if layer:
            load(10, kept[layer - 1].gz, hold.gz)
            load_late(layer - 1)

    for layer in reversed(range(layers)):
        one_layer(layer)
    out, qkv = reds[0][OUT], reds[0][QKV]
    for step, d in (
        (qkv.second, 2), (out.third, 2), (qkv.second, 3), (qkv.third, 2), (out.third, 3),
        (out.third, 1), (qkv.second, 1), (qkv.third, 3), (out.third, 0), (qkv.second, 0),
        (qkv.third, 1), (qkv.third, 0),
    ):
        steps.append(functools.partial(step, d))
    pump(len(steps))
    reds[0][UP].last(sums[0][UP], squares)
    for kind in (OUT, QKV):
        reds[0][kind].last(sums[0][kind], squares, (swaps[0][kind - 1], gots[0][kind - 1]))
    square_total.start()
    norm_total.end()
    square_total.middle()
    for red in reds:
        for kind in (QKV, OUT):
            red[kind].swapped.wait_recv()
    square_total.end()
    moves.finish()
    links.finish()


def backward(number, tables, gains, dh, held, dims):
    rows, model = dh.shape
    layers = len(held)
    weights_map, aux, coef = tables
    kept = held[0][1]
    hidden = kept.gz.shape[1]
    width = model + 128
    low, wide = jnp.bfloat16, jnp.float32
    vmem = pl.BlockSpec(memory_space=pltpu.VMEM)
    anywhere = pl.BlockSpec(memory_space=pl.ANY)
    sizes = dims[1:]
    scratch = [pltpu.VMEM((8 * r, 2 * w), low) for r, w in sizes] * 2
    early = [k == OUT for k in MATRICES]
    scratch += [pltpu.VMEM((1 if e else 2, 2 * r, w), low) for (r, w), e in zip(sizes, early)]
    scratch += [pltpu.VMEM((1 if e else 2, r, 2 * w), low) for (r, w), e in zip(sizes, early)]
    scratch += [pltpu.VMEM((1 if e else 4, r, w), low) for (r, w), e in zip(sizes, early)]
    scratch += [
        pltpu.VMEM((3, 2 * r, 2 * w) if e else (3, r, w), low) for (r, w), e in zip(sizes, early)
    ]
    for k in (DOWN, UP):
        scratch.append(pltpu.VMEM((8 * dims[k][0], 2 * dims[k][1]), low))
    scratch += [pltpu.VMEM((model, hidden), low)] * 2
    scratch.append(pltpu.VMEM((model, model), low))
    scratch += [pltpu.VMEM(a.shape, a.dtype) for a in kept[:2] + kept[3:]]
    scratch += [pltpu.VMEM((rows, model), low), pltpu.VMEM((model, rows), low)]
    scratch += [pltpu.VMEM((rows, 128), wide)]
    scratch += exchange_scratch(width, layers)
    halves = [(r, w // 2) for r, w in sizes[:2]]
    scratch += [pltpu.VMEM(s, wide) for s in halves] * layers
    for size in ((4 * layers, model), (8, 128)):
        scratch += [pltpu.VMEM((n,) + size, wide) for n in (2, 3, 7)]
    scratch += [pltpu.SemaphoreType.REGULAR((5,))]
    scratch += [pltpu.SemaphoreType.DMA((layers * 80 + 20,))] * 2
    scratch += [pltpu.SemaphoreType.DMA((layers * 20,))]
    outs = pl.pallas_call(
        functools.partial(backward_kernel, layers, model // 128),
        out_shape=[jax.ShapeDtypeStruct((rows, model), wide)]
        + [jax.ShapeDtypeStruct(s, wide) for s in halves + sizes[2:]] * layers
        + [jax.ShapeDtypeStruct(s, wide) for s in halves] * layers
        + [
            jax.ShapeDtypeStruct((4 * layers, model), wide),
            jax.ShapeDtypeStruct((8, 128), wide),
        ],
        in_specs=[vmem, vmem, vmem, anywhere, vmem]
        + [anywhere] * (16 * layers),
        out_specs=[vmem] * (3 + 6 * layers),
        scratch_shapes=scratch,
        compiler_params=pltpu.CompilerParams(
            collective_id=number, has_side_effects=True, vmem_limit_bytes=63 * 2**20
        ),
        name="backward_layers",
    )(
        coef, weights_map, aux, dh, gains,
        *[a for h in held for a in h[1]],
        *[a for h in held for a in h[0]],
    )
    sums = [outs[1 + 4 * i : 5 + 4 * i] for i in range(layers)]
    gots = [outs[1 + 4 * layers + 2 * i :][:2] for i in range(layers)]
    return outs[0], sums, gots, outs[-2], outs[-1]


def stream_meta(lengths, row_ids):
    seq_count = lengths.shape[0]
    seq_ends = jnp.cumsum(lengths, dtype=jnp.int32)
    seq_starts = seq_ends - lengths
    begun = seq_starts[None, :] <= row_ids[:, None]
    seg_raw = jnp.sum(begun.astype(jnp.int32), axis=1, dtype=jnp.int32) - 1
    seg_start = jnp.max(jnp.where(begun, seq_starts[None, :], 0), axis=1)
    inside = row_ids < seq_ends[seq_count - 1]
    seg_ids = jnp.where(inside, seg_raw, seq_count)
    offsets = jnp.where(inside, row_ids - seg_start, 0).astype(jnp.float32)
    angles = offsets * (0.5 * math.pi / LONGEST)
    return (seg_ids, jnp.cos(angles), jnp.sin(angles), inside.astype(jnp.float32))


def adam_step(weight, first_old, second_old, gradient, factor, step_rate, decay_coef):
    clipped = gradient * factor
    first_new = beta_one * first_old + (1.0 - beta_one) * clipped
    second_new = beta_two * second_old + (1.0 - beta_two) * clipped * clipped
    first_hat = first_new / (1.0 - beta_one**step_fixed)
    second_hat = second_new / (1.0 - beta_two**step_fixed)
    weight_new = weight - step_rate * (
        first_hat / (jnp.sqrt(second_hat) + adam_eps) + decay_coef * weight
    )
    return (weight_new, first_new, second_new)


def other_core(array):
    return lax.ppermute(array, "head", [(0, 1), (1, 0), (2, 3), (3, 2)])


def weight_pieces(w_qkv, w_out, w_up, w_down, norm_params):
    first = lax.axis_index("head") % 2 == 0
    low = [a.astype(jnp.bfloat16) for a in (w_qkv, w_out)]
    halves = [(a[:, : a.shape[1] // 2], a[:, a.shape[1] // 2 :]) for a in low]
    keep = [jnp.where(first, a, b) for a, b in halves]
    give = [jnp.where(first, b, a) for a, b in halves]
    wide = other_core(jnp.concatenate(give, axis=2))
    got = jnp.split(wide, (keep[0].shape[2],), axis=2)
    pieces = [
        jnp.where(first, jnp.concatenate([a, b], axis=2), jnp.concatenate([b, a], axis=2))
        for a, b in zip(keep, got)
    ]
    pieces.append(w_up.astype(jnp.bfloat16))
    pieces.append(w_down.astype(jnp.bfloat16).transpose(0, 2, 1))
    layers, _, part = norm_params.shape
    norm = norm_params.astype(jnp.bfloat16).reshape(layers, part)
    return [jnp.pad(norm, ((0, 16 - layers), (0, 128 - part)))] + pieces


def update_kernel(layers, count, *refs):
    out, norm_out = refs[count + 2 : count + 17], refs[count + 17]
    here, sem = refs[count + 20 : 2 * count + 20], refs[2 * count + 20]
    kept = refs[2 * count + 21 : 2 * count + 23]
    rows = [pltpu.make_async_copy(refs[count + i], kept[i], sem.at[count + i]) for i in range(2)]
    for copy in rows:
        copy.start()
    copies = [pltpu.make_async_copy(refs[i], here[i], sem.at[i]) for i in range(count)]
    for copy in copies:
        copy.start()
    sums = [here[4 * i : 4 * i + 4] for i in range(layers)]
    gots = [here[4 * layers + 2 * i :][:2] for i in range(layers)]
    norm_ref, square_ref = here[6 * layers : 6 * layers + 2]
    state = here[6 * layers + 2 :]
    z, x, y, c = place()
    dp, head = z * 2 + x, y * 2 + c
    for copy in copies:
        copy.wait()
    for copy in rows:
        copy.wait()
    rows = [
        pltpu.make_async_copy(kept[i], refs[count + 18 + i], sem.at[count + i]) for i in range(2)
    ]
    for copy in rows:
        copy.start()
    lines = norm_ref[...]
    total = jnp.sum(square_ref[...], axis=1, keepdims=True)
    total = jnp.sum(total, axis=0, keepdims=True)
    own = jnp.sum(lines * lines, axis=1, keepdims=True)
    total = total + jnp.sum(own, axis=0, keepdims=True)
    grad_norm = jnp.sqrt(total)
    factor = clip_limit / jnp.maximum(grad_norm, clip_limit)
    norm_out[0] = jnp.sum(grad_norm)

    def step(kind, layer, span, gradient, rate, decay):
        spot = (layer, span)
        old = [ref[spot] for ref in state[3 * kind : 3 * kind + 3]]
        new = adam_step(*old, gradient, factor, rate, decay)
        for ref, value in zip(out[3 * kind : 3 * kind + 3], new):
            ref[spot] = value

    for layer in range(layers):
        for kind, rate in ((0, rate_matrix), (1, rate_outproj)):
            mine, theirs = sums[layer][kind][...], gots[layer][kind][...]
            half = mine.shape[0]
            step(kind, layer, slice(0, half), jnp.where(c == 0, mine, theirs), rate, decay_rate)
            step(kind, layer, slice(half, 2 * half), jnp.where(c == 0, theirs, mine), rate, decay_rate)
        step(2, layer, slice(None), sums[layer][2][...], rate_matrix, decay_rate)
        step(3, layer, slice(None), sums[layer][3][...], rate_matrix, decay_rate)
        line = norm_ref[pl.ds(4 * layer + head, 1), :]
        part = state[12].shape[2]
        own = jnp.zeros((1, part), jnp.float32)
        for i in range(8):
            own = own + jnp.where(dp == i, line[:, i * part : (i + 1) * part], 0.0)
        step(4, layer, slice(None), own, rate_norm, 0.0)
    for copy in rows:
        copy.wait()


def update(sums, gots, norm_sum, squares, state, rows):
    vmem = pl.BlockSpec(memory_space=pltpu.VMEM)
    anywhere = pl.BlockSpec(memory_space=pl.ANY)
    inputs = [a for s in sums for a in s] + [a for g in gots for a in g]
    inputs += [norm_sum, squares, *state]
    count = len(inputs)
    return pl.pallas_call(
        functools.partial(update_kernel, len(sums), count),
        out_shape=[jax.ShapeDtypeStruct(a.shape, a.dtype) for a in state]
        + [jax.ShapeDtypeStruct((1,), jnp.float32)]
        + [jax.ShapeDtypeStruct(a.shape, a.dtype) for a in rows],
        in_specs=[anywhere] * (count + 2),
        out_specs=[vmem] * len(state) + [pl.BlockSpec(memory_space=pltpu.SMEM)] + [anywhere] * 2,
        scratch_shapes=[pltpu.VMEM(a.shape, a.dtype) for a in inputs]
        + [pltpu.SemaphoreType.DMA((count + 2,))]
        + [pltpu.VMEM(a.shape, a.dtype) for a in rows],
        compiler_params=pltpu.CompilerParams(vmem_limit_bytes=56 * 2**20),
        name="update",
    )(*inputs, *rows)


def near_step(inputs, cotangent, lengths, state):
    w_qkv, w_out, w_up, w_down, norm_params = state[::3]
    pieces = weight_pieces(w_qkv, w_out, w_up, w_down, norm_params)
    dims = [p.shape[-2:] for p in pieces]
    hidden, gains, tables, held = forward(0, lengths, inputs, pieces)
    grad, sums, gots, norm_sum, squares = backward(1, tables, gains, cotangent, held, dims)
    turned = [a.transpose(0, 2, 1) if 9 <= i < 12 else a for i, a in enumerate(state)]
    *new, norm, hidden, grad = update(sums, gots, norm_sum, squares, turned, (hidden, grad))
    new = [a.transpose(0, 2, 1) if 9 <= i < 12 else a for i, a in enumerate(new)]
    return (hidden, grad, norm, *new)


def layer_norm(inputs_row, gain_row, shift_row):
    mean_row = jnp.mean(inputs_row, axis=-1, keepdims=True)
    centered = inputs_row - mean_row
    variance = jnp.mean(centered * centered, axis=-1, keepdims=True)
    return centered * lax.rsqrt(variance + norm_eps) * gain_row + shift_row


def gelu_exact(inner_pre):
    return jax.nn.gelu(inner_pre, approximate=False)


def contract_rows(left, right):
    return lax.dot_general(
        left, right, (((0,), (0,)), ((), ())), preferred_element_type=jnp.float32
    )


def contract_cols(left, right):
    return lax.dot_general(
        left, right, (((1,), (1,)), ((), ())), preferred_element_type=jnp.float32
    )


def block_attention(queries, key_rows, value_rows, weights, aux):
    cos, sin, tail = aux[:, 0], aux[:, 1], aux[:, 3]
    raw = jnp.einsum("ihe,jhe->hij", queries, key_rows, preferred_element_type=jnp.float32)
    scores = (raw * weights[None]).astype(jnp.bfloat16)
    num = jnp.einsum("hij,jhe->ihe", scores, value_rows, preferred_element_type=jnp.float32)
    den = jnp.transpose(jnp.sum(scores.astype(jnp.float32), axis=2))
    out = []
    for angle in (cos, sin):
        turned = key_rows.astype(jnp.float32) * (angle * tail)[:, None, None]
        out.append(
            jnp.einsum(
                "jhe,jhf->hef", turned, value_rows.astype(jnp.float32), precision=exact_mode
            )
        )
        out.append(jnp.sum(turned, axis=0))
    return num, den, tuple(out)


def finish_rows(queries, num, den, state, aux):
    cos, sin, follow = aux[:, 0], aux[:, 1], aux[:, 2]
    for angle, kv, ks in ((cos, state[0], state[1]), (sin, state[2], state[3])):
        turned = queries.astype(jnp.float32) * (angle * follow)[:, None, None]
        num = num + jnp.einsum("ihe,hef->ihf", turned, kv, precision=exact_mode)
        den = den + jnp.einsum("ihe,he->ih", turned, ks, precision=exact_mode)
    return num / jnp.maximum(den, 1.0)[:, :, None]


class WidePlan:
    def __init__(self, lengths, rows):
        parts = lax.axis_size("dp") * lax.axis_size("head")
        me = lax.axis_index("dp") * lax.axis_size("head") + lax.axis_index("head")
        seg, cos, sin, valid = stream_meta(
            lengths, me * rows + jnp.arange(rows, dtype=jnp.int32)
        )
        starts = jnp.arange(parts, dtype=jnp.int32) * rows
        before = stream_meta(lengths, starts - 1)[0]
        last = stream_meta(lengths, starts + rows - 1)[0]
        follow = (seg == before[me]).astype(jnp.float32)
        tail = (seg == last[me]).astype(jnp.float32)
        place_ids = jnp.arange(rows)
        allowed = (seg[:, None] == seg[None, :]) & (place_ids[None, :] <= place_ids[:, None])
        close = cos[:, None] * cos[None, :] + sin[:, None] * sin[None, :]
        self.valid = valid
        self.weights = jnp.where(allowed, close, 0.0)
        self.aux = jnp.stack([cos, sin, follow, tail, valid], axis=1)
        devices = jnp.arange(parts)
        self.ahead = ((last == before[me]) & (devices < me)).astype(jnp.float32)
        self.behind = ((before == last[me]) & (devices > me)).astype(jnp.float32)

    def masked(self, state, coef):
        def one(a):
            everything = lax.all_gather(a.astype(jnp.bfloat16), ("dp", "head"))
            return jnp.einsum(
                "d,d...->...",
                coef.astype(jnp.bfloat16),
                everything,
                preferred_element_type=jnp.float32,
            )

        return jax.tree.map(one, state)

    def attend(self, q, k, v):
        rows, model = q.shape
        split = lambda a: a.reshape(rows, HEADS, model // HEADS)
        local = lambda *a: block_attention(*a, self.weights, self.aux)
        (num, den, state), pull = jax.vjp(local, split(q), split(k), split(v))
        state = self.masked(state, self.ahead)
        finish = lambda *a: finish_rows(*a, self.aux)
        out, finish_pull = jax.vjp(finish, split(q), num, den, state)
        return out.astype(jnp.bfloat16).reshape(rows, model), (pull, finish_pull)

    def attend_back(self, kept, dob):
        pull, finish_pull = kept
        rows, model = dob.shape
        grad = dob.astype(jnp.float32).reshape(rows, HEADS, model // HEADS)
        dq_one, dnum, dden, dstate = finish_pull(grad)
        dstate = self.masked(dstate, self.behind)
        dq, dk, dv = pull((dnum, dden, dstate))
        dq = dq.astype(jnp.float32) + dq_one.astype(jnp.float32)
        dk = dk.astype(jnp.float32) * self.valid[:, None, None]
        out = [a.reshape(rows, model).astype(jnp.bfloat16) for a in (dq, dk, dv)]
        return jnp.concatenate(out, axis=1)


def wide_gather(w_qkv, w_out, w_up, w_down, norm_params):
    fulls = []
    for a in (w_qkv, w_out, w_up, w_down):
        part = lax.all_gather(a.astype(jnp.bfloat16), "dp", axis=1, tiled=True)
        fulls.append(lax.all_gather(part, "head", axis=2, tiled=True))
    norm = lax.all_gather(norm_params.astype(jnp.bfloat16), "dp", axis=2, tiled=True)
    return fulls, lax.all_gather(norm, "head", axis=1, tiled=True)


def wide_reduce(grads, norm_grad):
    def one(a):
        part = lax.psum_scatter(a, "head", scatter_dimension=1, tiled=True)
        part = lax.psum_scatter(part.astype(jnp.float32), "dp", scatter_dimension=0, tiled=True)
        return part

    whole = [jnp.stack([one(layer[i]) for layer in grads]) for i in range(len(grads[0]))]
    part = lax.psum_scatter(norm_grad, "head", scatter_dimension=1, tiled=True)
    norm = lax.psum_scatter(part, "dp", scatter_dimension=2, tiled=True)
    squares = sum([jnp.sum(a * a) for a in whole + [norm]])
    return whole, norm, lax.psum(squares, ("dp", "head"))


def wide_step(inputs, cotangent, lengths, state):
    w_qkv, w_out, w_up, w_down, norm_params = state[::3]
    rows, model = inputs.shape
    layers = w_qkv.shape[0]
    plan = WidePlan(lengths, rows)
    fulls, norm_full = wide_gather(w_qkv, w_out, w_up, w_down, norm_params)
    norm_full = norm_full.astype(jnp.float32)
    hidden = inputs.astype(jnp.float32)
    kept = []
    for layer in range(layers):
        qkv_w, out_w, up_w, down_w = (a[layer] for a in fulls)
        gains = norm_full[layer]
        acts = hidden.astype(jnp.bfloat16)
        mixed = jnp.dot(acts, qkv_w, preferred_element_type=jnp.float32)
        soft = jax.nn.softplus(mixed[:, : 2 * model]).astype(jnp.bfloat16)
        q = soft[:, :model]
        k = soft[:, model:] * plan.valid[:, None].astype(jnp.bfloat16)
        v = mixed[:, 2 * model :].astype(jnp.bfloat16)
        attended, attend_kept = plan.attend(q, k, v)
        first_in = hidden + jnp.dot(attended, out_w, preferred_element_type=jnp.float32)
        first_out = layer_norm(first_in, gains[0], gains[1])
        first_low = first_out.astype(jnp.bfloat16)
        inner = jnp.dot(first_low, up_w, preferred_element_type=jnp.float32)
        act = gelu_exact(inner).astype(jnp.bfloat16)
        second_in = first_out + jnp.dot(act, down_w, preferred_element_type=jnp.float32)
        kept.append((acts, mixed, attend_kept, attended, first_in, first_low, inner, act, second_in))
        hidden = layer_norm(second_in, gains[2], gains[3])
    grad_hidden = cotangent.astype(jnp.float32)
    grads = [None] * layers
    norm_grads = [None] * layers
    for layer in reversed(range(layers)):
        acts, mixed, attend_kept, attended, first_in, first_low, inner, act, second_in = kept[layer]
        qkv_w, out_w, up_w, down_w = (a[layer] for a in fulls)
        gains = norm_full[layer]
        _, pull_two = jax.vjp(layer_norm, second_in, gains[2], gains[3])
        grad_second, dgain_two, dshift_two = pull_two(grad_hidden)
        branch_two = grad_second.astype(jnp.bfloat16)
        dw_down = contract_rows(act, branch_two).astype(jnp.bfloat16)
        grad_act = contract_cols(branch_two, down_w)
        _, gelu_pull = jax.vjp(gelu_exact, inner)
        grad_inner = gelu_pull(grad_act)[0].astype(jnp.bfloat16)
        dw_up = contract_rows(first_low, grad_inner).astype(jnp.bfloat16)
        grad_first = grad_second + contract_cols(grad_inner, up_w)
        _, pull_one = jax.vjp(layer_norm, first_in, gains[0], gains[1])
        grad_first_in, dgain_one, dshift_one = pull_one(grad_first)
        branch = grad_first_in.astype(jnp.bfloat16)
        dw_out = contract_rows(attended, branch).astype(jnp.bfloat16)
        dob = contract_cols(branch, out_w).astype(jnp.bfloat16)
        grad_mixed = plan.attend_back(attend_kept, dob)
        slope = jax.nn.sigmoid(mixed[:, : 2 * model])
        grad_soft = (grad_mixed[:, : 2 * model].astype(jnp.float32) * slope).astype(jnp.bfloat16)
        grad_pre = jnp.concatenate([grad_soft, grad_mixed[:, 2 * model :]], axis=1)
        dw_qkv = contract_rows(acts, grad_pre).astype(jnp.bfloat16)
        grad_hidden = grad_first_in + contract_cols(grad_pre, qkv_w)
        grads[layer] = (dw_qkv, dw_out, dw_up, dw_down)
        norm_grads[layer] = jnp.stack([dgain_one, dshift_one, dgain_two, dshift_two])
    whole, norm_sum, squares = wide_reduce(grads, jnp.stack(norm_grads))
    grad_norm = jnp.sqrt(squares)
    factor = clip_limit / jnp.maximum(grad_norm, clip_limit)
    new = []
    rates = (rate_matrix, rate_outproj, rate_matrix, rate_matrix, rate_norm)
    for i, gradient in enumerate(whole + [norm_sum]):
        decay = decay_rate if i < 4 else 0.0
        new += adam_step(*state[3 * i : 3 * i + 3], gradient, factor, rates[i], decay)
    return (hidden, grad_hidden, grad_norm.reshape(1), *new)


def body(inputs, cotangent, lengths, *state):
    near = lax.axis_size("dp") == 8 and lax.axis_size("head") == 4 and inputs.shape[0] == 512
    return (near_step if near else wide_step)(inputs, cotangent, lengths, state)


def solution(mesh):
    rows = P(("dp", "head"), None)
    weight = P(None, "dp", "head")
    norm = P(None, "head", "dp")
    in_specs = (rows, rows, P()) + (weight,) * 12 + (norm,) * 3
    out_specs = (rows, rows, P()) + (weight,) * 12 + (norm,) * 3
    return jax.shard_map(body, mesh=mesh, in_specs=in_specs, out_specs=out_specs, check_vma=False)
```
